256 devices in a mesh: seq: 64 (over z, x, core), head: 4 (over y).
Axes of the slice: x: 4, y: 4, z: 8, core: 2. Of those that a mesh axis runs over, the one named last changes fastest.
Arguments:
- query: bfloat16 [16384, 2048], P('seq', 'head'), may hold values from -24 to 24
- key: bfloat16 [16384, 512], P('seq', 'head'), may hold values from -24 to 24
- value: bfloat16 [16384, 512], P('seq', 'head'), may hold values from -6 to 6
- grad_out: bfloat16 [16384, 2048], P('seq', 'head'), may hold values from -6 to 6
- gate_score: int32 [4, 32, 32], P('head'), may hold values from 0 to 1048575
Outputs:
- attended: bfloat16 [16384, 2048], P('seq', 'head')
- grad_query: bfloat16 [16384, 2048], P('seq', 'head')
- grad_key: bfloat16 [16384, 512], P('seq', 'head')
- grad_value: bfloat16 [16384, 512], P('seq', 'head')
The draws below stay inside these ranges and needn't reach their ends.
All inputs are finite; a program needn't handle non-finite values.
Results may differ from the reference program's by a relative error of at most 0.03.
Values may be sent and summed in bfloat16 or wider, within the bound.
No kernel may reach another device: no remote copies, remote signals or barrier semaphores. Data moves between devices by JAX's collectives and lax.ppermute only.
A program may use at most 192 MiB of HBM per device.

```python
import math
import jax
import jax.numpy as jnp
from jax import lax

HEAD_DIM = 128
Q_HEADS = 16
KV_HEADS = 4
BLOCK = 512
TOPK = 8
TOKENS = 16384
NBLK = 32


def draw_key(key, part):
    key = jax.random.fold_in(key, 7)
    drawn = jnp.clip(jax.random.normal(key, (TOKENS, KV_HEADS * HEAD_DIM), jnp.float32), -6.0, 6.0)
    return drawn.astype(jnp.bfloat16)


def draw_query(key, part):
    key = jax.random.fold_in(key, 13)
    drawn = jnp.clip(jax.random.normal(key, (TOKENS, Q_HEADS * HEAD_DIM), jnp.float32), -6.0, 6.0)
    return drawn.astype(jnp.bfloat16)


def set_ends(result, key, least, largest):
    shape = result.shape
    place = [jax.random.randint(jax.random.fold_in(key, axis), (), 0, shape[axis]) for axis in range(len(shape))]
    result = result.at[tuple(place)].set(least)
    longest = shape.index(max(shape))
    place[longest] = (place[longest] + 1) % shape[longest]
    return result.at[tuple(place)].set(largest)


def levels(stream_key, dims, shards, low, largest):
    level, own = 1.0, jax.random.fold_in(stream_key, 6)
    for axis_at, blocks in shards:
        steps = jnp.exp(jax.random.uniform(jax.random.fold_in(own, axis_at), (blocks,), jnp.float32, low / len(shards), largest / len(shards)))
        level = level * jnp.repeat(steps, dims[axis_at] // blocks).reshape([-1 if axis == axis_at else 1 for axis in range(len(dims))])
    return level


def bell_draw(stream_key, dims, scale, most, pieces=(), held_as=jnp.bfloat16):
    level = levels(stream_key, dims, pieces, -0.22, 0.18) if pieces else 1.0
    drawn = jax.random.normal(stream_key, dims, jnp.float32) * scale * level
    return jnp.minimum(jnp.maximum(drawn, -most), most).astype(held_as)


def setup_inputs(seed: int = 0) -> dict:
    seeds = jax.random.split(jax.random.key(seed), 6)
    return {
        "query": draw_query(jax.random.fold_in(seeds[5], 71), 0),
        "key": draw_key(jax.random.fold_in(seeds[5], 71), 0),
        "value": bell_draw(seeds[2], (TOKENS, KV_HEADS * HEAD_DIM), 1.0, 6.0, ((0, 64), (1, 4))),
        "grad_out": bell_draw(seeds[3], (TOKENS, Q_HEADS * HEAD_DIM), 1.0, 6.0, ((0, 64), (1, 4))),
        "gate_score": set_ends(jax.random.randint(seeds[4], (KV_HEADS, NBLK, NBLK), 0, 1048576), jax.random.fold_in(seeds[4], 1), 0, 1048575).astype(jnp.int32),
    }


def pick_blocks(totals, own, count):
    columns = jnp.arange(count, dtype=jnp.int32)
    ranked = jnp.where(columns[None, :] < own[:, None], totals * count + columns[None, :], -1).astype(jnp.int32)
    filler = jnp.full((ranked.shape[0], TOPK), -1, jnp.int32)
    ranked = jnp.concatenate([ranked, filler], axis=1)
    values_top, index_top = lax.top_k(ranked, TOPK)
    picked = jnp.where(values_top >= 0, index_top.astype(jnp.int32), -1).astype(jnp.int32)
    return jnp.concatenate([picked, own[:, None].astype(jnp.int32)], axis=1)

def reference(query, key, value, grad_out, gate_score):
    group = Q_HEADS // KV_HEADS
    scale = 1.0 / math.sqrt(HEAD_DIM)
    slots = TOPK + 1
    totals = lax.optimization_barrier(jnp.sum(gate_score, axis=0, dtype=jnp.int32))
    numbers = jnp.arange(NBLK, dtype=jnp.int32)
    blocks = pick_blocks(totals, numbers, NBLK)
    queries = query.reshape(TOKENS, KV_HEADS, group, HEAD_DIM)
    grads = grad_out.reshape(TOKENS, KV_HEADS, group, HEAD_DIM)
    keys_all = key.reshape(TOKENS, KV_HEADS, HEAD_DIM)
    values_all = value.reshape(TOKENS, KV_HEADS, HEAD_DIM)
    offsets = jnp.arange(BLOCK, dtype=jnp.int32)
    slot_ids = jnp.repeat(jnp.arange(slots, dtype=jnp.int32), BLOCK)

    def step(carry, number):
        grad_k, grad_v = carry
        chosen = blocks[number]
        rows = (jnp.maximum(chosen, 0)[:, None] * BLOCK + offsets[None, :]).reshape(-1).astype(jnp.int32)
        live = jnp.repeat(chosen >= 0, BLOCK)
        key_pos = (chosen[:, None] * BLOCK + offsets[None, :]).reshape(-1)
        query_pos = number * BLOCK + offsets
        allowed = live[None, :] & ((slot_ids[None, :] < TOPK) | (key_pos[None, :] <= query_pos[:, None]))
        keys = keys_all[rows].astype(jnp.float32)
        vals = values_all[rows].astype(jnp.float32)
        start = (number * BLOCK).astype(jnp.int32)
        q_block = lax.dynamic_slice_in_dim(queries, start, BLOCK, 0).astype(jnp.float32)
        g_block = lax.dynamic_slice_in_dim(grads, start, BLOCK, 0).astype(jnp.float32)
        scores = jnp.einsum('qhgd,shd->hgqs', q_block, keys) * scale
        masked = jnp.where(allowed, scores, -jnp.inf)
        top = lax.optimization_barrier(jnp.max(masked, axis=-1, keepdims=True))
        lse = top + jnp.log(lax.optimization_barrier(jnp.sum(jnp.exp(masked - top), axis=-1, keepdims=True)))
        weight = jnp.where(allowed, jnp.exp(jnp.where(allowed, scores, 0.0) - lse), 0.0)
        prob = lax.optimization_barrier(weight.astype(jnp.bfloat16)).astype(jnp.float32)
        out_block = jnp.einsum('hgqs,shd->qhgd', prob, vals).astype(jnp.bfloat16)
        out_wide = lax.optimization_barrier(out_block).astype(jnp.float32)
        delta = jnp.transpose(lax.optimization_barrier(jnp.sum(g_block * out_wide, axis=-1)), (1, 2, 0))
        dprob = jnp.einsum('qhgd,shd->hgqs', g_block, vals)
        dscore = lax.optimization_barrier((weight * (dprob - delta[..., None])).astype(jnp.bfloat16)).astype(jnp.float32)
        dq_block = (jnp.einsum('hgqs,shd->qhgd', dscore, keys) * scale).astype(jnp.bfloat16)
        dk_part = jnp.einsum('hgqs,qhgd->shd', dscore, q_block)
        dv_part = jnp.einsum('hgqs,qhgd->shd', prob, g_block)
        grad_k = grad_k.at[rows].add(dk_part)
        grad_v = grad_v.at[rows].add(dv_part)
        return ((grad_k, grad_v), (out_block, dq_block))
    zeros = jnp.zeros((TOKENS, KV_HEADS, HEAD_DIM), jnp.float32)
    (grad_k, grad_v), (outs, dqs) = lax.scan(step, (zeros, zeros), numbers)
    attended = outs.reshape(TOKENS, Q_HEADS * HEAD_DIM)
    grad_query = dqs.reshape(TOKENS, Q_HEADS * HEAD_DIM)
    grad_key = (grad_k * scale).astype(jnp.bfloat16).reshape(TOKENS, KV_HEADS * HEAD_DIM)
    grad_value = grad_v.astype(jnp.bfloat16).reshape(TOKENS, KV_HEADS * HEAD_DIM)
    return (attended, grad_query, grad_key, grad_value)
```

```python
import functools
import math

import jax
import jax.numpy as jnp
from jax import lax
from jax.experimental import pallas as pl
from jax.experimental.pallas import tpu as pltpu
from jax.sharding import Mesh
from jax.sharding import PartitionSpec as P

HEAD_DIM = 128
GROUP = 4
TOPK = 8
NBLK = 32
HALF = 256
COLS = GROUP * HALF
PIECES = 32
SCALE = 1.0 / math.sqrt(HEAD_DIM)
SCALE2 = SCALE / math.log(2.0)
NEG = -1e30
MASKED = -3e38
BF = jnp.bfloat16
F32 = jnp.float32
SIZES = {"z": 8, "x": 4, "core": 2, "head": 4}
NT = (((1,), (1,)), ((), ()))
TN = (((0,), (0,)), ((), ()))
NN = (((1,), (0,)), ((), ()))


def dot(a, b, dims):
    return lax.dot_general(a, b, dims, preferred_element_type=F32)


def shift(a, axis, d):
    n = SIZES[axis]
    return lax.ppermute(a, axis, [(i, (i + d) % n) for i in range(n)])


def ring(piece, axis, up):
    n = SIZES[axis]
    out = [None] * n
    out[0] = piece
    f = b = piece
    for s in range(1, n // 2):
        f = shift(f, axis, 1)
        b = shift(b, axis, -1)
        out[s] = f
        out[n - s] = b
    out[n // 2] = shift(f, axis, 1) if up else shift(b, axis, -1)
    return out


def wide(a):
    return a.astype(F32)


def reduce_ring(terms, axis, up):
    n = SIZES[axis]
    h = n // 2
    b = None
    for d in range(h if up else h - 1, 0, -1):
        t = terms[d] if b is None else (wide(b) + wide(terms[d])).astype(BF)
        b = shift(t, axis, -1)
    f = None
    for d in range(h - 1 if up else h, 0, -1):
        t = terms[n - d] if f is None else (wide(f) + wide(terms[n - d])).astype(BF)
        f = shift(t, axis, 1)
    return wide(b) + wide(f) + wide(terms[0])


def score_rows(k, q):
    return dot(k, q, NT) * SCALE2


def keep_mask(off):
    i = lax.broadcasted_iota(jnp.int32, (HALF, HALF), 0)
    j = lax.broadcasted_iota(jnp.int32, (HALF, HALF), 1)
    return (i - j) <= off


def forward_kernel(info, k_ref, v_ref, q_ref, m_ref, l_ref, acc_ref):
    slot = pl.program_id(0)
    core = info[32]

    @pl.when(slot == 0)
    def _():
        m_ref[...] = jnp.full_like(m_ref, NEG)
        l_ref[...] = jnp.zeros_like(l_ref)
        acc_ref[...] = jnp.zeros_like(acc_ref)

    def step(masked):
        k = k_ref[0]
        v = v_ref[0]
        for half in range(2):
            if masked:
                keep = keep_mask(half * HALF * (1 - 2 * core))
            for h in range(GROUP):
                cols = pl.ds(h * HALF, HALF)
                s = score_rows(k, q_ref[half, cols, :])
                if masked:
                    s = jnp.where(keep, s, MASKED)
                m_old = m_ref[half, :, cols]
                m_new = jnp.maximum(m_old, jnp.max(s, axis=0, keepdims=True))
                alpha = jnp.exp2(m_old - m_new)
                p = jnp.exp2(s - m_new)
                m_ref[half, :, cols] = m_new
                l_ref[half, :, cols] = l_ref[half, :, cols] * alpha + jnp.sum(p, axis=0, keepdims=True)
                acc_ref[half, :, cols] = acc_ref[half, :, cols] * alpha + dot(v, p.astype(BF), TN)

    @pl.when(slot == 0)
    def _():
        step(True)

    @pl.when((slot > 0) & (slot <= info[33]))
    def _():
        step(False)


def backward_kernel(
    info, k_ref, v_ref, q_ref, g_ref, m_ref, l_ref, acc_ref, m2_ref, l2_ref, acc2_ref, gk_in, gv_in,
    att_ref, dq_ref, gk_ref, gv_ref, lse_ref, delta_ref, dqt_ref, p_ref, ds_ref,
):
    slot = pl.program_id(0)
    core = info[32]

    @pl.when(slot == 0)
    def _():
        dqt_ref[...] = jnp.zeros_like(dqt_ref)
        for half in range(2):
            other = 1 - half
            m0 = m_ref[half]
            m1 = m2_ref[other]
            m = jnp.maximum(m0, m1)
            e0 = jnp.exp2(m0 - m)
            e1 = jnp.exp2(m1 - m)
            total = l_ref[half] * e0 + l2_ref[other] * e1
            lse_ref[half] = m + jnp.log2(total)
            inv = 1.0 / total
            e0 = e0 * inv
            e1 = e1 * inv
            for h in range(GROUP):
                cols = pl.ds(h * HALF, HALF)
                part = slice(h * HALF, (h + 1) * HALF)
                out = acc_ref[half, :, cols] * e0[:, part] + acc2_ref[other, :, cols] * e1[:, part]
                rows = jnp.transpose(out).astype(BF)
                if half == 0:
                    att_ref[:, h * HEAD_DIM : (h + 1) * HEAD_DIM] = rows
                g = wide(g_ref[half, cols, :])
                d = jnp.sum(jnp.transpose(g * wide(rows)), axis=0, keepdims=True)
                delta_ref[half, :, cols] = d

    def step(masked):
        k = k_ref[0]
        v = v_ref[0]
        for half in range(2):
            if masked:
                keep = keep_mask(half * HALF * (1 - 2 * core))
            for h in range(GROUP):
                cols = pl.ds(h * HALF, HALF)
                flat = pl.ds(half * COLS + h * HALF, HALF)
                s = score_rows(k, q_ref[half, cols, :])
                if masked:
                    s = jnp.where(keep, s, MASKED)
                p = jnp.exp2(s - lse_ref[half, :, cols])
                p_ref[:, flat] = p.astype(BF)
                dp = dot(v, g_ref[half, cols, :], NT)
                ds = (p * (dp - delta_ref[half, :, cols])).astype(BF)
                ds_ref[:, flat] = ds
                dqt_ref[half, :, cols] += dot(k, ds, TN)
        q = q_ref[...].reshape(2 * COLS, HEAD_DIM)
        g = g_ref[...].reshape(2 * COLS, HEAD_DIM)
        gk_ref[0] = dot(ds_ref[...], q, NN).astype(BF)
        gv_ref[0] = dot(p_ref[...], g, NN).astype(BF)

    @pl.when(slot == 0)
    def _():
        step(True)

    @pl.when((slot > 0) & (slot <= info[33]))
    def _():
        step(False)

    @pl.when(slot > info[33])
    def _():
        gk_ref[...] = jnp.zeros_like(gk_ref)
        gv_ref[...] = jnp.zeros_like(gv_ref)

    @pl.when(slot == TOPK)
    def _():
        for half in range(2):
            for h in range(GROUP):
                cols = pl.ds(h * HALF, HALF)
                dq_ref[half, :, h * HEAD_DIM : (h + 1) * HEAD_DIM] = jnp.transpose(dqt_ref[half, :, cols])


def whole(shape):
    return pl.BlockSpec(shape, lambda i, info: (0,) * len(shape))


def piece_spec(base):
    return pl.BlockSpec((1, HALF, HEAD_DIM), lambda i, info: (info[base + i], 0, 0))


VMEM_LIMIT = 48 * 1024 * 1024
STAT = (2, 1, COLS)
ACC = (2, HEAD_DIM, COLS)
ROWS = (2, COLS, HEAD_DIM)
FLOPS = 2 * 9 * HALF * 2 * COLS * HEAD_DIM


def forward(info, k, v, q):
    return pl.pallas_call(
        forward_kernel,
        grid_spec=pltpu.PrefetchScalarGridSpec(
            num_scalar_prefetch=1,
            grid=(TOPK + 1,),
            in_specs=[piece_spec(0), piece_spec(10), whole(ROWS)],
            out_specs=[whole(STAT), whole(STAT), whole(ACC)],
        ),
        out_shape=[
            jax.ShapeDtypeStruct(STAT, F32),
            jax.ShapeDtypeStruct(STAT, F32),
            jax.ShapeDtypeStruct(ACC, F32),
        ],
        compiler_params=pltpu.CompilerParams(vmem_limit_bytes=VMEM_LIMIT),
        cost_estimate=pl.CostEstimate(flops=2 * FLOPS, bytes_accessed=1 << 22, transcendentals=1 << 22),
        name="forward",
    )(info, k, v, q)


def backward(info, k, v, q, g, mine, other, gk, gv):
    return pl.pallas_call(
        backward_kernel,
        grid_spec=pltpu.PrefetchScalarGridSpec(
            num_scalar_prefetch=1,
            grid=(TOPK + 1,),
            in_specs=[piece_spec(0), piece_spec(10), whole(ROWS), whole(ROWS)]
            + [whole(STAT), whole(STAT), whole(ACC)] * 2
            + [pl.BlockSpec(memory_space=pl.ANY)] * 2,
            out_specs=[
                whole((HALF, GROUP * HEAD_DIM)),
                whole((2, HALF, GROUP * HEAD_DIM)),
                piece_spec(20),
                piece_spec(34),
            ],
            scratch_shapes=[
                pltpu.VMEM(STAT, F32),
                pltpu.VMEM(STAT, F32),
                pltpu.VMEM(ACC, F32),
                pltpu.VMEM((HALF, 2 * COLS), BF),
                pltpu.VMEM((HALF, 2 * COLS), BF),
            ],
        ),
        out_shape=[
            jax.ShapeDtypeStruct((HALF, GROUP * HEAD_DIM), BF),
            jax.ShapeDtypeStruct((2, HALF, GROUP * HEAD_DIM), F32),
            jax.ShapeDtypeStruct(gk.shape, BF),
            jax.ShapeDtypeStruct(gv.shape, BF),
        ],
        input_output_aliases={11: 2, 12: 3},
        compiler_params=pltpu.CompilerParams(vmem_limit_bytes=VMEM_LIMIT),
        cost_estimate=pl.CostEstimate(flops=5 * FLOPS, bytes_accessed=1 << 23, transcendentals=1 << 22),
        name="backward",
    )(info, k, v, q, g, *mine, *other, gk, gv)


def plan(gate_score):
    z = lax.axis_index("z")
    x = lax.axis_index("x")
    core = lax.axis_index("core")
    own = z * 4 + x
    totals = lax.psum(gate_score.reshape(8, 128), "head").reshape(NBLK, NBLK)
    row = lax.dynamic_slice_in_dim(totals, own, 1, 0)[0]
    columns = jnp.arange(NBLK, dtype=jnp.int32)
    ranked = jnp.where(columns < own, row * NBLK + columns, -1)
    rank = jnp.sum((ranked[None, :] > ranked[:, None]).astype(jnp.int32), axis=1)
    hit = (rank[None, :] == columns[:TOPK, None]) & (ranked[None, :] >= 0)
    picked = jnp.sum(jnp.where(hit, columns[None, :], 0), axis=1)
    count = jnp.minimum(own, TOPK)
    live = columns[:TOPK] < count
    dz = jnp.where(live, (z - picked // 4) % 8, 0)
    dx = jnp.where(live, (x - picked % 4) % 4, 0)
    zero = jnp.zeros((1,), jnp.int32)
    at_k = jnp.concatenate([zero, dz * 4 + dx])
    at_v = jnp.concatenate([zero, dx * 8 + dz])
    to_k = jnp.concatenate([zero, jnp.where(live, dz * 4 + dx, PIECES)])
    to_v = jnp.concatenate([zero, jnp.where(live, dx * 8 + dz, PIECES)])
    return jnp.concatenate([at_k, zero, at_v, zero, to_k, zero, zero, zero, core[None], count[None], to_v])


def heads_first(a):
    return jnp.transpose(a.reshape(HALF, GROUP, HEAD_DIM), (1, 0, 2)).reshape(COLS, HEAD_DIM)


def on_device(query, key, value, grad_out, gate_score):
    swap = functools.partial(shift, axis="core", d=1)
    q_own = heads_first(query)
    g_own = heads_first(grad_out)
    q = jnp.stack([q_own, swap(q_own)])
    g = jnp.stack([g_own, swap(g_own)])
    info = plan(gate_score)

    row = jnp.stack([key, shift(key, "x", 1), shift(key, "x", 2), shift(key, "x", -1)])
    k = jnp.concatenate(ring(row, "z", True))
    column = jnp.stack(ring(value, "z", False))
    v = jnp.concatenate(ring(column, "x", False))

    mine = forward(info, k, v, q)
    other = [swap(a) for a in mine]
    gk = jnp.zeros((PIECES + 1, HALF, HEAD_DIM), BF)
    gv = jnp.zeros((PIECES + 1, HALF, HEAD_DIM), BF)
    attended, dq, gk, gv = backward(info, k, v, q, g, mine, other, gk, gv)
    grad_query = ((dq[0] + swap(dq[1])) * SCALE).astype(BF)

    s = reduce_ring([gk[4 * d : 4 * d + 4] for d in range(8)], "z", True).astype(BF)
    total = wide(s[0]) + wide(shift(s[1], "x", -1)) + wide(shift(s[2], "x", 2)) + wide(shift(s[3], "x", 1))
    grad_key = (total * SCALE).astype(BF)
    s = reduce_ring([gv[8 * d : 8 * d + 8] for d in range(4)], "x", False).astype(BF)
    grad_value = reduce_ring([s[d] for d in range(8)], "z", False).astype(BF)
    return (attended, grad_query, grad_key, grad_value)


def solution(mesh):
    devices = mesh.devices.reshape(8, 4, 2, 4)
    split = Mesh(devices, ("z", "x", "core", "head"))
    seq = ("z", "x", "core")
    spec = P(seq, "head")
    return jax.shard_map(
        on_device,
        mesh=split,
        in_specs=(spec, spec, spec, spec, P("head", None, None)),
        out_specs=(spec, spec, spec, spec),
        check_vma=False,
    )
```

```python
import functools
import math

import jax
import jax.numpy as jnp
from jax import lax
from jax.experimental import pallas as pl
from jax.experimental.pallas import tpu as pltpu
from jax.sharding import Mesh
from jax.sharding import PartitionSpec as P

HEAD_DIM = 128
GROUP = 4
TOPK = 8
NBLK = 32
HALF = 256
COLS = GROUP * HALF
SCALE = 1.0 / math.sqrt(HEAD_DIM)
SCALE2 = SCALE / math.log(2.0)
NEG = -1e30
MASKED = -3e38
BF = jnp.bfloat16
F32 = jnp.float32
SIZES = {"z": 8, "x": 4, "core": 2, "head": 4}
NT = (((1,), (1,)), ((), ()))
NN = (((1,), (0,)), ((), ()))
CORE_AT = 32
VMEM_LIMIT = 40 * 1024 * 1024
STAT = (2, 3, COLS)
ACC = (HEAD_DIM, COLS)
ROWS = (COLS, HEAD_DIM)
PIECE = (HALF, 2 * HEAD_DIM)
SLOT_FLOPS = 2 * HALF * 2 * COLS * HEAD_DIM


def dot(a, b, dims):
    return lax.dot_general(a, b, dims, preferred_element_type=F32)


def wide(a):
    return a.astype(F32)


def shift(a, axis, d):
    n = SIZES[axis]
    return lax.ppermute(a, axis, [(i, (i + d) % n) for i in range(n)])


def keep_mask(off):
    i = lax.broadcasted_iota(jnp.int32, (HALF, HALF), 0)
    j = lax.broadcasted_iota(jnp.int32, (HALF, HALF), 1)
    return (i - j) <= off


def fetch(i, kv_refs, sizes, kv_buf):
    if len(kv_refs) == 1:
        return kv_refs[0][0]

    @pl.when(i < sizes[0])
    def _():
        kv_buf[...] = kv_refs[0][0]

    @pl.when(i >= sizes[0])
    def _():
        kv_buf[...] = kv_refs[1][0]

    return kv_buf[...]


def forward_kernel(base, sizes, first, last, info, *refs):
    n = len(sizes)
    kv_refs, refs = refs[:n], refs[n:]
    q_refs, refs = refs[:2], refs[2:]
    if last:
        g_refs, refs = refs[:2], refs[2:]
    if not first:
        stat_in, acc_in, refs = refs[0], refs[1:3], refs[3:]
    stat_ref, acc_refs, (s_ref, p_ref, kv_buf) = refs[0], refs[1:3], refs[3:]
    i = pl.program_id(0)
    core = info[CORE_AT]

    @pl.when(i == 0)
    def _():
        if first:
            stat_ref[:, 0:1, :] = jnp.full((2, 1, COLS), NEG, F32)
            stat_ref[:, 1:3, :] = jnp.zeros((2, 2, COLS), F32)
            for half in range(2):
                acc_refs[half][...] = jnp.zeros(ACC, F32)
        else:
            stat_ref[...] = stat_in[...]
            for half in range(2):
                acc_refs[half][...] = acc_in[half][...]

    def step(masked):
        kv = fetch(i, kv_refs, sizes, kv_buf)
        k = kv[:, :HEAD_DIM]
        vt = jnp.transpose(kv[:, HEAD_DIM:])
        for half in range(2):
            s_ref[:, pl.ds(half * COLS, COLS)] = dot(k, q_refs[half][...], NT)
        for half in range(2):
            acc = acc_refs[half]
            if masked:
                keep = keep_mask(half * HALF * (1 - 2 * core))
            for h in range(GROUP):
                cols = pl.ds(h * HALF, HALF)
                flat = pl.ds(half * COLS + h * HALF, HALF)
                s = s_ref[:, flat]
                if masked:
                    s = jnp.where(keep, s, MASKED)
                m_old = stat_ref[half, 0:1, cols]
                m_new = jnp.maximum(m_old, jnp.max(s, axis=0, keepdims=True) * SCALE2)
                alpha = jnp.exp2(m_old - m_new)
                p = jnp.exp2(s * SCALE2 - m_new)
                stat_ref[half, 0:1, cols] = m_new
                stat_ref[half, 1:2, cols] = stat_ref[half, 1:2, cols] * alpha + jnp.sum(p, axis=0, keepdims=True)
                acc[:, cols] = acc[:, cols] * alpha
                p_ref[:, flat] = p.astype(BF)
            acc[...] += dot(vt, p_ref[:, pl.ds(half * COLS, COLS)], NN)

    if first:
        pl.when(i == 0)(lambda: step(True))
        pl.when((i > 0) & (info[base + i] > 0))(lambda: step(False))
    else:
        pl.when(info[base + i] > 0)(lambda: step(False))

    if last:

        @pl.when(i == sum(sizes) - 1)
        def _():
            eye = (
                lax.broadcasted_iota(jnp.int32, (HEAD_DIM, HEAD_DIM), 0)
                == lax.broadcasted_iota(jnp.int32, (HEAD_DIM, HEAD_DIM), 1)
            ).astype(F32).astype(BF)
            for half in range(2):
                turned = dot(eye, g_refs[half][...], NT)
                stat_ref[half, 2:3, :] = jnp.sum(turned * acc_refs[half][...], axis=0, keepdims=True)


def combine(mine, other, half):
    m0 = mine[half, 0:1, :]
    m1 = other[1 - half, 0:1, :]
    m = jnp.maximum(m0, m1)
    e0 = jnp.exp2(m0 - m)
    e1 = jnp.exp2(m1 - m)
    total = mine[half, 1:2, :] * e0 + other[1 - half, 1:2, :] * e1
    return m + jnp.log2(total), e0 / total, e1 / total


def backward_kernel(base, sizes, first, masks, info, *refs):
    n = len(sizes)
    kv_refs, refs = refs[:n], refs[n:]
    q_refs, g_refs, mine, other, refs = refs[:2], refs[2:4], refs[4], refs[5], refs[6:]
    if not first:
        dq_in, refs = refs[:2], refs[2:]
    dq_refs, out_refs, refs = refs[:2], refs[2 : 2 + n], refs[2 + n :]
    row_ref, s_ref, dp_ref, p_ref, ds_ref, kv_buf, out_buf = refs
    i = pl.program_id(0)
    core = info[CORE_AT]

    @pl.when(i == 0)
    def _():
        for half in range(2):
            lse, w0, w1 = combine(mine, other, half)
            row_ref[half, 0:1, :] = lse
            row_ref[half, 1:2, :] = mine[half, 2:3, :] * w0 + other[1 - half, 2:3, :] * w1
            dq_refs[half][...] = jnp.zeros(ACC, F32) if first else dq_in[half][...]

    def step(masked):
        kv = fetch(i, kv_refs, sizes, kv_buf)
        k = kv[:, :HEAD_DIM]
        v = kv[:, HEAD_DIM:]
        kt = jnp.transpose(k)
        for half in range(2):
            cols = pl.ds(half * COLS, COLS)
            s_ref[:, cols] = dot(k, q_refs[half][...], NT)
            dp_ref[:, cols] = dot(v, g_refs[half][...], NT)
        for half in range(2):
            if masked:
                keep = keep_mask(half * HALF * (1 - 2 * core))
            for h in range(GROUP):
                cols = pl.ds(h * HALF, HALF)
                flat = pl.ds(half * COLS + h * HALF, HALF)
                p = jnp.exp2(s_ref[:, flat] * SCALE2 - row_ref[half, 0:1, cols])
                if masked:
                    p = jnp.where(keep, p, 0.0)
                p_ref[:, flat] = p.astype(BF)
                ds_ref[:, flat] = (p * (dp_ref[:, flat] - row_ref[half, 1:2, cols])).astype(BF)
            dq_refs[half][...] += dot(kt, ds_ref[:, pl.ds(half * COLS, COLS)], NN)
        dk = jnp.zeros((HALF, HEAD_DIM), F32)
        dv = jnp.zeros((HALF, HEAD_DIM), F32)
        for half in range(2):
            cols = pl.ds(half * COLS, COLS)
            dk = dk + dot(ds_ref[:, cols], q_refs[half][...], NN)
            dv = dv + dot(p_ref[:, cols], g_refs[half][...], NN)
        out_buf[:, :HEAD_DIM] = dk.astype(BF)
        out_buf[:, HEAD_DIM:] = dv.astype(BF)

    live = info[base + i] > 0
    if masks:
        pl.when(i == 0)(lambda: step(True))
        pl.when((i > 0) & live)(lambda: step(False))
    else:
        pl.when(live)(lambda: step(False))

    @pl.when(jnp.logical_not(live))
    def _():
        out_buf[...] = jnp.zeros(PIECE, BF)

    if n == 1:
        out_refs[0][0] = out_buf[...]
    else:

        @pl.when(i < sizes[0])
        def _():
            out_refs[0][0] = out_buf[...]

        @pl.when(i >= sizes[0])
        def _():
            out_refs[1][0] = out_buf[...]


def finish_kernel(mine, other, acc_mine, acc_other, dq_mine, dq_other, att_ref, dq_ref):
    lse, w0, w1 = combine(mine, other, 0)
    for h in range(GROUP):
        cols = slice(h * HALF, (h + 1) * HALF)
        rows = slice(h * HEAD_DIM, (h + 1) * HEAD_DIM)
        out = acc_mine[:, cols] * w0[:, cols] + acc_other[:, cols] * w1[:, cols]
        att_ref[:, rows] = jnp.transpose(out).astype(BF)
        dq_ref[:, rows] = jnp.transpose((dq_mine[:, cols] + dq_other[:, cols]) * SCALE).astype(BF)


def whole(shape):
    return pl.BlockSpec(shape, lambda i, info: (0,) * len(shape))


def piece_specs(sizes):
    block = (1,) + PIECE
    if len(sizes) == 1:
        return [pl.BlockSpec(block, lambda i, info: (i, 0, 0))]
    n = sizes[0]
    return [
        pl.BlockSpec(block, lambda i, info: (jnp.minimum(i, n - 1), 0, 0)),
        pl.BlockSpec(block, lambda i, info: (jnp.maximum(i - n, 0), 0, 0)),
    ]


def cost(slots, products):
    return pl.CostEstimate(
        flops=slots * products * SLOT_FLOPS, bytes_accessed=1 << 22, transcendentals=slots * HALF * 2 * COLS
    )


def forward(base, info, kvs, q, state, g):
    sizes = [a.shape[0] for a in kvs]
    first = state is None
    last = g is not None
    ins = list(kvs) + list(q) + (list(g) if last else []) + ([] if first else list(state))
    specs = piece_specs(sizes) + [whole(ROWS)] * (4 if last else 2)
    if not first:
        specs += [whole(STAT), whole(ACC), whole(ACC)]
    return pl.pallas_call(
        functools.partial(forward_kernel, base, sizes, first, last),
        grid_spec=pltpu.PrefetchScalarGridSpec(
            num_scalar_prefetch=1,
            grid=(sum(sizes),),
            in_specs=specs,
            out_specs=[whole(STAT), whole(ACC), whole(ACC)],
            scratch_shapes=[
                pltpu.VMEM((HALF, 2 * COLS), F32),
                pltpu.VMEM((HALF, 2 * COLS), BF),
                pltpu.VMEM(PIECE, BF),
            ],
        ),
        out_shape=[jax.ShapeDtypeStruct(s, F32) for s in (STAT, ACC, ACC)],
        compiler_params=pltpu.CompilerParams(vmem_limit_bytes=VMEM_LIMIT),
        cost_estimate=cost(3, 2),
        name="forward",
    )(info, *ins)


def backward(base, info, kvs, q, g, mine, other, dq):
    sizes = [a.shape[0] for a in kvs]
    first = dq is None
    ins = list(kvs) + list(q) + list(g) + [mine, other] + ([] if first else list(dq))
    specs = piece_specs(sizes) + [whole(ROWS)] * 4 + [whole(STAT)] * 2
    if not first:
        specs += [whole(ACC), whole(ACC)]
    wide_shape = (HALF, 2 * COLS)
    res = pl.pallas_call(
        functools.partial(backward_kernel, base, sizes, first, base == 0),
        grid_spec=pltpu.PrefetchScalarGridSpec(
            num_scalar_prefetch=1,
            grid=(sum(sizes),),
            in_specs=specs,
            out_specs=[whole(ACC), whole(ACC)] + piece_specs(sizes),
            scratch_shapes=[
                pltpu.VMEM((2, 2, COLS), F32),
                pltpu.VMEM(wide_shape, F32),
                pltpu.VMEM(wide_shape, F32),
                pltpu.VMEM(wide_shape, BF),
                pltpu.VMEM(wide_shape, BF),
                pltpu.VMEM(PIECE, BF),
                pltpu.VMEM(PIECE, BF),
            ],
        ),
        out_shape=[jax.ShapeDtypeStruct(ACC, F32)] * 2 + [jax.ShapeDtypeStruct(a.shape, BF) for a in kvs],
        compiler_params=pltpu.CompilerParams(vmem_limit_bytes=VMEM_LIMIT),
        cost_estimate=cost(3, 5),
        name="backward",
    )(info, *ins)
    return res[:2], res[2:]


def finish(mine, other, acc_mine, acc_other, dq_mine, dq_other):
    shape = jax.ShapeDtypeStruct((HALF, GROUP * HEAD_DIM), BF)
    return pl.pallas_call(
        finish_kernel,
        out_shape=[shape, shape],
        compiler_params=pltpu.CompilerParams(vmem_limit_bytes=VMEM_LIMIT),
        cost_estimate=pl.CostEstimate(flops=1 << 20, bytes_accessed=1 << 22, transcendentals=0),
        name="finish",
    )(mine, other, acc_mine, acc_other, dq_mine, dq_other)


def plan(gate_score):
    z = lax.axis_index("z")
    x = lax.axis_index("x")
    own = z * 4 + x
    mine = lax.optimization_barrier(gate_score.reshape(8, 128))
    totals = mine + shift(mine, "head", 1) + shift(mine, "head", 2) + shift(mine, "head", 3)
    row = lax.dynamic_slice_in_dim(totals.reshape(NBLK, NBLK), own, 1, 0)[0]
    columns = jnp.arange(NBLK, dtype=jnp.int32)
    ranked = jnp.where(columns < own, row * NBLK + columns, -1)
    rank = jnp.sum((ranked[None, :] > ranked[:, None]).astype(jnp.int32), axis=1)
    used = ((rank < TOPK) & (ranked >= 0)) | (columns == own)
    dz = (z - columns // 4) % 8
    dx = (x - columns % 4) % 4
    group = jnp.where(dx < 2, dx, 5 - dx)
    place = group * 8 + dz
    live = jnp.sum((place[None, :] == columns[:, None]) & used[None, :], axis=1, dtype=jnp.int32)
    return jnp.concatenate([live, lax.axis_index("core")[None]])


def heads_first(a):
    return jnp.transpose(a.reshape(HALF, GROUP, HEAD_DIM), (1, 0, 2)).reshape(ROWS)


def gather_z(piece):
    a1, b1 = shift(piece, "z", 1), shift(piece, "z", -1)
    a2, b2 = shift(piece, "z", 2), shift(piece, "z", -2)
    a3, b3, a4 = shift(a2, "z", 1), shift(b2, "z", -1), shift(a2, "z", 2)
    return jnp.stack([piece, a1, a2, a3, a4, b3, b2, b1])


def scatter_z(t):
    a = shift(t[3], "z", -1)
    b = shift(t[4], "z", -2)
    c = shift(t[5], "z", 1)
    t2 = (wide(t[2]) + wide(a) + wide(b)).astype(BF)
    t6 = (wide(t[6]) + wide(c)).astype(BF)
    parts = [shift(t2, "z", -2), shift(t[1], "z", -1), shift(t6, "z", 2), shift(t[7], "z", 1)]
    return wide(t[0]) + sum(wide(a) for a in parts)


def on_device(query, key, value, grad_out, gate_score):
    swap = functools.partial(shift, axis="core", d=1)
    kv0 = gather_z(jnp.concatenate([key, value], axis=1))
    q = heads_first(query)
    g = heads_first(grad_out)
    q = (q, swap(q))
    g = (g, swap(g))
    info = plan(gate_score)

    kv1 = shift(kv0, "x", 1)
    kv3 = shift(kv0, "x", -1)
    kv2 = (shift(kv1[:4], "x", 1), shift(kv3[4:], "x", -1))

    state = forward(0, info, [kv0], q, None, None)
    state = forward(8, info, [kv1, kv3], q, state, None)
    mine, acc, acc_away = forward(24, info, kv2, q, state, g)
    other = swap(mine)
    acc_other = swap(acc_away)

    dq, (low, high) = backward(24, info, kv2, q, g, mine, other, None)
    low = shift(low, "x", -1)
    high = shift(high, "x", 1)
    dq, (t1, t3) = backward(8, info, [kv1, kv3], q, g, mine, other, dq)
    t1 = jnp.concatenate([(wide(t1[:4]) + wide(low)).astype(BF), t1[4:]])
    t3 = jnp.concatenate([t3[:4], (wide(t3[4:]) + wide(high)).astype(BF)])
    t1 = shift(t1, "x", -1)
    t3 = shift(t3, "x", 1)
    dq, (t0,) = backward(0, info, [kv0], q, g, mine, other, dq)
    total = scatter_z((wide(t0) + wide(t1) + wide(t3)).astype(BF))
    grad_key = (total[:, :HEAD_DIM] * SCALE).astype(BF)
    grad_value = total[:, HEAD_DIM:].astype(BF)
    attended, grad_query = finish(mine, other, acc, acc_other, dq[0], swap(dq[1]))
    return (attended, grad_query, grad_key, grad_value)


def solution(mesh):
    devices = mesh.devices.reshape(8, 4, 2, 4)
    split = Mesh(devices, ("z", "x", "core", "head"))
    spec = P(("z", "x", "core"), "head")
    return jax.shard_map(
        on_device,
        mesh=split,
        in_specs=(spec, spec, spec, spec, P("head", None, None)),
        out_specs=(spec, spec, spec, spec),
        check_vma=False,
    )
```

```python
import functools
import math

import jax
import jax.numpy as jnp
from jax import lax
from jax.experimental import pallas as pl
from jax.experimental.pallas import tpu as pltpu
from jax.sharding import Mesh
from jax.sharding import PartitionSpec as P

HEAD_DIM = 128
GROUP = 4
TOPK = 8
NBLK = 32
HALF = 256
COLS = GROUP * HALF
SCALE = 1.0 / math.sqrt(HEAD_DIM)
SCALE2 = SCALE / math.log(2.0)
NEG = -1e30
MASKED = -3e38
BF = jnp.bfloat16
F32 = jnp.float32
SIZES = {"z": 8, "x": 4, "core": 2, "head": 4}
NT = (((1,), (1,)), ((), ()))
NN = (((1,), (0,)), ((), ()))
CORE_AT = 32
QUAD = 4
VMEM_LIMIT = 40 * 1024 * 1024
STAT = (2, 3, COLS)
ACC = (HEAD_DIM, COLS)
PAIR = (2, COLS, HEAD_DIM)
PIECE = (HALF, 2 * HEAD_DIM)


def dot(a, b, dims):
    return lax.dot_general(a, b, dims, preferred_element_type=F32)


def wide(a):
    return a.astype(F32)


def shift(a, axis, d):
    n = SIZES[axis]
    return lax.ppermute(a, axis, [(i, (i + d) % n) for i in range(n)])


def keep_mask(off):
    i = lax.broadcasted_iota(jnp.int32, (HALF, HALF), 0)
    j = lax.broadcasted_iota(jnp.int32, (HALF, HALF), 1)
    return (i - j) <= off


def fetch(i, kv_refs, kv_buf):
    for a, ref in enumerate(kv_refs):

        @pl.when(i // QUAD == a)
        def _():
            kv_buf[...] = ref[0]

    return kv_buf[...]


def query_refs(refs):
    return [ref.at[0] for ref in refs]


def grad_refs(refs):
    return [ref.at[1] for ref in refs]


def forward_kernel(base, n, first, last, info, *refs):
    kv_refs, refs = refs[:n], refs[n:]
    q_refs, g_refs, refs = query_refs(refs[:2]), grad_refs(refs[:2]), refs[2:]
    if not first:
        stat_in, acc_in, refs = refs[0], refs[1:3], refs[3:]
    stat_ref, acc_refs, (s_ref, p_ref, kv_buf) = refs[0], refs[1:3], refs[3:]
    i = pl.program_id(0)
    core = info[CORE_AT]

    @pl.when(i == 0)
    def _():
        if first:
            stat_ref[:, 0:1, :] = jnp.full((2, 1, COLS), NEG, F32)
            stat_ref[:, 1:3, :] = jnp.zeros((2, 2, COLS), F32)
            for half in range(2):
                acc_refs[half][...] = jnp.zeros(ACC, F32)
        else:
            stat_ref[...] = stat_in[...]
            for half in range(2):
                acc_refs[half][...] = acc_in[half][...]

    def step(masked):
        kv = fetch(i, kv_refs, kv_buf)
        k = kv[:, :HEAD_DIM]
        vt = jnp.transpose(kv[:, HEAD_DIM:])
        for half in range(2):
            s_ref[:, pl.ds(half * COLS, COLS)] = dot(k, q_refs[half][...], NT)
        for half in range(2):
            acc = acc_refs[half]
            if masked:
                keep = keep_mask(half * HALF * (1 - 2 * core))
            for h in range(GROUP):
                cols = pl.ds(h * HALF, HALF)
                flat = pl.ds(half * COLS + h * HALF, HALF)
                s = s_ref[:, flat]
                if masked:
                    s = jnp.where(keep, s, MASKED)
                m_old = stat_ref[half, 0:1, cols]
                m_new = jnp.maximum(m_old, jnp.max(s, axis=0, keepdims=True) * SCALE2)
                alpha = jnp.exp2(m_old - m_new)
                p = jnp.exp2(s * SCALE2 - m_new)
                stat_ref[half, 0:1, cols] = m_new
                stat_ref[half, 1:2, cols] = stat_ref[half, 1:2, cols] * alpha + jnp.sum(p, axis=0, keepdims=True)
                acc[:, cols] = acc[:, cols] * alpha
                p_ref[:, flat] = p.astype(BF)
            acc[...] += dot(vt, p_ref[:, pl.ds(half * COLS, COLS)], NN)

    if first:
        pl.when(i == 0)(lambda: step(True))
        pl.when((i > 0) & (info[base + i] > 0))(lambda: step(False))
    else:
        pl.when(info[base + i] > 0)(lambda: step(False))

    if last:

        @pl.when(i == QUAD * n - 1)
        def _():
            eye = (
                lax.broadcasted_iota(jnp.int32, (HEAD_DIM, HEAD_DIM), 0)
                == lax.broadcasted_iota(jnp.int32, (HEAD_DIM, HEAD_DIM), 1)
            ).astype(F32).astype(BF)
            for half in range(2):
                turned = dot(eye, g_refs[half][...], NT)
                stat_ref[half, 2:3, :] = jnp.sum(turned * acc_refs[half][...], axis=0, keepdims=True)


def combine(mine, other, half):
    m0 = mine[half, 0:1, :]
    m1 = other[1 - half, 0:1, :]
    m = jnp.maximum(m0, m1)
    e0 = jnp.exp2(m0 - m)
    e1 = jnp.exp2(m1 - m)
    total = mine[half, 1:2, :] * e0 + other[1 - half, 1:2, :] * e1
    return m + jnp.log2(total), e0 / total, e1 / total


def backward_kernel(base, n, first, masks, info, *refs):
    kv_refs, refs = refs[:n], refs[n:]
    q_refs, g_refs, refs = query_refs(refs[:2]), grad_refs(refs[:2]), refs[2:]
    mine, other, refs = refs[0], refs[1], refs[2:]
    if not first:
        dq_in, refs = refs[:2], refs[2:]
    dq_refs, out_refs, refs = refs[:2], refs[2 : 2 + n], refs[2 + n :]
    row_ref, s_ref, dp_ref, p_ref, ds_ref, kv_buf, out_buf = refs
    i = pl.program_id(0)
    core = info[CORE_AT]

    @pl.when(i == 0)
    def _():
        for half in range(2):
            lse, w0, w1 = combine(mine, other, half)
            row_ref[half, 0:1, :] = lse
            row_ref[half, 1:2, :] = mine[half, 2:3, :] * w0 + other[1 - half, 2:3, :] * w1
            dq_refs[half][...] = jnp.zeros(ACC, F32) if first else dq_in[half][...]

    def step(masked):
        kv = fetch(i, kv_refs, kv_buf)
        k = kv[:, :HEAD_DIM]
        v = kv[:, HEAD_DIM:]
        kt = jnp.transpose(k)
        for half in range(2):
            cols = pl.ds(half * COLS, COLS)
            s_ref[:, cols] = dot(k, q_refs[half][...], NT)
            dp_ref[:, cols] = dot(v, g_refs[half][...], NT)
        for half in range(2):
            if masked:
                keep = keep_mask(half * HALF * (1 - 2 * core))
            for h in range(GROUP):
                cols = pl.ds(h * HALF, HALF)
                flat = pl.ds(half * COLS + h * HALF, HALF)
                p = jnp.exp2(s_ref[:, flat] * SCALE2 - row_ref[half, 0:1, cols])
                if masked:
                    p = jnp.where(keep, p, 0.0)
                p_ref[:, flat] = p.astype(BF)
                ds_ref[:, flat] = (p * (dp_ref[:, flat] - row_ref[half, 1:2, cols])).astype(BF)
            dq_refs[half][...] += dot(kt, ds_ref[:, pl.ds(half * COLS, COLS)], NN)
        dk = jnp.zeros((HALF, HEAD_DIM), F32)
        dv = jnp.zeros((HALF, HEAD_DIM), F32)
        for half in range(2):
            cols = pl.ds(half * COLS, COLS)
            dk = dk + dot(ds_ref[:, cols], q_refs[half][...], NN)
            dv = dv + dot(p_ref[:, cols], g_refs[half][...], NN)
        out_buf[:, :HEAD_DIM] = dk.astype(BF)
        out_buf[:, HEAD_DIM:] = dv.astype(BF)

    live = info[base + i] > 0
    if masks:
        pl.when(i == 0)(lambda: step(True))
        pl.when((i > 0) & live)(lambda: step(False))
    else:
        pl.when(live)(lambda: step(False))

    @pl.when(jnp.logical_not(live))
    def _():
        out_buf[...] = jnp.zeros(PIECE, BF)

    for a, ref in enumerate(out_refs):

        @pl.when(i // QUAD == a)
        def _():
            ref[0] = out_buf[...]


def finish_kernel(mine, other, acc_mine, acc_other, dq_mine, dq_other, att_ref, dq_ref):
    lse, w0, w1 = combine(mine, other, 0)
    for h in range(GROUP):
        cols = slice(h * HALF, (h + 1) * HALF)
        rows = slice(h * HEAD_DIM, (h + 1) * HEAD_DIM)
        out = acc_mine[:, cols] * w0[:, cols] + acc_other[:, cols] * w1[:, cols]
        att_ref[:, rows] = jnp.transpose(out).astype(BF)
        dq_ref[:, rows] = jnp.transpose((dq_mine[:, cols] + dq_other[:, cols]) * SCALE).astype(BF)


def whole(shape):
    return pl.BlockSpec(shape, lambda i, info: (0,) * len(shape))


def piece_specs(n):
    def spec(a):
        return pl.BlockSpec((1,) + PIECE, lambda i, info: (jnp.clip(i - QUAD * a, 0, QUAD - 1), 0, 0))

    return [spec(a) for a in range(n)]


def cost(flops):
    return pl.CostEstimate(flops=flops, bytes_accessed=1 << 16, transcendentals=0)


def forward(base, info, kvs, qg, state, last):
    n = len(kvs)
    first = state is None
    ins = list(kvs) + list(qg) + ([] if first else list(state))
    specs = piece_specs(n) + [whole(PAIR)] * 2
    if not first:
        specs += [whole(STAT), whole(ACC), whole(ACC)]
    return pl.pallas_call(
        functools.partial(forward_kernel, base, n, first, last),
        grid_spec=pltpu.PrefetchScalarGridSpec(
            num_scalar_prefetch=1,
            grid=(QUAD * n,),
            in_specs=specs,
            out_specs=[whole(STAT), whole(ACC), whole(ACC)],
            scratch_shapes=[
                pltpu.VMEM((HALF, 2 * COLS), F32),
                pltpu.VMEM((HALF, 2 * COLS), BF),
                pltpu.VMEM(PIECE, BF),
            ],
        ),
        out_shape=[jax.ShapeDtypeStruct(s, F32) for s in (STAT, ACC, ACC)],
        compiler_params=pltpu.CompilerParams(vmem_limit_bytes=VMEM_LIMIT),
        cost_estimate=cost(200_000_000),
        name="forward",
    )(info, *ins)


def backward(base, info, kvs, qg, mine, other, dq):
    n = len(kvs)
    first = dq is None
    ins = list(kvs) + list(qg) + [mine, other] + ([] if first else list(dq))
    specs = piece_specs(n) + [whole(PAIR)] * 2 + [whole(STAT)] * 2
    if not first:
        specs += [whole(ACC), whole(ACC)]
    wide_shape = (HALF, 2 * COLS)
    res = pl.pallas_call(
        functools.partial(backward_kernel, base, n, first, base == 0),
        grid_spec=pltpu.PrefetchScalarGridSpec(
            num_scalar_prefetch=1,
            grid=(QUAD * n,),
            in_specs=specs,
            out_specs=[whole(ACC), whole(ACC)] + piece_specs(n),
            scratch_shapes=[
                pltpu.VMEM((2, 2, COLS), F32),
                pltpu.VMEM(wide_shape, F32),
                pltpu.VMEM(wide_shape, F32),
                pltpu.VMEM(wide_shape, BF),
                pltpu.VMEM(wide_shape, BF),
                pltpu.VMEM(PIECE, BF),
                pltpu.VMEM(PIECE, BF),
            ],
        ),
        out_shape=[jax.ShapeDtypeStruct(ACC, F32)] * 2 + [jax.ShapeDtypeStruct(a.shape, BF) for a in kvs],
        compiler_params=pltpu.CompilerParams(vmem_limit_bytes=VMEM_LIMIT),
        cost_estimate=cost(200_000_000),
        name="backward",
    )(info, *ins)
    return res[:2], res[2:]


def finish(mine, other, acc_mine, acc_other, dq_mine, dq_other):
    shape = jax.ShapeDtypeStruct((HALF, GROUP * HEAD_DIM), BF)
    return pl.pallas_call(
        finish_kernel,
        out_shape=[shape, shape],
        compiler_params=pltpu.CompilerParams(vmem_limit_bytes=VMEM_LIMIT),
        cost_estimate=pl.CostEstimate(flops=1 << 20, bytes_accessed=1 << 16, transcendentals=0),
        name="finish",
    )(mine, other, acc_mine, acc_other, dq_mine, dq_other)


def join_kernel(k_ref, v_ref, out_ref):
    out_ref[:, :HEAD_DIM] = k_ref[...]
    out_ref[:, HEAD_DIM:] = v_ref[...]


def join(k, v):
    return pl.pallas_call(join_kernel, out_shape=jax.ShapeDtypeStruct(PIECE, BF), name="join")(k, v)


def prepare_kernel(query, grad_out, gate, after, qg_ref, gate_ref):
    for h in range(GROUP):
        rows = slice(h * HALF, (h + 1) * HALF)
        cols = slice(h * HEAD_DIM, (h + 1) * HEAD_DIM)
        qg_ref[0, rows, :] = query[:, cols]
        qg_ref[1, rows, :] = grad_out[:, cols]
    gate_ref[...] = gate[...]


def prepare(query, grad_out, gate, after):
    ins = pl.BlockSpec(memory_space=pltpu.VMEM)
    return pl.pallas_call(
        prepare_kernel,
        in_specs=[ins, ins, ins, pl.BlockSpec(memory_space=pl.ANY)],
        out_shape=[jax.ShapeDtypeStruct(PAIR, BF), jax.ShapeDtypeStruct(gate.shape, jnp.int32)],
        cost_estimate=cost(100_000_000),
        name="prepare",
    )(query, grad_out, gate, after)


def stack_kernel(*refs):
    for i in range(QUAD):
        refs[-1][i] = refs[i][...]


def stack(*pieces):
    return pl.pallas_call(stack_kernel, out_shape=jax.ShapeDtypeStruct((QUAD,) + PIECE, BF), name="stack")(*pieces)


def sum_high_kernel(own, one, three, keep, near_up, near_down, far):
    def total(i):
        return wide(own[i]) + wide(one[i]) + wide(three[i])

    keep[...] = total(0)
    near_down[...] = total(1).astype(BF)
    near_up[...] = total(2).astype(BF)
    far[...] = total(3).astype(BF)


def sum_high(own, one, three):
    shape = jax.ShapeDtypeStruct(PIECE, BF)
    return pl.pallas_call(
        sum_high_kernel,
        out_shape=[jax.ShapeDtypeStruct(PIECE, F32), shape, shape, shape],
        cost_estimate=cost(100_000_000),
        name="sum_high",
    )(own, one, three)


def sum_low_kernel(own, one, three, keep, down, far, up, own_out, near_down, near_up, two_down, two_up):
    def total(i):
        return wide(own[i]) + wide(one[i]) + wide(three[i])

    own_out[...] = total(0)
    near_down[...] = total(1).astype(BF)
    near_up[...] = total(2).astype(BF)
    two_down[...] = (total(3) + wide(down[...]) + wide(far[...])).astype(BF)
    two_up[...] = (keep[...] + wide(up[...])).astype(BF)


def sum_low(own, one, three, keep, down, far, up):
    shape = jax.ShapeDtypeStruct(PIECE, BF)
    return pl.pallas_call(
        sum_low_kernel,
        out_shape=[jax.ShapeDtypeStruct(PIECE, F32), shape, shape, shape, shape],
        cost_estimate=cost(100_000_000),
        name="sum_low",
    )(own, one, three, keep, down, far, up)


def close_kernel(own, a, b, c, d, dk_ref, dv_ref):
    total = own[...] + wide(a[...]) + wide(b[...]) + wide(c[...]) + wide(d[...])
    dk_ref[...] = (total[:, :HEAD_DIM] * SCALE).astype(BF)
    dv_ref[...] = total[:, HEAD_DIM:].astype(BF)


def close(own, parts):
    shape = jax.ShapeDtypeStruct((HALF, HEAD_DIM), BF)
    return pl.pallas_call(close_kernel, out_shape=[shape, shape], name="close")(own, *parts)


def plan(gate):
    z = lax.axis_index("z")
    x = lax.axis_index("x")
    own = z * 4 + x
    totals = gate + lax.ppermute(gate, "head", [(0, 1), (1, 0), (2, 3), (3, 2)])
    totals = totals + lax.ppermute(totals, "head", [(0, 2), (2, 0), (1, 3), (3, 1)])
    row = lax.dynamic_slice_in_dim(totals.reshape(NBLK, NBLK), own, 1, 0)[0]
    columns = jnp.arange(NBLK, dtype=jnp.int32)
    ranked = jnp.where(columns < own, row * NBLK + columns, -1)
    rank = jnp.sum((ranked[None, :] > ranked[:, None]).astype(jnp.int32), axis=1)
    used = ((rank < TOPK) & (ranked >= 0)) | (columns == own)
    dz = (z - columns // 4) % 8
    dx = (x - columns % 4) % 4
    pos = jnp.where(dz == 0, 0, jnp.where(dz <= 4, 2 * dz - 1, 2 * (8 - dz)))
    side = 8 + 4 * (dx // 2) + jnp.where(pos < QUAD, pos, pos + QUAD)
    place = jnp.where(dx == 0, pos, jnp.where(dx == 2, 24 + pos, side))
    live = jnp.sum((place[None, :] == columns[:, None]) & used[None, :], axis=1, dtype=jnp.int32)
    return jnp.concatenate([live, lax.axis_index("core")[None]])


def on_device(query, key, value, grad_out, gate_score):
    swap = functools.partial(shift, axis="core", d=1)
    piece = join(key, value)
    a1, b1 = shift(piece, "z", 1), shift(piece, "z", -1)
    a2, b2 = shift(piece, "z", 2), shift(piece, "z", -2)
    a3, b3, a4 = shift(a2, "z", 1), shift(b2, "z", -1), shift(a2, "z", 2)
    low0 = stack(piece, a1, b1, a2)
    high0 = stack(b2, a3, b3, a4)
    low1, low3 = shift(low0, "x", 1), shift(low0, "x", -1)
    high1, high3 = shift(high0, "x", 1), shift(high0, "x", -1)
    low2, high2 = shift(low1, "x", 1), shift(high3, "x", -1)

    qg, gate = prepare(query, grad_out, gate_score.reshape(8, 128), a3)
    info = plan(gate)
    qg = (qg, swap(qg))

    state = forward(0, info, [low0, high0], qg, None, False)
    state = forward(8, info, [low1, low3, high1, high3], qg, state, False)
    mine, acc, acc_away = forward(24, info, [low2, high2], qg, state, True)
    other = swap(mine)
    acc_other = swap(acc_away)

    dq, (low2, high2) = backward(24, info, [low2, high2], qg, mine, other, None)
    low2 = shift(low2, "x", -1)
    high2 = shift(high2, "x", 1)
    dq, (low1, low3, high1, high3) = backward(8, info, [low1, low3, high1, high3], qg, mine, other, dq)
    high1, low3 = shift(high1, "x", -1), shift(low3, "x", 1)
    high3 = shift((wide(high3) + wide(high2)).astype(BF), "x", 1)
    low1 = shift((wide(low1) + wide(low2)).astype(BF), "x", -1)
    dq, (low0, high0) = backward(0, info, [low0, high0], qg, mine, other, dq)

    keep, up, down, far = sum_high(high0, high1, high3)
    down, far, up = shift(down, "z", -1), shift(far, "z", -2), shift(up, "z", 1)
    own, near_down, near_up, two_down, two_up = sum_low(low0, low1, low3, keep, down, far, up)
    parts = [
        shift(two_up, "z", 2),
        shift(two_down, "z", -2),
        shift(near_down, "z", -1),
        shift(near_up, "z", 1),
    ]
    grad_key, grad_value = close(own, parts)
    attended, grad_query = finish(mine, other, acc, acc_other, dq[0], swap(dq[1]))
    return (attended, grad_query, grad_key, grad_value)


def solution(mesh):
    devices = mesh.devices.reshape(8, 4, 2, 4)
    split = Mesh(devices, ("z", "x", "core", "head"))
    spec = P(("z", "x", "core"), "head")
    return jax.shard_map(
        on_device,
        mesh=split,
        in_specs=(spec, spec, spec, spec, P("head", None, None)),
        out_specs=(spec, spec, spec, spec),
        check_vma=False,
    )
```

```python
import functools
import math

import jax
import jax.numpy as jnp
from jax import lax
from jax.experimental import pallas as pl
from jax.experimental.pallas import tpu as pltpu
from jax.sharding import Mesh
from jax.sharding import PartitionSpec as P

HEAD_DIM = 128
GROUP = 4
TOPK = 8
NBLK = 32
HALF = 256
COLS = GROUP * HALF
SCALE = 1.0 / math.sqrt(HEAD_DIM)
SCALE2 = SCALE / math.log(2.0)
NEG = -1e30
MASKED = -3e38
BF = jnp.bfloat16
F32 = jnp.float32
SIZES = {"z": 8, "x": 4}
NT = (((1,), (1,)), ((), ()))
NN = (((1,), (0,)), ((), ()))
CORE_AT = 32
QUAD = 4
VMEM_LIMIT = 40 * 1024 * 1024
STAT = (2, 3, COLS)
ACC = (HEAD_DIM, COLS)
PAIR = (2, COLS, HEAD_DIM)
PIECE = (HALF, 2 * HEAD_DIM)


def dot(a, b, dims):
    return lax.dot_general(a, b, dims, preferred_element_type=F32)


def wide(a):
    return a.astype(F32)


def shift(a, axis, d):
    n = SIZES[axis]
    return lax.ppermute(a, (axis, "core"), [(2 * i + c, 2 * ((i + d * (1 - 2 * c)) % n) + c) for i in range(n) for c in range(2)])


def swap(a):
    return lax.ppermute(a, "core", [(0, 1), (1, 0)])


def keep_mask(off):
    i = lax.broadcasted_iota(jnp.int32, (HALF, HALF), 0)
    j = lax.broadcasted_iota(jnp.int32, (HALF, HALF), 1)
    return (i - j) <= off


def fetch(i, kv_refs, kv_buf):
    for a, ref in enumerate(kv_refs):

        @pl.when(i // QUAD == a)
        def _():
            kv_buf[...] = ref[0]

    return kv_buf[...]


def query_refs(refs):
    return [ref.at[0] for ref in refs]


def grad_refs(refs):
    return [ref.at[1] for ref in refs]


def forward_kernel(base, n, first, last, info, *refs):
    kv_refs, refs = refs[:n], refs[n:]
    q_refs, g_refs, refs = query_refs(refs[:2]), grad_refs(refs[:2]), refs[2:]
    if not first:
        stat_in, acc_in, refs = refs[0], refs[1:3], refs[3:]
    stat_ref, acc_refs, (s_ref, p_ref, kv_buf) = refs[0], refs[1:3], refs[3:]
    i = pl.program_id(0)
    core = info[CORE_AT]

    @pl.when(i == 0)
    def _():
        if first:
            stat_ref[:, 0:1, :] = jnp.full((2, 1, COLS), NEG, F32)
            stat_ref[:, 1:3, :] = jnp.zeros((2, 2, COLS), F32)
            for half in range(2):
                acc_refs[half][...] = jnp.zeros(ACC, F32)
        else:
            stat_ref[...] = stat_in[...]
            for half in range(2):
                acc_refs[half][...] = acc_in[half][...]

    def step(masked):
        kv = fetch(i, kv_refs, kv_buf)
        k = kv[:, :HEAD_DIM]
        vt = jnp.transpose(kv[:, HEAD_DIM:])
        for half in range(2):
            s_ref[:, pl.ds(half * COLS, COLS)] = dot(k, q_refs[half][...], NT)
        for half in range(2):
            acc = acc_refs[half]
            if masked:
                keep = keep_mask(half * HALF * (1 - 2 * core))
            for h in range(GROUP):
                cols = pl.ds(h * HALF, HALF)
                flat = pl.ds(half * COLS + h * HALF, HALF)
                s = s_ref[:, flat]
                if masked:
                    s = jnp.where(keep, s, MASKED)
                m_old = stat_ref[half, 0:1, cols]
                m_new = jnp.maximum(m_old, jnp.max(s, axis=0, keepdims=True) * SCALE2)
                alpha = jnp.exp2(m_old - m_new)
                p = jnp.exp2(s * SCALE2 - m_new)
                stat_ref[half, 0:1, cols] = m_new
                stat_ref[half, 1:2, cols] = stat_ref[half, 1:2, cols] * alpha + jnp.sum(p, axis=0, keepdims=True)
                acc[:, cols] = acc[:, cols] * alpha
                p_ref[:, flat] = p.astype(BF)
            acc[...] += dot(vt, p_ref[:, pl.ds(half * COLS, COLS)], NN)

    if first:
        pl.when(i == 0)(lambda: step(True))
        pl.when((i > 0) & (info[base + i] > 0))(lambda: step(False))
    else:
        pl.when(info[base + i] > 0)(lambda: step(False))

    if last:

        @pl.when(i == QUAD * n - 1)
        def _():
            eye = (
                lax.broadcasted_iota(jnp.int32, (HEAD_DIM, HEAD_DIM), 0)
                == lax.broadcasted_iota(jnp.int32, (HEAD_DIM, HEAD_DIM), 1)
            ).astype(F32).astype(BF)
            for half in range(2):
                turned = dot(eye, g_refs[half][...], NT)
                stat_ref[half, 2:3, :] = jnp.sum(turned * acc_refs[half][...], axis=0, keepdims=True)


def combine(mine, other, half):
    m0 = mine[half, 0:1, :]
    m1 = other[1 - half, 0:1, :]
    m = jnp.maximum(m0, m1)
    e0 = jnp.exp2(m0 - m)
    e1 = jnp.exp2(m1 - m)
    total = mine[half, 1:2, :] * e0 + other[1 - half, 1:2, :] * e1
    return m + jnp.log2(total), e0 / total, e1 / total


def backward_kernel(base, n, first, masks, info, *refs):
    kv_refs, refs = refs[:n], refs[n:]
    q_refs, g_refs, refs = query_refs(refs[:2]), grad_refs(refs[:2]), refs[2:]
    mine, other, refs = refs[0], refs[1], refs[2:]
    if not first:
        dq_in, refs = refs[:2], refs[2:]
    dq_refs, out_refs, refs = refs[:2], refs[2 : 2 + n], refs[2 + n :]
    row_ref, s_ref, dp_ref, p_ref, ds_ref, kv_buf, out_buf = refs
    i = pl.program_id(0)
    core = info[CORE_AT]

    @pl.when(i == 0)
    def _():
        for half in range(2):
            lse, w0, w1 = combine(mine, other, half)
            row_ref[half, 0:1, :] = lse
            row_ref[half, 1:2, :] = mine[half, 2:3, :] * w0 + other[1 - half, 2:3, :] * w1
            dq_refs[half][...] = jnp.zeros(ACC, F32) if first else dq_in[half][...]

    def step(masked):
        kv = fetch(i, kv_refs, kv_buf)
        k = kv[:, :HEAD_DIM]
        v = kv[:, HEAD_DIM:]
        kt = jnp.transpose(k)
        for half in range(2):
            cols = pl.ds(half * COLS, COLS)
            s_ref[:, cols] = dot(k, q_refs[half][...], NT)
            dp_ref[:, cols] = dot(v, g_refs[half][...], NT)
        for half in range(2):
            if masked:
                keep = keep_mask(half * HALF * (1 - 2 * core))
            for h in range(GROUP):
                cols = pl.ds(h * HALF, HALF)
                flat = pl.ds(half * COLS + h * HALF, HALF)
                p = jnp.exp2(s_ref[:, flat] * SCALE2 - row_ref[half, 0:1, cols])
                if masked:
                    p = jnp.where(keep, p, 0.0)
                p_ref[:, flat] = p.astype(BF)
                ds_ref[:, flat] = (p * (dp_ref[:, flat] - row_ref[half, 1:2, cols])).astype(BF)
            dq_refs[half][...] += dot(kt, ds_ref[:, pl.ds(half * COLS, COLS)], NN)
        dk = jnp.zeros((HALF, HEAD_DIM), F32)
        dv = jnp.zeros((HALF, HEAD_DIM), F32)
        for half in range(2):
            cols = pl.ds(half * COLS, COLS)
            dk = dk + dot(ds_ref[:, cols], q_refs[half][...], NN)
            dv = dv + dot(p_ref[:, cols], g_refs[half][...], NN)
        out_buf[:, :HEAD_DIM] = dk.astype(BF)
        out_buf[:, HEAD_DIM:] = dv.astype(BF)

    live = info[base + i] > 0
    if masks:
        pl.when(i == 0)(lambda: step(True))
        pl.when((i > 0) & live)(lambda: step(False))
    else:
        pl.when(live)(lambda: step(False))

    @pl.when(jnp.logical_not(live))
    def _():
        out_buf[...] = jnp.zeros(PIECE, BF)

    for a, ref in enumerate(out_refs):

        @pl.when(i // QUAD == a)
        def _():
            ref[0] = out_buf[...]


def finish_kernel(mine, other, acc_mine, acc_other, dq_mine, dq_other, att_ref, dq_ref):
    lse, w0, w1 = combine(mine, other, 0)
    for h in range(GROUP):
        cols = slice(h * HALF, (h + 1) * HALF)
        rows = slice(h * HEAD_DIM, (h + 1) * HEAD_DIM)
        out = acc_mine[:, cols] * w0[:, cols] + acc_other[:, cols] * w1[:, cols]
        att_ref[:, rows] = jnp.transpose(out).astype(BF)
        dq_ref[:, rows] = jnp.transpose((dq_mine[:, cols] + dq_other[:, cols]) * SCALE).astype(BF)


def whole(shape):
    return pl.BlockSpec(shape, lambda i, info: (0,) * len(shape))


def piece_specs(n):
    def spec(a):
        return pl.BlockSpec((1,) + PIECE, lambda i, info: (jnp.clip(i - QUAD * a, 0, QUAD - 1), 0, 0))

    return [spec(a) for a in range(n)]


def cost(flops):
    return pl.CostEstimate(flops=flops, bytes_accessed=1 << 16, transcendentals=0)


def forward(base, info, kvs, qg, state, last):
    n = len(kvs)
    first = state is None
    ins = list(kvs) + list(qg) + ([] if first else list(state))
    specs = piece_specs(n) + [whole(PAIR)] * 2
    if not first:
        specs += [whole(STAT), whole(ACC), whole(ACC)]
    return pl.pallas_call(
        functools.partial(forward_kernel, base, n, first, last),
        grid_spec=pltpu.PrefetchScalarGridSpec(
            num_scalar_prefetch=1,
            grid=(QUAD * n,),
            in_specs=specs,
            out_specs=[whole(STAT), whole(ACC), whole(ACC)],
            scratch_shapes=[
                pltpu.VMEM((HALF, 2 * COLS), F32),
                pltpu.VMEM((HALF, 2 * COLS), BF),
                pltpu.VMEM(PIECE, BF),
            ],
        ),
        out_shape=[jax.ShapeDtypeStruct(s, F32) for s in (STAT, ACC, ACC)],
        compiler_params=pltpu.CompilerParams(vmem_limit_bytes=VMEM_LIMIT),
        cost_estimate=cost(200_000_000),
        name="forward",
    )(info, *ins)


def backward(base, info, kvs, qg, mine, other, dq):
    n = len(kvs)
    first = dq is None
    ins = list(kvs) + list(qg) + [mine, other] + ([] if first else list(dq))
    specs = piece_specs(n) + [whole(PAIR)] * 2 + [whole(STAT)] * 2
    if not first:
        specs += [whole(ACC), whole(ACC)]
    wide_shape = (HALF, 2 * COLS)
    res = pl.pallas_call(
        functools.partial(backward_kernel, base, n, first, base == 0),
        grid_spec=pltpu.PrefetchScalarGridSpec(
            num_scalar_prefetch=1,
            grid=(QUAD * n,),
            in_specs=specs,
            out_specs=[whole(ACC), whole(ACC)] + piece_specs(n),
            scratch_shapes=[
                pltpu.VMEM((2, 2, COLS), F32),
                pltpu.VMEM(wide_shape, F32),
                pltpu.VMEM(wide_shape, F32),
                pltpu.VMEM(wide_shape, BF),
                pltpu.VMEM(wide_shape, BF),
                pltpu.VMEM(PIECE, BF),
                pltpu.VMEM(PIECE, BF),
            ],
        ),
        out_shape=[jax.ShapeDtypeStruct(ACC, F32)] * 2 + [jax.ShapeDtypeStruct(a.shape, BF) for a in kvs],
        compiler_params=pltpu.CompilerParams(vmem_limit_bytes=VMEM_LIMIT),
        cost_estimate=cost(200_000_000),
        name="backward",
    )(info, *ins)
    return res[:2], res[2:]


def finish(mine, other, acc_mine, acc_other, dq_mine, dq_other):
    shape = jax.ShapeDtypeStruct((HALF, GROUP * HEAD_DIM), BF)
    return pl.pallas_call(
        finish_kernel,
        in_specs=[VMEM] * 6,
        out_specs=[VMEM] * 2,
        out_shape=[shape, shape],
        compiler_params=pltpu.CompilerParams(vmem_limit_bytes=VMEM_LIMIT),
        cost_estimate=pl.CostEstimate(flops=1 << 20, bytes_accessed=1 << 16, transcendentals=0),
        name="finish",
    )(mine, other, acc_mine, acc_other, dq_mine, dq_other)


VMEM = pl.BlockSpec(memory_space=pltpu.VMEM)
SMALL = pltpu.CompilerParams(vmem_limit_bytes=16 * 1024 * 1024)


def join_kernel(k_ref, v_ref, out_ref):
    out_ref[:, :HEAD_DIM] = k_ref[...]
    out_ref[:, HEAD_DIM:] = v_ref[...]


def join(k, v):
    return pl.pallas_call(join_kernel, out_shape=jax.ShapeDtypeStruct(PIECE, BF), in_specs=[VMEM] * 2, out_specs=VMEM, name="join")(k, v)


def prepare_kernel(query, grad_out, gate, after, qg_ref, gate_ref):
    for h in range(GROUP):
        rows = slice(h * HALF, (h + 1) * HALF)
        cols = slice(h * HEAD_DIM, (h + 1) * HEAD_DIM)
        qg_ref[0, rows, :] = query[:, cols]
        qg_ref[1, rows, :] = grad_out[:, cols]
    gate_ref[...] = gate[...]


def prepare(query, grad_out, gate, after):
    return pl.pallas_call(
        prepare_kernel,
        in_specs=[VMEM] * 3 + [pl.BlockSpec(memory_space=pl.ANY)],
        out_specs=[VMEM] * 2,
        out_shape=[jax.ShapeDtypeStruct(PAIR, BF), jax.ShapeDtypeStruct(gate.shape, jnp.int32)],
        cost_estimate=cost(100_000_000),
        name="prepare",
    )(query, grad_out, gate, after)


def stack_kernel(*refs):
    for i in range(QUAD):
        refs[-1][i] = refs[i][...]


def stack(*pieces):
    return pl.pallas_call(stack_kernel, out_shape=jax.ShapeDtypeStruct((QUAD,) + PIECE, BF), in_specs=[VMEM] * QUAD, out_specs=VMEM, name="stack")(*pieces)


def sum_high_kernel(own, one, three, keep, near_up, near_down, far):
    def total(i):
        return wide(own[i]) + wide(one[i]) + wide(three[i])

    keep[...] = total(0)
    near_down[...] = total(1).astype(BF)
    near_up[...] = total(2).astype(BF)
    far[...] = total(3).astype(BF)


def sum_high(own, one, three):
    shape = jax.ShapeDtypeStruct(PIECE, BF)
    return pl.pallas_call(
        sum_high_kernel,
        in_specs=[VMEM] * 3,
        out_specs=[VMEM] * 4,
        out_shape=[jax.ShapeDtypeStruct(PIECE, F32), shape, shape, shape],
        cost_estimate=cost(100_000_000),
        name="sum_high",
    )(own, one, three)


def sum_low_kernel(own, one, three, keep, down, far, up, own_out, near_down, near_up, two_down, two_up):
    def total(i):
        return wide(own[i]) + wide(one[i]) + wide(three[i])

    own_out[...] = total(0)
    near_down[...] = total(1).astype(BF)
    near_up[...] = total(2).astype(BF)
    two_down[...] = (total(3) + wide(down[...]) + wide(far[...])).astype(BF)
    two_up[...] = (keep[...] + wide(up[...])).astype(BF)


def sum_low(own, one, three, keep, down, far, up):
    shape = jax.ShapeDtypeStruct(PIECE, BF)
    return pl.pallas_call(
        sum_low_kernel,
        in_specs=[VMEM] * 7,
        out_specs=[VMEM] * 5,
        out_shape=[jax.ShapeDtypeStruct(PIECE, F32), shape, shape, shape, shape],
        cost_estimate=cost(100_000_000),
        name="sum_low",
    )(own, one, three, keep, down, far, up)


def close_kernel(own, a, b, c, d, dk_ref, dv_ref):
    total = own[...] + wide(a[...]) + wide(b[...]) + wide(c[...]) + wide(d[...])
    dk_ref[...] = (total[:, :HEAD_DIM] * SCALE).astype(BF)
    dv_ref[...] = total[:, HEAD_DIM:].astype(BF)


def close(own, parts):
    shape = jax.ShapeDtypeStruct((HALF, HEAD_DIM), BF)
    return pl.pallas_call(
        close_kernel, out_shape=[shape, shape], in_specs=[VMEM] * 5, out_specs=[VMEM] * 2, name="close"
    )(own, *parts)


def plan(gate):
    z = lax.axis_index("z")
    x = lax.axis_index("x")
    own = z * 4 + x
    totals = gate + lax.ppermute(gate, "head", [(0, 1), (1, 0), (2, 3), (3, 2)])
    totals = totals + lax.ppermute(totals, "head", [(0, 2), (2, 0), (1, 3), (3, 1)])
    row = lax.dynamic_slice_in_dim(totals.reshape(NBLK, NBLK), own, 1, 0)[0]
    columns = jnp.arange(NBLK, dtype=jnp.int32)
    ranked = jnp.where(columns < own, row * NBLK + columns, -1)
    rank = jnp.sum((ranked[None, :] > ranked[:, None]).astype(jnp.int32), axis=1)
    used = ((rank < TOPK) & (ranked >= 0)) | (columns == own)
    core = lax.axis_index("core")
    way = 1 - 2 * core
    dz = (way * (z - columns // 4)) % 8
    dx = (way * (x - columns % 4)) % 4
    pos = jnp.where(dz == 0, 0, jnp.where(dz <= 4, 2 * dz - 1, 2 * (8 - dz)))
    place = dx * 8 + pos
    live = jnp.sum((place[None, :] == columns[:, None]) & used[None, :], axis=1, dtype=jnp.int32)
    return jnp.concatenate([live, core[None]])


def on_device(query, key, value, grad_out, gate_score):
    piece = join(key, value)
    a1, b1 = shift(piece, "z", 1), shift(piece, "z", -1)
    a2, b2 = shift(piece, "z", 2), shift(piece, "z", -2)
    a3, b3, a4 = shift(a2, "z", 1), shift(b2, "z", -1), shift(a2, "z", 2)
    low0 = stack(piece, a1, b1, a2)
    high0 = stack(b2, a3, b3, a4)
    low1, high1 = shift(low0, "x", 1), shift(high0, "x", 1)
    low2, high2 = shift(low1, "x", 1), shift(high1, "x", 1)
    low3, high3 = shift(low0, "x", -1), shift(high0, "x", -1)

    qg, gate = prepare(query, grad_out, gate_score.reshape(8, 128), a3)
    info = plan(gate)
    qg = (qg, swap(qg))

    state = forward(0, info, [low0, high0], qg, None, False)
    state = forward(8, info, [low1, high1], qg, state, False)
    state = forward(24, info, [low3, high3], qg, state, False)
    mine, acc, acc_away = forward(16, info, [low2, high2], qg, state, True)
    other = swap(mine)
    acc_other = swap(acc_away)

    dq, (low2, high2) = backward(16, info, [low2, high2], qg, mine, other, None)
    high2, low2 = shift(high2, "x", -1), shift(low2, "x", -1)
    dq, (low3, high3) = backward(24, info, [low3, high3], qg, mine, other, dq)
    high3, low3 = shift(high3, "x", 1), shift(low3, "x", 1)
    dq, (low1, high1) = backward(8, info, [low1, high1], qg, mine, other, dq)
    high1 = shift((wide(high1) + wide(high2)).astype(BF), "x", -1)
    low1 = shift((wide(low1) + wide(low2)).astype(BF), "x", -1)
    dq, (low0, high0) = backward(0, info, [low0, high0], qg, mine, other, dq)

    keep, up, down, far = sum_high(high0, high1, high3)
    down, far, up = shift(down, "z", -1), shift(far, "z", -2), shift(up, "z", 1)
    own, near_down, near_up, two_down, two_up = sum_low(low0, low1, low3, keep, down, far, up)
    parts = [
        shift(two_up, "z", 2),
        shift(two_down, "z", -2),
        shift(near_down, "z", -1),
        shift(near_up, "z", 1),
    ]
    grad_key, grad_value = close(own, parts)
    attended, grad_query = finish(mine, other, acc, acc_other, dq[0], swap(dq[1]))
    return (attended, grad_query, grad_key, grad_value)


def solution(mesh):
    devices = mesh.devices.reshape(8, 4, 2, 4)
    split = Mesh(devices, ("z", "x", "core", "head"))
    spec = P(("z", "x", "core"), "head")
    return jax.shard_map(
        on_device,
        mesh=split,
        in_specs=(spec, spec, spec, spec, P("head", None, None)),
        out_specs=(spec, spec, spec, spec),
        check_vma=False,
    )
```

```python
import functools
import math

import jax
import jax.numpy as jnp
from jax import lax
from jax.experimental import pallas as pl
from jax.experimental.pallas import tpu as pltpu
from jax.sharding import Mesh
from jax.sharding import PartitionSpec as P

HEAD_DIM = 128
GROUP = 4
TOPK = 8
NBLK = 32
HALF = 256
COLS = GROUP * HALF
SCALE = 1.0 / math.sqrt(HEAD_DIM)
SCALE2 = SCALE / math.log(2.0)
NEG = -1e30
MASKED = -3e38
BF = jnp.bfloat16
F32 = jnp.float32
SIZES = {"z": 8, "x": 4}
NT = (((1,), (1,)), ((), ()))
NN = (((1,), (0,)), ((), ()))
CORE_AT = 32
QUAD = 4
VMEM_LIMIT = 24 * 1024 * 1024
STAT = (2, 3, COLS)
ACC = (HEAD_DIM, COLS)
PAIR = (2, COLS, HEAD_DIM)
PIECE = (HALF, 2 * HEAD_DIM)


def dot(a, b, dims):
    return lax.dot_general(a, b, dims, preferred_element_type=F32)


def wide(a):
    return a.astype(F32)


def shift(a, axis, d):
    n = SIZES[axis]
    return lax.ppermute(a, (axis, "core"), [(2 * i + c, 2 * ((i + d * (1 - 2 * c)) % n) + c) for i in range(n) for c in range(2)])


def swap(a):
    return lax.ppermute(a, "core", [(0, 1), (1, 0)])


def keep_mask(off):
    i = lax.broadcasted_iota(jnp.int32, (HALF, HALF), 0)
    j = lax.broadcasted_iota(jnp.int32, (HALF, HALF), 1)
    return (i - j) <= off


def fetch(i, kv_refs, kv_buf):
    for a, ref in enumerate(kv_refs):

        @pl.when(i // QUAD == a)
        def _():
            kv_buf[...] = ref[0]

    return kv_buf[...]


def query_refs(refs):
    return [ref.at[0] for ref in refs]


def grad_refs(refs):
    return [ref.at[1] for ref in refs]


def forward_kernel(base, n, first, last, info, *refs):
    kv_refs, refs = refs[:n], refs[n:]
    q_refs, g_refs, refs = query_refs(refs[:2]), grad_refs(refs[:2]), refs[2:]
    if not first:
        stat_in, acc_in, refs = refs[0], refs[1:3], refs[3:]
    stat_ref, acc_refs, (s_ref, p_ref, kv_buf) = refs[0], refs[1:3], refs[3:]
    i = pl.program_id(0)
    core = info[CORE_AT]

    @pl.when(i == 0)
    def _():
        if first:
            stat_ref[:, 0:1, :] = jnp.full((2, 1, COLS), NEG, F32)
            stat_ref[:, 1:3, :] = jnp.zeros((2, 2, COLS), F32)
            for half in range(2):
                acc_refs[half][...] = jnp.zeros(ACC, F32)
        else:
            stat_ref[...] = stat_in[...]
            for half in range(2):
                acc_refs[half][...] = acc_in[half][...]

    def step(masked):
        kv = fetch(i, kv_refs, kv_buf)
        k = kv[:, :HEAD_DIM]
        vt = jnp.transpose(kv[:, HEAD_DIM:])
        for half in range(2):
            s_ref[:, pl.ds(half * COLS, COLS)] = dot(k, q_refs[half][...], NT)
        for half in range(2):
            acc = acc_refs[half]
            if masked:
                keep = keep_mask(jnp.where(i == 0, half * HALF * (1 - 2 * core), HALF))
            for h in range(GROUP):
                cols = pl.ds(h * HALF, HALF)
                flat = pl.ds(half * COLS + h * HALF, HALF)
                s = s_ref[:, flat]
                if masked:
                    s = jnp.where(keep, s, MASKED)
                m_old = stat_ref[half, 0:1, cols]
                m_new = jnp.maximum(m_old, jnp.max(s, axis=0, keepdims=True) * SCALE2)
                alpha = jnp.exp2(m_old - m_new)
                p = jnp.exp2(s * SCALE2 - m_new)
                stat_ref[half, 0:1, cols] = m_new
                stat_ref[half, 1:2, cols] = stat_ref[half, 1:2, cols] * alpha + jnp.sum(p, axis=0, keepdims=True)
                acc[:, cols] = acc[:, cols] * alpha
                p_ref[:, flat] = p.astype(BF)
            acc[...] += dot(vt, p_ref[:, pl.ds(half * COLS, COLS)], NN)

    pl.when(info[base + i] > 0)(lambda: step(first))

    if last:

        @pl.when(i == QUAD * n - 1)
        def _():
            eye = (
                lax.broadcasted_iota(jnp.int32, (HEAD_DIM, HEAD_DIM), 0)
                == lax.broadcasted_iota(jnp.int32, (HEAD_DIM, HEAD_DIM), 1)
            ).astype(F32).astype(BF)
            for half in range(2):
                turned = dot(eye, g_refs[half][...], NT)
                stat_ref[half, 2:3, :] = jnp.sum(turned * acc_refs[half][...], axis=0, keepdims=True)


def combine(mine, other, half):
    m0 = mine[half, 0:1, :]
    m1 = other[1 - half, 0:1, :]
    m = jnp.maximum(m0, m1)
    e0 = jnp.exp2(m0 - m)
    e1 = jnp.exp2(m1 - m)
    total = mine[half, 1:2, :] * e0 + other[1 - half, 1:2, :] * e1
    return m + jnp.log2(total), e0 / total, e1 / total


def backward_kernel(base, n, first, masks, info, *refs):
    kv_refs, refs = refs[:n], refs[n:]
    q_refs, g_refs, refs = query_refs(refs[:2]), grad_refs(refs[:2]), refs[2:]
    mine, other, refs = refs[0], refs[1], refs[2:]
    if not first:
        dq_in, refs = refs[:2], refs[2:]
    dq_refs, out_refs, refs = refs[:2], refs[2 : 2 + n], refs[2 + n :]
    row_ref, s_ref, dp_ref, p_ref, ds_ref, kv_buf, out_buf = refs
    i = pl.program_id(0)
    core = info[CORE_AT]

    @pl.when(i == 0)
    def _():
        for half in range(2):
            lse, w0, w1 = combine(mine, other, half)
            row_ref[half, 0:1, :] = lse
            row_ref[half, 1:2, :] = mine[half, 2:3, :] * w0 + other[1 - half, 2:3, :] * w1
            dq_refs[half][...] = jnp.zeros(ACC, F32) if first else dq_in[half][...]

    def step(masked):
        kv = fetch(i, kv_refs, kv_buf)
        k = kv[:, :HEAD_DIM]
        v = kv[:, HEAD_DIM:]
        kt = jnp.transpose(k)
        for half in range(2):
            cols = pl.ds(half * COLS, COLS)
            s_ref[:, cols] = dot(k, q_refs[half][...], NT)
            dp_ref[:, cols] = dot(v, g_refs[half][...], NT)
        for half in range(2):
            if masked:
                keep = keep_mask(jnp.where(i == 0, half * HALF * (1 - 2 * core), HALF))
            for h in range(GROUP):
                cols = pl.ds(h * HALF, HALF)
                flat = pl.ds(half * COLS + h * HALF, HALF)
                p = jnp.exp2(s_ref[:, flat] * SCALE2 - row_ref[half, 0:1, cols])
                if masked:
                    p = jnp.where(keep, p, 0.0)
                p_ref[:, flat] = p.astype(BF)
                ds_ref[:, flat] = (p * (dp_ref[:, flat] - row_ref[half, 1:2, cols])).astype(BF)
            dq_refs[half][...] += dot(kt, ds_ref[:, pl.ds(half * COLS, COLS)], NN)
        dk = jnp.zeros((HALF, HEAD_DIM), F32)
        dv = jnp.zeros((HALF, HEAD_DIM), F32)
        for half in range(2):
            cols = pl.ds(half * COLS, COLS)
            dk = dk + dot(ds_ref[:, cols], q_refs[half][...], NN)
            dv = dv + dot(p_ref[:, cols], g_refs[half][...], NN)
        out_buf[:, :HEAD_DIM] = dk.astype(BF)
        out_buf[:, HEAD_DIM:] = dv.astype(BF)

    live = info[base + i] > 0
    pl.when(live)(lambda: step(masks))

    @pl.when(jnp.logical_not(live))
    def _():
        out_buf[...] = jnp.zeros(PIECE, BF)

    for a, ref in enumerate(out_refs):

        @pl.when(i // QUAD == a)
        def _():
            ref[0] = out_buf[...]


def finish_kernel(mine, other, acc_mine, acc_other, dq_mine, dq_other, att_ref, dq_ref):
    lse, w0, w1 = combine(mine, other, 0)
    for h in range(GROUP):
        cols = slice(h * HALF, (h + 1) * HALF)
        rows = slice(h * HEAD_DIM, (h + 1) * HEAD_DIM)
        out = acc_mine[:, cols] * w0[:, cols] + acc_other[:, cols] * w1[:, cols]
        att_ref[:, rows] = jnp.transpose(out).astype(BF)
        dq_ref[:, rows] = jnp.transpose((dq_mine[:, cols] + dq_other[:, cols]) * SCALE).astype(BF)


def whole(shape):
    return pl.BlockSpec(shape, lambda i, info: (0,) * len(shape))


def piece_specs(n):
    def spec(a):
        return pl.BlockSpec((1,) + PIECE, lambda i, info: (jnp.clip(i - QUAD * a, 0, QUAD - 1), 0, 0))

    return [spec(a) for a in range(n)]


def cost(flops):
    return pl.CostEstimate(flops=flops, bytes_accessed=1 << 16, transcendentals=0)


def forward(base, info, kvs, qg, state, last):
    n = len(kvs)
    first = state is None
    ins = list(kvs) + list(qg) + ([] if first else list(state))
    specs = piece_specs(n) + [whole(PAIR)] * 2
    if not first:
        specs += [whole(STAT), whole(ACC), whole(ACC)]
    return pl.pallas_call(
        functools.partial(forward_kernel, base, n, first, last),
        grid_spec=pltpu.PrefetchScalarGridSpec(
            num_scalar_prefetch=1,
            grid=(QUAD * n,),
            in_specs=specs,
            out_specs=[whole(STAT), whole(ACC), whole(ACC)],
            scratch_shapes=[
                pltpu.VMEM((HALF, 2 * COLS), F32),
                pltpu.VMEM((HALF, 2 * COLS), BF),
                pltpu.VMEM(PIECE, BF),
            ],
        ),
        out_shape=[jax.ShapeDtypeStruct(s, F32) for s in (STAT, ACC, ACC)],
        compiler_params=pltpu.CompilerParams(vmem_limit_bytes=VMEM_LIMIT),
        cost_estimate=cost(200_000_000),
        name="forward",
    )(info, *ins)


def backward(base, info, kvs, qg, mine, other, dq):
    n = len(kvs)
    first = dq is None
    ins = list(kvs) + list(qg) + [mine, other] + ([] if first else list(dq))
    specs = piece_specs(n) + [whole(PAIR)] * 2 + [whole(STAT)] * 2
    if not first:
        specs += [whole(ACC), whole(ACC)]
    wide_shape = (HALF, 2 * COLS)
    res = pl.pallas_call(
        functools.partial(backward_kernel, base, n, first, base == 0),
        grid_spec=pltpu.PrefetchScalarGridSpec(
            num_scalar_prefetch=1,
            grid=(QUAD * n,),
            in_specs=specs,
            out_specs=[whole(ACC), whole(ACC)] + piece_specs(n),
            scratch_shapes=[
                pltpu.VMEM((2, 2, COLS), F32),
                pltpu.VMEM(wide_shape, F32),
                pltpu.VMEM(wide_shape, F32),
                pltpu.VMEM(wide_shape, BF),
                pltpu.VMEM(wide_shape, BF),
                pltpu.VMEM(PIECE, BF),
                pltpu.VMEM(PIECE, BF),
            ],
        ),
        out_shape=[jax.ShapeDtypeStruct(ACC, F32)] * 2 + [jax.ShapeDtypeStruct(a.shape, BF) for a in kvs],
        compiler_params=pltpu.CompilerParams(vmem_limit_bytes=VMEM_LIMIT),
        cost_estimate=cost(200_000_000),
        name="backward",
    )(info, *ins)
    return res[:2], res[2:]


def finish(mine, other, acc_mine, acc_other, dq_mine, dq_other):
    shape = jax.ShapeDtypeStruct((HALF, GROUP * HEAD_DIM), BF)
    return pl.pallas_call(
        finish_kernel,
        in_specs=[VMEM] * 6,
        out_specs=[VMEM] * 2,
        out_shape=[shape, shape],
        compiler_params=SMALL,
        cost_estimate=pl.CostEstimate(flops=1 << 20, bytes_accessed=1 << 16, transcendentals=0),
        name="finish",
    )(mine, other, acc_mine, acc_other, dq_mine, dq_other)


VMEM = pl.BlockSpec(memory_space=pltpu.VMEM)
SMALL = pltpu.CompilerParams(vmem_limit_bytes=8 * 1024 * 1024)


def join_kernel(k_ref, v_ref, out_ref):
    out_ref[:, :HEAD_DIM] = k_ref[...]
    out_ref[:, HEAD_DIM:] = v_ref[...]


def join(k, v):
    return pl.pallas_call(join_kernel, out_shape=jax.ShapeDtypeStruct(PIECE, BF), in_specs=[VMEM] * 2, out_specs=VMEM, compiler_params=SMALL, name="join")(k, v)


def prepare_kernel(query, grad_out, gate, after, qg_ref, gate_ref):
    for h in range(GROUP):
        rows = slice(h * HALF, (h + 1) * HALF)
        cols = slice(h * HEAD_DIM, (h + 1) * HEAD_DIM)
        qg_ref[0, rows, :] = query[:, cols]
        qg_ref[1, rows, :] = grad_out[:, cols]
    gate_ref[...] = gate[...]


def prepare(query, grad_out, gate, after):
    return pl.pallas_call(
        prepare_kernel,
        in_specs=[VMEM] * 3 + [pl.BlockSpec(memory_space=pl.ANY)],
        out_specs=[VMEM] * 2,
        out_shape=[jax.ShapeDtypeStruct(PAIR, BF), jax.ShapeDtypeStruct(gate.shape, jnp.int32)],
        cost_estimate=cost(100_000_000),
        compiler_params=SMALL, name="prepare",
    )(query, grad_out, gate, after)


def stack_kernel(*refs):
    for i in range(QUAD):
        refs[-1][i] = refs[i][...]


def stack(*pieces):
    return pl.pallas_call(stack_kernel, out_shape=jax.ShapeDtypeStruct((QUAD,) + PIECE, BF), in_specs=[VMEM] * QUAD, out_specs=VMEM, compiler_params=SMALL, name="stack")(*pieces)


def sum_high_kernel(own, one, three, keep, near_up, near_down, far):
    def total(i):
        return wide(own[i]) + wide(one[i]) + wide(three[i])

    keep[...] = total(0)
    near_down[...] = total(1).astype(BF)
    near_up[...] = total(2).astype(BF)
    far[...] = total(3).astype(BF)


def sum_high(own, one, three):
    shape = jax.ShapeDtypeStruct(PIECE, BF)
    return pl.pallas_call(
        sum_high_kernel,
        in_specs=[VMEM] * 3,
        out_specs=[VMEM] * 4,
        out_shape=[jax.ShapeDtypeStruct(PIECE, F32), shape, shape, shape],
        cost_estimate=cost(100_000_000),
        compiler_params=SMALL, name="sum_high",
    )(own, one, three)


def sum_low_kernel(own, one, three, keep, down, far, up, own_out, near_down, near_up, two_down, two_up):
    def total(i):
        return wide(own[i]) + wide(one[i]) + wide(three[i])

    own_out[...] = total(0)
    near_down[...] = total(1).astype(BF)
    near_up[...] = total(2).astype(BF)
    two_down[...] = (total(3) + wide(down[...]) + wide(far[...])).astype(BF)
    two_up[...] = (keep[...] + wide(up[...])).astype(BF)


def sum_low(own, one, three, keep, down, far, up):
    shape = jax.ShapeDtypeStruct(PIECE, BF)
    return pl.pallas_call(
        sum_low_kernel,
        in_specs=[VMEM] * 7,
        out_specs=[VMEM] * 5,
        out_shape=[jax.ShapeDtypeStruct(PIECE, F32), shape, shape, shape, shape],
        cost_estimate=cost(100_000_000),
        compiler_params=SMALL, name="sum_low",
    )(own, one, three, keep, down, far, up)


def close_kernel(own, a, b, c, d, dk_ref, dv_ref):
    total = own[...] + wide(a[...]) + wide(b[...]) + wide(c[...]) + wide(d[...])
    dk_ref[...] = (total[:, :HEAD_DIM] * SCALE).astype(BF)
    dv_ref[...] = total[:, HEAD_DIM:].astype(BF)


def close(own, parts):
    shape = jax.ShapeDtypeStruct((HALF, HEAD_DIM), BF)
    return pl.pallas_call(
        close_kernel, out_shape=[shape, shape], in_specs=[VMEM] * 5, out_specs=[VMEM] * 2, compiler_params=SMALL, name="close"
    )(own, *parts)


def plan(gate):
    z = lax.axis_index("z")
    x = lax.axis_index("x")
    own = z * 4 + x
    totals = gate + lax.ppermute(gate, "head", [(0, 1), (1, 0), (2, 3), (3, 2)])
    totals = totals + lax.ppermute(totals, "head", [(0, 2), (2, 0), (1, 3), (3, 1)])
    row = lax.dynamic_slice_in_dim(totals, own, 1, 0)[0]
    columns = jnp.arange(NBLK, dtype=jnp.int32)
    ranked = jnp.where(columns < own, row * NBLK + columns, -1)
    rank = jnp.sum((ranked[None, :] > ranked[:, None]).astype(jnp.int32), axis=1)
    used = ((rank < TOPK) & (ranked >= 0)) | (columns == own)
    core = lax.axis_index("core")
    way = 1 - 2 * core
    dz = (way * (z - columns // 4)) % 8
    dx = (way * (x - columns % 4)) % 4
    pos = jnp.where(dz == 0, 0, jnp.where(dz <= 4, 2 * dz - 1, 2 * (8 - dz)))
    place = dx * 8 + pos
    live = jnp.sum((place[None, :] == columns[:, None]) & used[None, :], axis=1, dtype=jnp.int32)
    return jnp.concatenate([live, core[None]])


def on_device(query, key, value, grad_out, gate_score):
    piece = join(key, value)
    a1, b1 = shift(piece, "z", 1), shift(piece, "z", -1)
    a2, b2 = shift(piece, "z", 2), shift(piece, "z", -2)
    a3, b3, a4 = shift(a2, "z", 1), shift(b2, "z", -1), shift(a2, "z", 2)
    low0 = stack(piece, a1, b1, a2)
    high0 = stack(b2, a3, b3, a4)
    low1, high1 = shift(low0, "x", 1), shift(high0, "x", 1)
    low2, high2 = shift(low1, "x", 1), shift(high1, "x", 1)
    low3, high3 = shift(low0, "x", -1), shift(high0, "x", -1)

    qg, gate = prepare(query, grad_out, gate_score[0], a3)
    info = plan(gate)
    qg = (qg, swap(qg))

    state = forward(0, info, [low0, high0], qg, None, False)
    state = forward(8, info, [low1, high1], qg, state, False)
    state = forward(24, info, [low3, high3], qg, state, False)
    mine, acc, acc_away = forward(16, info, [low2, high2], qg, state, True)
    other = swap(mine)
    acc_other = swap(acc_away)

    dq, (low2, high2) = backward(16, info, [low2, high2], qg, mine, other, None)
    high2, low2 = shift(high2, "x", -1), shift(low2, "x", -1)
    dq, (low3, high3) = backward(24, info, [low3, high3], qg, mine, other, dq)
    high3, low3 = shift(high3, "x", 1), shift(low3, "x", 1)
    dq, (low1, high1) = backward(8, info, [low1, high1], qg, mine, other, dq)
    high1 = shift((wide(high1) + wide(high2)).astype(BF), "x", -1)
    low1 = shift((wide(low1) + wide(low2)).astype(BF), "x", -1)
    dq, (low0, high0) = backward(0, info, [low0, high0], qg, mine, other, dq)

    keep, up, down, far = sum_high(high0, high1, high3)
    down, far, up = shift(down, "z", -1), shift(far, "z", -2), shift(up, "z", 1)
    own, near_down, near_up, two_down, two_up = sum_low(low0, low1, low3, keep, down, far, up)
    parts = [
        shift(two_up, "z", 2),
        shift(two_down, "z", -2),
        shift(near_down, "z", -1),
        shift(near_up, "z", 1),
    ]
    grad_key, grad_value = close(own, parts)
    attended, grad_query = finish(mine, other, acc, acc_other, dq[0], swap(dq[1]))
    return (attended, grad_query, grad_key, grad_value)


def solution(mesh):
    devices = mesh.devices.reshape(8, 4, 2, 4)
    split = Mesh(devices, ("z", "x", "core", "head"))
    spec = P(("z", "x", "core"), "head")
    return jax.shard_map(
        on_device,
        mesh=split,
        in_specs=(spec, spec, spec, spec, P("head", None, None)),
        out_specs=(spec, spec, spec, spec),
        check_vma=False,
    )
```

```python
import functools
import math

import jax
import jax.numpy as jnp
from jax import lax
from jax.experimental import pallas as pl
from jax.experimental.pallas import tpu as pltpu
from jax.sharding import Mesh
from jax.sharding import PartitionSpec as P

HEAD_DIM = 128
GROUP = 4
TOPK = 8
NBLK = 32
HALF = 256
COLS = GROUP * HALF
SCALE = 1.0 / math.sqrt(HEAD_DIM)
SCALE2 = SCALE / math.log(2.0)
NEG = -1e30
MASKED = -3e38
BF = jnp.bfloat16
F32 = jnp.float32
SIZES = {"z": 8, "x": 4}
NT = (((1,), (1,)), ((), ()))
NN = (((1,), (0,)), ((), ()))
CORE_AT = 32
QUAD = 4
VMEM_LIMIT = 24 * 1024 * 1024
STAT = (2, 3, COLS)
ACC = (HEAD_DIM, COLS)
PAIR = (2, COLS, HEAD_DIM)
PIECE = (HALF, 2 * HEAD_DIM)


def dot(a, b, dims):
    return lax.dot_general(a, b, dims, preferred_element_type=F32)


def wide(a):
    return a.astype(F32)


def shift(a, axis, d):
    n = SIZES[axis]
    return lax.ppermute(a, (axis, "core"), [(2 * i + c, 2 * ((i + d * (1 - 2 * c)) % n) + c) for i in range(n) for c in range(2)])


def swap(a):
    return lax.ppermute(a, "core", [(0, 1), (1, 0)])


def keep_mask(off):
    i = lax.broadcasted_iota(jnp.int32, (HALF, HALF), 0)
    j = lax.broadcasted_iota(jnp.int32, (HALF, HALF), 1)
    return (i - j) <= off


def fetch(i, kv_refs, kv_buf):
    for a, ref in enumerate(kv_refs):

        @pl.when(i // QUAD == a)
        def _():
            kv_buf[...] = ref[0]

    return kv_buf[...]


def query_refs(refs):
    return [ref.at[0] for ref in refs]


def grad_refs(refs):
    return [ref.at[1] for ref in refs]


def forward_kernel(base, n, first, last, info, *refs):
    kv_refs, refs = refs[:n], refs[n:]
    q_refs, g_refs, refs = query_refs(refs[:2]), grad_refs(refs[:2]), refs[2:]
    if not first:
        stat_in, acc_in, refs = refs[0], refs[1:3], refs[3:]
    stat_ref, acc_refs, (s_ref, p_ref, kv_buf) = refs[0], refs[1:3], refs[3:]
    i = pl.program_id(0)
    core = info[CORE_AT]

    @pl.when(i == 0)
    def _():
        if first:
            stat_ref[:, 0:1, :] = jnp.full((2, 1, COLS), NEG, F32)
            stat_ref[:, 1:3, :] = jnp.zeros((2, 2, COLS), F32)
            for half in range(2):
                acc_refs[half][...] = jnp.zeros(ACC, F32)
        else:
            stat_ref[...] = stat_in[...]
            for half in range(2):
                acc_refs[half][...] = acc_in[half][...]

    def step(masked):
        kv = fetch(i, kv_refs, kv_buf)
        k = kv[:, :HEAD_DIM]
        vt = jnp.transpose(kv[:, HEAD_DIM:])
        for half in range(2):
            s_ref[:, pl.ds(half * COLS, COLS)] = dot(k, q_refs[half][...], NT)
        for half in range(2):
            acc = acc_refs[half]
            if masked:
                keep = keep_mask(jnp.where(i == 0, half * HALF * (1 - 2 * core), HALF))
            for h in range(GROUP):
                cols = pl.ds(h * HALF, HALF)
                flat = pl.ds(half * COLS + h * HALF, HALF)
                s = s_ref[:, flat]
                if masked:
                    s = jnp.where(keep, s, MASKED)
                m_old = stat_ref[half, 0:1, cols]
                m_new = jnp.maximum(m_old, jnp.max(s, axis=0, keepdims=True) * SCALE2)
                alpha = jnp.exp2(m_old - m_new)
                p = jnp.exp2(s * SCALE2 - m_new)
                stat_ref[half, 0:1, cols] = m_new
                stat_ref[half, 1:2, cols] = stat_ref[half, 1:2, cols] * alpha + jnp.sum(p, axis=0, keepdims=True)
                acc[:, cols] = acc[:, cols] * alpha
                p_ref[:, flat] = p.astype(BF)
            acc[...] += dot(vt, p_ref[:, pl.ds(half * COLS, COLS)], NN)

    pl.when(info[base + i] > 0)(lambda: step(first))

    if last:

        @pl.when(i == QUAD * n - 1)
        def _():
            eye = (
                lax.broadcasted_iota(jnp.int32, (HEAD_DIM, HEAD_DIM), 0)
                == lax.broadcasted_iota(jnp.int32, (HEAD_DIM, HEAD_DIM), 1)
            ).astype(F32).astype(BF)
            for half in range(2):
                turned = dot(eye, g_refs[half][...], NT)
                stat_ref[half, 2:3, :] = jnp.sum(turned * acc_refs[half][...], axis=0, keepdims=True)


def combine(mine, other, half):
    m0 = mine[half, 0:1, :]
    m1 = other[1 - half, 0:1, :]
    m = jnp.maximum(m0, m1)
    e0 = jnp.exp2(m0 - m)
    e1 = jnp.exp2(m1 - m)
    total = mine[half, 1:2, :] * e0 + other[1 - half, 1:2, :] * e1
    return m + jnp.log2(total), e0 / total, e1 / total


def backward_kernel(base, n, first, masks, info, *refs):
    kv_refs, refs = refs[:n], refs[n:]
    q_refs, g_refs, refs = query_refs(refs[:2]), grad_refs(refs[:2]), refs[2:]
    mine, other, refs = refs[0], refs[1], refs[2:]
    if not first:
        dq_in, refs = refs[:2], refs[2:]
    dq_refs, out_refs, refs = refs[:2], refs[2 : 2 + n], refs[2 + n :]
    row_ref, s_ref, dp_ref, p_ref, ds_ref, kv_buf, out_buf = refs
    i = pl.program_id(0)
    core = info[CORE_AT]

    @pl.when(i == 0)
    def _():
        for half in range(2):
            lse, w0, w1 = combine(mine, other, half)
            row_ref[half, 0:1, :] = lse
            row_ref[half, 1:2, :] = mine[half, 2:3, :] * w0 + other[1 - half, 2:3, :] * w1
            dq_refs[half][...] = jnp.zeros(ACC, F32) if first else dq_in[half][...]

    def step(masked):
        kv = fetch(i, kv_refs, kv_buf)
        k = kv[:, :HEAD_DIM]
        v = kv[:, HEAD_DIM:]
        kt = jnp.transpose(k)
        for half in range(2):
            cols = pl.ds(half * COLS, COLS)
            s_ref[:, cols] = dot(k, q_refs[half][...], NT)
            dp_ref[:, cols] = dot(v, g_refs[half][...], NT)
        for half in range(2):
            if masked:
                keep = keep_mask(jnp.where(i == 0, half * HALF * (1 - 2 * core), HALF))
            for h in range(GROUP):
                cols = pl.ds(h * HALF, HALF)
                flat = pl.ds(half * COLS + h * HALF, HALF)
                p = jnp.exp2(s_ref[:, flat] * SCALE2 - row_ref[half, 0:1, cols])
                if masked:
                    p = jnp.where(keep, p, 0.0)
                p_ref[:, flat] = p.astype(BF)
                ds_ref[:, flat] = (p * (dp_ref[:, flat] - row_ref[half, 1:2, cols])).astype(BF)
            dq_refs[half][...] += dot(kt, ds_ref[:, pl.ds(half * COLS, COLS)], NN)
        dk = jnp.zeros((HALF, HEAD_DIM), F32)
        dv = jnp.zeros((HALF, HEAD_DIM), F32)
        for half in range(2):
            cols = pl.ds(half * COLS, COLS)
            dk = dk + dot(ds_ref[:, cols], q_refs[half][...], NN)
            dv = dv + dot(p_ref[:, cols], g_refs[half][...], NN)
        out_buf[:, :HEAD_DIM] = dk.astype(BF)
        out_buf[:, HEAD_DIM:] = dv.astype(BF)

    live = info[base + i] > 0
    pl.when(live)(lambda: step(masks))

    @pl.when(jnp.logical_not(live))
    def _():
        out_buf[...] = jnp.zeros(PIECE, BF)

    for a, ref in enumerate(out_refs):

        @pl.when(i // QUAD == a)
        def _():
            ref[0] = out_buf[...]


def finish_kernel(mine, other, acc_mine, acc_other, dq_mine, dq_other, att_ref, dq_ref):
    lse, w0, w1 = combine(mine, other, 0)
    for h in range(GROUP):
        cols = slice(h * HALF, (h + 1) * HALF)
        rows = slice(h * HEAD_DIM, (h + 1) * HEAD_DIM)
        out = acc_mine[:, cols] * w0[:, cols] + acc_other[:, cols] * w1[:, cols]
        att_ref[:, rows] = jnp.transpose(out).astype(BF)
        dq_ref[:, rows] = jnp.transpose((dq_mine[:, cols] + dq_other[:, cols]) * SCALE).astype(BF)


def whole(shape):
    return pl.BlockSpec(shape, lambda i, info: (0,) * len(shape))


def piece_specs(n):
    def spec(a):
        return pl.BlockSpec((1,) + PIECE, lambda i, info: (jnp.clip(i - QUAD * a, 0, QUAD - 1), 0, 0))

    return [spec(a) for a in range(n)]


def cost(flops):
    return pl.CostEstimate(flops=flops, bytes_accessed=1 << 16, transcendentals=0)


def forward(base, info, kvs, qg, state, last):
    n = len(kvs)
    first = state is None
    ins = list(kvs) + list(qg) + ([] if first else list(state))
    specs = piece_specs(n) + [whole(PAIR)] * 2
    if not first:
        specs += [whole(STAT), whole(ACC), whole(ACC)]
    return pl.pallas_call(
        functools.partial(forward_kernel, base, n, first, last),
        grid_spec=pltpu.PrefetchScalarGridSpec(
            num_scalar_prefetch=1,
            grid=(QUAD * n,),
            in_specs=specs,
            out_specs=[whole(STAT), whole(ACC), whole(ACC)],
            scratch_shapes=[
                pltpu.VMEM((HALF, 2 * COLS), F32),
                pltpu.VMEM((HALF, 2 * COLS), BF),
                pltpu.VMEM(PIECE, BF),
            ],
        ),
        out_shape=[jax.ShapeDtypeStruct(s, F32) for s in (STAT, ACC, ACC)],
        compiler_params=pltpu.CompilerParams(vmem_limit_bytes=VMEM_LIMIT),
        cost_estimate=cost(200_000_000),
        name="forward",
    )(info, *ins)


def backward(base, info, kvs, qg, mine, other, dq):
    n = len(kvs)
    first = dq is None
    ins = list(kvs) + list(qg) + [mine, other] + ([] if first else list(dq))
    specs = piece_specs(n) + [whole(PAIR)] * 2 + [whole(STAT)] * 2
    if not first:
        specs += [whole(ACC), whole(ACC)]
    wide_shape = (HALF, 2 * COLS)
    res = pl.pallas_call(
        functools.partial(backward_kernel, base, n, first, base == 0),
        grid_spec=pltpu.PrefetchScalarGridSpec(
            num_scalar_prefetch=1,
            grid=(QUAD * n,),
            in_specs=specs,
            out_specs=[whole(ACC), whole(ACC)] + piece_specs(n),
            scratch_shapes=[
                pltpu.VMEM((2, 2, COLS), F32),
                pltpu.VMEM(wide_shape, F32),
                pltpu.VMEM(wide_shape, F32),
                pltpu.VMEM(wide_shape, BF),
                pltpu.VMEM(wide_shape, BF),
                pltpu.VMEM(PIECE, BF),
                pltpu.VMEM(PIECE, BF),
            ],
        ),
        out_shape=[jax.ShapeDtypeStruct(ACC, F32)] * 2 + [jax.ShapeDtypeStruct(a.shape, BF) for a in kvs],
        compiler_params=pltpu.CompilerParams(vmem_limit_bytes=VMEM_LIMIT),
        cost_estimate=cost(200_000_000),
        name="backward",
    )(info, *ins)
    return res[:2], res[2:]


def finish(mine, other, acc_mine, acc_other, dq_mine, dq_other):
    shape = jax.ShapeDtypeStruct((HALF, GROUP * HEAD_DIM), BF)
    return pl.pallas_call(
        finish_kernel,
        in_specs=[VMEM] * 6,
        out_specs=[VMEM] * 2,
        out_shape=[shape, shape],
        compiler_params=SMALL,
        cost_estimate=pl.CostEstimate(flops=1 << 20, bytes_accessed=1 << 16, transcendentals=0),
        name="finish",
    )(mine, other, acc_mine, acc_other, dq_mine, dq_other)


VMEM = pl.BlockSpec(memory_space=pltpu.VMEM)
SMALL = pltpu.CompilerParams(vmem_limit_bytes=8 * 1024 * 1024)


def join_kernel(k_ref, v_ref, out_ref, sems):
    copies = [
        pltpu.make_async_copy(k_ref, out_ref.at[:, pl.ds(0, HEAD_DIM)], sems.at[0]),
        pltpu.make_async_copy(v_ref, out_ref.at[:, pl.ds(HEAD_DIM, HEAD_DIM)], sems.at[1]),
    ]
    for copy in copies:
        copy.start()
    for copy in copies:
        copy.wait()


def join(k, v):
    return pl.pallas_call(
        join_kernel,
        out_shape=jax.ShapeDtypeStruct(PIECE, BF),
        in_specs=[pl.BlockSpec(memory_space=pl.ANY)] * 2,
        out_specs=VMEM,
        scratch_shapes=[pltpu.SemaphoreType.DMA((2,))],
        name="join",
    )(k, v)


def prepare_kernel(query, grad_out, gate, after, qg_ref, gate_ref):
    for h in range(GROUP):
        rows = slice(h * HALF, (h + 1) * HALF)
        cols = slice(h * HEAD_DIM, (h + 1) * HEAD_DIM)
        qg_ref[0, rows, :] = query[:, cols]
        qg_ref[1, rows, :] = grad_out[:, cols]
    gate_ref[...] = gate[...]


def prepare(query, grad_out, gate, after):
    return pl.pallas_call(
        prepare_kernel,
        in_specs=[VMEM] * 3 + [pl.BlockSpec(memory_space=pl.ANY)],
        out_specs=[VMEM] * 2,
        out_shape=[jax.ShapeDtypeStruct(PAIR, BF), jax.ShapeDtypeStruct(gate.shape, jnp.int32)],
        cost_estimate=cost(100_000_000),
        compiler_params=SMALL, name="prepare",
    )(query, grad_out, gate, after)


def stack_kernel(*refs):
    for i in range(QUAD):
        refs[-1][i] = refs[i][...]


def stack(*pieces):
    return pl.pallas_call(stack_kernel, out_shape=jax.ShapeDtypeStruct((QUAD,) + PIECE, BF), in_specs=[VMEM] * QUAD, out_specs=VMEM, compiler_params=SMALL, name="stack")(*pieces)


def sum_high_kernel(own, one, three, keep, near_up, near_down, far):
    def total(i):
        return wide(own[i]) + wide(one[i]) + wide(three[i])

    keep[...] = total(0)
    near_down[...] = total(1).astype(BF)
    near_up[...] = total(2).astype(BF)
    far[...] = total(3).astype(BF)


def sum_high(own, one, three):
    shape = jax.ShapeDtypeStruct(PIECE, BF)
    return pl.pallas_call(
        sum_high_kernel,
        in_specs=[VMEM] * 3,
        out_specs=[VMEM] * 4,
        out_shape=[jax.ShapeDtypeStruct(PIECE, F32), shape, shape, shape],
        cost_estimate=cost(100_000_000),
        compiler_params=SMALL, name="sum_high",
    )(own, one, three)


def sum_low_kernel(own, one, three, own_out, near_down, near_up, keep):
    def total(i):
        return wide(own[i]) + wide(one[i]) + wide(three[i])

    own_out[...] = total(0)
    near_down[...] = total(1).astype(BF)
    near_up[...] = total(2).astype(BF)
    keep[...] = total(3)


def sum_low(own, one, three):
    kept = jax.ShapeDtypeStruct(PIECE, F32)
    shape = jax.ShapeDtypeStruct(PIECE, BF)
    return pl.pallas_call(
        sum_low_kernel,
        in_specs=[VMEM] * 3,
        out_specs=[VMEM] * 4,
        out_shape=[kept, shape, shape, kept],
        cost_estimate=cost(100_000_000),
        compiler_params=SMALL,
        name="sum_low",
    )(own, one, three)


def sum_two_kernel(high, low, down, far, up, two_down, two_up):
    two_down[...] = (low[...] + wide(down[...]) + wide(far[...])).astype(BF)
    two_up[...] = (high[...] + wide(up[...])).astype(BF)


def sum_two(high, low, down, far, up):
    shape = jax.ShapeDtypeStruct(PIECE, BF)
    return pl.pallas_call(
        sum_two_kernel,
        in_specs=[VMEM] * 5,
        out_specs=[VMEM] * 2,
        out_shape=[shape, shape],
        cost_estimate=cost(100_000_000),
        compiler_params=SMALL,
        name="sum_two",
    )(high, low, down, far, up)


def close_kernel(own, a, b, c, d, dk_ref, dv_ref):
    total = own[...] + wide(a[...]) + wide(b[...]) + wide(c[...]) + wide(d[...])
    dk_ref[...] = (total[:, :HEAD_DIM] * SCALE).astype(BF)
    dv_ref[...] = total[:, HEAD_DIM:].astype(BF)


def close(own, parts):
    shape = jax.ShapeDtypeStruct((HALF, HEAD_DIM), BF)
    return pl.pallas_call(
        close_kernel, out_shape=[shape, shape], in_specs=[VMEM] * 5, out_specs=[VMEM] * 2, compiler_params=SMALL, name="close"
    )(own, *parts)


def plan(gate):
    z = lax.axis_index("z")
    x = lax.axis_index("x")
    own = z * 4 + x
    totals = gate + lax.ppermute(gate, "head", [(0, 1), (1, 0), (2, 3), (3, 2)])
    totals = totals + lax.ppermute(totals, "head", [(0, 2), (2, 0), (1, 3), (3, 1)])
    row = lax.dynamic_slice_in_dim(totals, own, 1, 0)[0]
    columns = jnp.arange(NBLK, dtype=jnp.int32)
    ranked = jnp.where(columns < own, row * NBLK + columns, -1)
    rank = jnp.sum((ranked[None, :] > ranked[:, None]).astype(jnp.int32), axis=1)
    used = ((rank < TOPK) & (ranked >= 0)) | (columns == own)
    core = lax.axis_index("core")
    way = 1 - 2 * core
    dz = (way * (z - columns // 4)) % 8
    dx = (way * (x - columns % 4)) % 4
    pos = jnp.where(dz == 0, 0, jnp.where(dz <= 4, 2 * dz - 1, 2 * (8 - dz)))
    place = dx * 8 + pos
    live = jnp.sum((place[None, :] == columns[:, None]) & used[None, :], axis=1, dtype=jnp.int32)
    return jnp.concatenate([live, core[None]])


def on_device(query, key, value, grad_out, gate_score):
    piece = join(key, value)
    a1, b1 = shift(piece, "z", 1), shift(piece, "z", -1)
    a2, b2 = shift(piece, "z", 2), shift(piece, "z", -2)
    a3, b3, a4 = shift(a2, "z", 1), shift(b2, "z", -1), shift(a2, "z", 2)
    low0 = stack(piece, a1, b1, a2)
    high0 = stack(b2, a3, b3, a4)
    low1, high1 = shift(low0, "x", 1), shift(high0, "x", 1)
    low2, high2 = shift(low1, "x", 1), shift(high1, "x", 1)
    low3, high3 = shift(low0, "x", -1), shift(high0, "x", -1)

    qg, gate = prepare(query, grad_out, gate_score[0], a3)
    info = plan(gate)
    qg = (qg, swap(qg))

    state = forward(0, info, [low0, high0], qg, None, False)
    state = forward(8, info, [low1, high1], qg, state, False)
    state = forward(24, info, [low3, high3], qg, state, False)
    mine, acc, acc_away = forward(16, info, [low2, high2], qg, state, True)
    other = swap(mine)
    acc_other = swap(acc_away)

    dq, (low2, high2) = backward(16, info, [low2, high2], qg, mine, other, None)
    high2, low2 = shift(high2, "x", -1), shift(low2, "x", -1)
    dq, (low3, high3) = backward(24, info, [low3, high3], qg, mine, other, dq)
    high3, low3 = shift(high3, "x", 1), shift(low3, "x", 1)
    dq, (low1, high1) = backward(8, info, [low1, high1], qg, mine, other, dq)
    high1 = shift((wide(high1) + wide(high2)).astype(BF), "x", -1)
    low1 = shift((wide(low1) + wide(low2)).astype(BF), "x", -1)
    dq, (low0, high0) = backward(0, info, [low0, high0], qg, mine, other, dq)

    keep_high, up, down, far = sum_high(high0, high1, high3)
    down, far, up = shift(down, "z", -1), shift(far, "z", -2), shift(up, "z", 1)
    own, near_down, near_up, keep_low = sum_low(low0, low1, low3)
    two_down, two_up = sum_two(keep_high, keep_low, down, far, up)
    parts = [
        shift(near_down, "z", -1),
        shift(near_up, "z", 1),
        shift(two_up, "z", 2),
        shift(two_down, "z", -2),
    ]
    grad_key, grad_value = close(own, parts)
    attended, grad_query = finish(mine, other, acc, acc_other, dq[0], swap(dq[1]))
    return (attended, grad_query, grad_key, grad_value)


def solution(mesh):
    devices = mesh.devices.reshape(8, 4, 2, 4)
    split = Mesh(devices, ("z", "x", "core", "head"))
    spec = P(("z", "x", "core"), "head")
    return jax.shard_map(
        on_device,
        mesh=split,
        in_specs=(spec, spec, spec, spec, P("head", None, None)),
        out_specs=(spec, spec, spec, spec),
        check_vma=False,
    )
```

```python
import functools
import math

import jax
import jax.numpy as jnp
from jax import lax
from jax.experimental import pallas as pl
from jax.experimental.pallas import tpu as pltpu
from jax.sharding import Mesh
from jax.sharding import PartitionSpec as P

HEAD_DIM = 128
GROUP = 4
TOPK = 8
NBLK = 32
HALF = 256
COLS = GROUP * HALF
SCALE = 1.0 / math.sqrt(HEAD_DIM)
SCALE2 = SCALE / math.log(2.0)
NEG = -1e30
MASKED = -3e38
BF = jnp.bfloat16
F32 = jnp.float32
SIZES = {"z": 8, "x": 4}
NT = (((1,), (1,)), ((), ()))
NN = (((1,), (0,)), ((), ()))
CORE_AT = 32
QUAD = 4
VMEM_LIMIT = 24 * 1024 * 1024
STAT = (2, 3, COLS)
ACC = (HEAD_DIM, COLS)
PAIR = (2, COLS, HEAD_DIM)
PIECE = (HALF, 2 * HEAD_DIM)


def dot(a, b, dims):
    return lax.dot_general(a, b, dims, preferred_element_type=F32)


def wide(a):
    return a.astype(F32)


def shift(a, axis, d):
    n = SIZES[axis]
    return lax.ppermute(a, (axis, "core"), [(2 * i + c, 2 * ((i + d * (1 - 2 * c)) % n) + c) for i in range(n) for c in range(2)])


def swap(a):
    return lax.ppermute(a, "core", [(0, 1), (1, 0)])


def keep_mask(off):
    i = lax.broadcasted_iota(jnp.int32, (HALF, HALF), 0)
    j = lax.broadcasted_iota(jnp.int32, (HALF, HALF), 1)
    return (i - j) <= off


def fetch(i, kv_refs, kv_buf):
    for a, ref in enumerate(kv_refs):

        @pl.when(i // QUAD == a)
        def _():
            kv_buf[...] = ref[0]

    return kv_buf[...]


def query_refs(refs):
    return [ref.at[0] for ref in refs]


def grad_refs(refs):
    return [ref.at[1] for ref in refs]


def forward_kernel(base, n, first, last, info, *refs):
    kv_refs, refs = refs[:n], refs[n:]
    q_refs, g_refs, refs = query_refs(refs[:2]), grad_refs(refs[:2]), refs[2:]
    if not first:
        stat_in, acc_in, refs = refs[0], refs[1:3], refs[3:]
    stat_ref, acc_refs, (s_ref, p_ref, kv_buf) = refs[0], refs[1:3], refs[3:]
    i = pl.program_id(0)
    core = info[CORE_AT]

    @pl.when(i == 0)
    def _():
        if first:
            stat_ref[:, 0:1, :] = jnp.full((2, 1, COLS), NEG, F32)
            stat_ref[:, 1:3, :] = jnp.zeros((2, 2, COLS), F32)
            for half in range(2):
                acc_refs[half][...] = jnp.zeros(ACC, F32)
        else:
            stat_ref[...] = stat_in[...]
            for half in range(2):
                acc_refs[half][...] = acc_in[half][...]

    def step(masked):
        kv = fetch(i, kv_refs, kv_buf)
        k = kv[:, :HEAD_DIM]
        vt = jnp.transpose(kv[:, HEAD_DIM:])
        for half in range(2):
            s_ref[:, pl.ds(half * COLS, COLS)] = dot(k, q_refs[half][...], NT)
        for half in range(2):
            acc = acc_refs[half]
            if masked:
                keep = keep_mask(jnp.where(i == 0, half * HALF * (1 - 2 * core), HALF))
            for h in range(GROUP):
                cols = pl.ds(h * HALF, HALF)
                flat = pl.ds(half * COLS + h * HALF, HALF)
                s = s_ref[:, flat]
                if masked:
                    s = jnp.where(keep, s, MASKED)
                m_old = stat_ref[half, 0:1, cols]
                m_new = jnp.maximum(m_old, jnp.max(s, axis=0, keepdims=True) * SCALE2)
                alpha = jnp.exp2(m_old - m_new)
                p = jnp.exp2(s * SCALE2 - m_new)
                stat_ref[half, 0:1, cols] = m_new
                stat_ref[half, 1:2, cols] = stat_ref[half, 1:2, cols] * alpha + jnp.sum(p, axis=0, keepdims=True)
                acc[:, cols] = acc[:, cols] * alpha
                p_ref[:, flat] = p.astype(BF)
            acc[...] += dot(vt, p_ref[:, pl.ds(half * COLS, COLS)], NN)

    pl.when(info[base + i] > 0)(lambda: step(first))

    if last:

        @pl.when(i == QUAD * n - 1)
        def _():
            eye = (
                lax.broadcasted_iota(jnp.int32, (HEAD_DIM, HEAD_DIM), 0)
                == lax.broadcasted_iota(jnp.int32, (HEAD_DIM, HEAD_DIM), 1)
            ).astype(F32).astype(BF)
            for half in range(2):
                turned = dot(eye, g_refs[half][...], NT)
                stat_ref[half, 2:3, :] = jnp.sum(turned * acc_refs[half][...], axis=0, keepdims=True)


def combine(mine, other, half):
    m0 = mine[half, 0:1, :]
    m1 = other[1 - half, 0:1, :]
    m = jnp.maximum(m0, m1)
    e0 = jnp.exp2(m0 - m)
    e1 = jnp.exp2(m1 - m)
    total = mine[half, 1:2, :] * e0 + other[1 - half, 1:2, :] * e1
    return m + jnp.log2(total), e0 / total, e1 / total


def backward_kernel(base, n, first, masks, info, *refs):
    kv_refs, refs = refs[:n], refs[n:]
    q_refs, g_refs, refs = query_refs(refs[:2]), grad_refs(refs[:2]), refs[2:]
    mine, other, refs = refs[0], refs[1], refs[2:]
    if not first:
        dq_in, refs = refs[:2], refs[2:]
    dq_refs, out_refs, refs = refs[:2], refs[2 : 2 + n], refs[2 + n :]
    row_ref, s_ref, dp_ref, p_ref, ds_ref, kv_buf, out_buf = refs
    i = pl.program_id(0)
    core = info[CORE_AT]

    @pl.when(i == 0)
    def _():
        for half in range(2):
            lse, w0, w1 = combine(mine, other, half)
            row_ref[half, 0:1, :] = lse
            row_ref[half, 1:2, :] = mine[half, 2:3, :] * w0 + other[1 - half, 2:3, :] * w1
            dq_refs[half][...] = jnp.zeros(ACC, F32) if first else dq_in[half][...]

    def step(masked):
        kv = fetch(i, kv_refs, kv_buf)
        k = kv[:, :HEAD_DIM]
        v = kv[:, HEAD_DIM:]
        kt = jnp.transpose(k)
        for half in range(2):
            cols = pl.ds(half * COLS, COLS)
            s_ref[:, cols] = dot(k, q_refs[half][...], NT)
            dp_ref[:, cols] = dot(v, g_refs[half][...], NT)
        for half in range(2):
            if masked:
                keep = keep_mask(jnp.where(i == 0, half * HALF * (1 - 2 * core), HALF))
            for h in range(GROUP):
                cols = pl.ds(h * HALF, HALF)
                flat = pl.ds(half * COLS + h * HALF, HALF)
                p = jnp.exp2(s_ref[:, flat] * SCALE2 - row_ref[half, 0:1, cols])
                if masked:
                    p = jnp.where(keep, p, 0.0)
                p_ref[:, flat] = p.astype(BF)
                ds_ref[:, flat] = (p * (dp_ref[:, flat] - row_ref[half, 1:2, cols])).astype(BF)
            dq_refs[half][...] += dot(kt, ds_ref[:, pl.ds(half * COLS, COLS)], NN)
        dk = jnp.zeros((HALF, HEAD_DIM), F32)
        dv = jnp.zeros((HALF, HEAD_DIM), F32)
        for half in range(2):
            cols = pl.ds(half * COLS, COLS)
            dk = dk + dot(ds_ref[:, cols], q_refs[half][...], NN)
            dv = dv + dot(p_ref[:, cols], g_refs[half][...], NN)
        out_buf[:, :HEAD_DIM] = dk.astype(BF)
        out_buf[:, HEAD_DIM:] = dv.astype(BF)

    live = info[base + i] > 0
    pl.when(live)(lambda: step(masks))

    @pl.when(jnp.logical_not(live))
    def _():
        out_buf[...] = jnp.zeros(PIECE, BF)

    for a, ref in enumerate(out_refs):

        @pl.when(i // QUAD == a)
        def _():
            ref[0] = out_buf[...]


def finish_kernel(mine, other, acc_mine, acc_other, dq_mine, dq_other, att_ref, dq_ref):
    lse, w0, w1 = combine(mine, other, 0)
    for h in range(GROUP):
        cols = slice(h * HALF, (h + 1) * HALF)
        rows = slice(h * HEAD_DIM, (h + 1) * HEAD_DIM)
        out = acc_mine[:, cols] * w0[:, cols] + acc_other[:, cols] * w1[:, cols]
        att_ref[:, rows] = jnp.transpose(out).astype(BF)
        dq_ref[:, rows] = jnp.transpose((dq_mine[:, cols] + dq_other[:, cols]) * SCALE).astype(BF)


def whole(shape):
    return pl.BlockSpec(shape, lambda i, info: (0,) * len(shape))


def piece_specs(n):
    def spec(a):
        return pl.BlockSpec((1,) + PIECE, lambda i, info: (jnp.clip(i - QUAD * a, 0, QUAD - 1), 0, 0))

    return [spec(a) for a in range(n)]


def cost(flops):
    return pl.CostEstimate(flops=flops, bytes_accessed=1 << 16, transcendentals=0)


def forward(base, info, kvs, qg, state, last):
    n = len(kvs)
    first = state is None
    ins = list(kvs) + list(qg) + ([] if first else list(state))
    specs = piece_specs(n) + [whole(PAIR)] * 2
    if not first:
        specs += [whole(STAT), whole(ACC), whole(ACC)]
    return pl.pallas_call(
        functools.partial(forward_kernel, base, n, first, last),
        grid_spec=pltpu.PrefetchScalarGridSpec(
            num_scalar_prefetch=1,
            grid=(QUAD * n,),
            in_specs=specs,
            out_specs=[whole(STAT), whole(ACC), whole(ACC)],
            scratch_shapes=[
                pltpu.VMEM((HALF, 2 * COLS), F32),
                pltpu.VMEM((HALF, 2 * COLS), BF),
                pltpu.VMEM(PIECE, BF),
            ],
        ),
        out_shape=[jax.ShapeDtypeStruct(s, F32) for s in (STAT, ACC, ACC)],
        compiler_params=pltpu.CompilerParams(vmem_limit_bytes=VMEM_LIMIT),
        cost_estimate=cost(200_000_000),
        name="forward",
    )(info, *ins)


def backward(base, info, kvs, qg, mine, other, dq):
    n = len(kvs)
    first = dq is None
    ins = list(kvs) + list(qg) + [mine, other] + ([] if first else list(dq))
    specs = piece_specs(n) + [whole(PAIR)] * 2 + [whole(STAT)] * 2
    if not first:
        specs += [whole(ACC), whole(ACC)]
    wide_shape = (HALF, 2 * COLS)
    res = pl.pallas_call(
        functools.partial(backward_kernel, base, n, first, base == 0),
        grid_spec=pltpu.PrefetchScalarGridSpec(
            num_scalar_prefetch=1,
            grid=(QUAD * n,),
            in_specs=specs,
            out_specs=[whole(ACC), whole(ACC)] + piece_specs(n),
            scratch_shapes=[
                pltpu.VMEM((2, 2, COLS), F32),
                pltpu.VMEM(wide_shape, F32),
                pltpu.VMEM(wide_shape, F32),
                pltpu.VMEM(wide_shape, BF),
                pltpu.VMEM(wide_shape, BF),
                pltpu.VMEM(PIECE, BF),
                pltpu.VMEM(PIECE, BF),
            ],
        ),
        out_shape=[jax.ShapeDtypeStruct(ACC, F32)] * 2 + [jax.ShapeDtypeStruct(a.shape, BF) for a in kvs],
        compiler_params=pltpu.CompilerParams(vmem_limit_bytes=VMEM_LIMIT),
        cost_estimate=cost(200_000_000),
        name="backward",
    )(info, *ins)
    return res[:2], res[2:]


def finish(mine, other, acc_mine, acc_other, dq_mine, dq_other):
    shape = jax.ShapeDtypeStruct((HALF, GROUP * HEAD_DIM), BF)
    return pl.pallas_call(
        finish_kernel,
        in_specs=[VMEM] * 6,
        out_specs=[VMEM] * 2,
        out_shape=[shape, shape],
        compiler_params=SMALL,
        cost_estimate=pl.CostEstimate(flops=1 << 20, bytes_accessed=1 << 16, transcendentals=0),
        name="finish",
    )(mine, other, acc_mine, acc_other, dq_mine, dq_other)


VMEM = pl.BlockSpec(memory_space=pltpu.VMEM)
SMALL = pltpu.CompilerParams(vmem_limit_bytes=8 * 1024 * 1024)


def join_kernel(k_ref, v_ref, out_ref, sems):
    copies = [
        pltpu.make_async_copy(k_ref, out_ref.at[:, pl.ds(0, HEAD_DIM)], sems.at[0]),
        pltpu.make_async_copy(v_ref, out_ref.at[:, pl.ds(HEAD_DIM, HEAD_DIM)], sems.at[1]),
    ]
    for copy in copies:
        copy.start()
    for copy in copies:
        copy.wait()


def join(k, v):
    return pl.pallas_call(
        join_kernel,
        out_shape=jax.ShapeDtypeStruct(PIECE, BF),
        in_specs=[pl.BlockSpec(memory_space=pl.ANY)] * 2,
        out_specs=VMEM,
        scratch_shapes=[pltpu.SemaphoreType.DMA((2,))],
        name="join",
    )(k, v)


def prepare_kernel(query, grad_out, after, qg_ref):
    for h in range(GROUP):
        rows = slice(h * HALF, (h + 1) * HALF)
        cols = slice(h * HEAD_DIM, (h + 1) * HEAD_DIM)
        qg_ref[0, rows, :] = query[:, cols]
        qg_ref[1, rows, :] = grad_out[:, cols]


def prepare(query, grad_out, after):
    return pl.pallas_call(
        prepare_kernel,
        in_specs=[VMEM] * 2 + [pl.BlockSpec(memory_space=pl.ANY)],
        out_specs=VMEM,
        out_shape=jax.ShapeDtypeStruct(PAIR, BF),
        cost_estimate=cost(100_000_000),
        compiler_params=SMALL,
        name="prepare",
    )(query, grad_out, after)


def stack_kernel(*refs):
    for i in range(QUAD):
        refs[-1][i] = refs[i][...]


def stack(*pieces):
    return pl.pallas_call(stack_kernel, out_shape=jax.ShapeDtypeStruct((QUAD,) + PIECE, BF), in_specs=[VMEM] * QUAD, out_specs=VMEM, compiler_params=SMALL, name="stack")(*pieces)


def sum_high_kernel(own, one, three, keep, near_up, near_down, far):
    def total(i):
        return wide(own[i]) + wide(one[i]) + wide(three[i])

    keep[...] = total(0)
    near_down[...] = total(1).astype(BF)
    near_up[...] = total(2).astype(BF)
    far[...] = total(3).astype(BF)


def sum_high(own, one, three):
    shape = jax.ShapeDtypeStruct(PIECE, BF)
    return pl.pallas_call(
        sum_high_kernel,
        in_specs=[VMEM] * 3,
        out_specs=[VMEM] * 4,
        out_shape=[jax.ShapeDtypeStruct(PIECE, F32), shape, shape, shape],
        cost_estimate=cost(100_000_000),
        compiler_params=SMALL, name="sum_high",
    )(own, one, three)


def sum_low_kernel(own, one, three, own_out, near_down, near_up, keep):
    def total(i):
        return wide(own[i]) + wide(one[i]) + wide(three[i])

    own_out[...] = total(0)
    near_down[...] = total(1).astype(BF)
    near_up[...] = total(2).astype(BF)
    keep[...] = total(3)


def sum_low(own, one, three):
    kept = jax.ShapeDtypeStruct(PIECE, F32)
    shape = jax.ShapeDtypeStruct(PIECE, BF)
    return pl.pallas_call(
        sum_low_kernel,
        in_specs=[VMEM] * 3,
        out_specs=[VMEM] * 4,
        out_shape=[kept, shape, shape, kept],
        cost_estimate=cost(100_000_000),
        compiler_params=SMALL,
        name="sum_low",
    )(own, one, three)


def sum_two_kernel(high, low, down, far, up, two_down, two_up):
    two_down[...] = (low[...] + wide(down[...]) + wide(far[...])).astype(BF)
    two_up[...] = (high[...] + wide(up[...])).astype(BF)


def sum_two(high, low, down, far, up):
    shape = jax.ShapeDtypeStruct(PIECE, BF)
    return pl.pallas_call(
        sum_two_kernel,
        in_specs=[VMEM] * 5,
        out_specs=[VMEM] * 2,
        out_shape=[shape, shape],
        cost_estimate=cost(100_000_000),
        compiler_params=SMALL,
        name="sum_two",
    )(high, low, down, far, up)


def close_kernel(own, a, b, c, d, dk_ref, dv_ref):
    total = own[...] + wide(a[...]) + wide(b[...]) + wide(c[...]) + wide(d[...])
    dk_ref[...] = (total[:, :HEAD_DIM] * SCALE).astype(BF)
    dv_ref[...] = total[:, HEAD_DIM:].astype(BF)


def close(own, parts):
    shape = jax.ShapeDtypeStruct((HALF, HEAD_DIM), BF)
    return pl.pallas_call(
        close_kernel, out_shape=[shape, shape], in_specs=[VMEM] * 5, out_specs=[VMEM] * 2, compiler_params=SMALL, name="close"
    )(own, *parts)


def plan(gate):
    z = lax.axis_index("z")
    x = lax.axis_index("x")
    own = z * 4 + x
    totals = gate + lax.ppermute(gate, "head", [(0, 1), (1, 0), (2, 3), (3, 2)])
    totals = totals + lax.ppermute(totals, "head", [(0, 2), (2, 0), (1, 3), (3, 1)])
    row = lax.dynamic_slice_in_dim(totals, own, 1, 0)[0]
    columns = jnp.arange(NBLK, dtype=jnp.int32)
    ranked = jnp.where(columns < own, row * NBLK + columns, -1)
    rank = jnp.sum((ranked[None, :] > ranked[:, None]).astype(jnp.int32), axis=1)
    used = ((rank < TOPK) & (ranked >= 0)) | (columns == own)
    core = lax.axis_index("core")
    way = 1 - 2 * core
    dz = (way * (z - columns // 4)) % 8
    dx = (way * (x - columns % 4)) % 4
    pos = jnp.where(dz == 0, 0, jnp.where(dz <= 4, 2 * dz - 1, 2 * (8 - dz)))
    place = dx * 8 + pos
    live = jnp.sum((place[None, :] == columns[:, None]) & used[None, :], axis=1, dtype=jnp.int32)
    return jnp.concatenate([live, core[None]])


def on_device(query, key, value, grad_out, gate_score):
    piece = join(key, value)
    a1, b1 = shift(piece, "z", 1), shift(piece, "z", -1)
    a2, b2 = shift(piece, "z", 2), shift(piece, "z", -2)
    a3, b3, a4 = shift(a2, "z", 1), shift(b2, "z", -1), shift(a2, "z", 2)
    low0 = stack(piece, a1, b1, a2)
    high0 = stack(b2, a3, b3, a4)
    low1, high1 = shift(low0, "x", 1), shift(high0, "x", 1)
    low2, high2 = shift(low1, "x", 1), shift(high1, "x", 1)
    low3, high3 = shift(low0, "x", -1), shift(high0, "x", -1)

    qg = prepare(query, grad_out, a3)
    info = plan(gate_score[0])
    qg = (qg, swap(qg))

    state = forward(0, info, [low0, high0, low1, high1], qg, None, False)
    state = forward(24, info, [low3, high3], qg, state, False)
    mine, acc, acc_away = forward(16, info, [low2, high2], qg, state, True)
    other = swap(mine)
    acc_other = swap(acc_away)

    dq, (high2,) = backward(20, info, [high2], qg, mine, other, None)
    high2 = shift(high2, "x", -1)
    dq, (low2,) = backward(16, info, [low2], qg, mine, other, dq)
    low2 = shift(low2, "x", -1)
    dq, (low3, high3) = backward(24, info, [low3, high3], qg, mine, other, dq)
    high3, low3 = shift(high3, "x", 1), shift(low3, "x", 1)
    dq, (low1, high1) = backward(8, info, [low1, high1], qg, mine, other, dq)
    high1 = shift((wide(high1) + wide(high2)).astype(BF), "x", -1)
    low1 = shift((wide(low1) + wide(low2)).astype(BF), "x", -1)
    dq, (low0, high0) = backward(0, info, [low0, high0], qg, mine, other, dq)

    keep_high, up, down, far = sum_high(high0, high1, high3)
    down, far, up = shift(down, "z", -1), shift(far, "z", -2), shift(up, "z", 1)
    own, near_down, near_up, keep_low = sum_low(low0, low1, low3)
    two_down, two_up = sum_two(keep_high, keep_low, down, far, up)
    parts = [
        shift(near_down, "z", -1),
        shift(near_up, "z", 1),
        shift(two_up, "z", 2),
        shift(two_down, "z", -2),
    ]
    grad_key, grad_value = close(own, parts)
    attended, grad_query = finish(mine, other, acc, acc_other, dq[0], swap(dq[1]))
    return (attended, grad_query, grad_key, grad_value)


def solution(mesh):
    devices = mesh.devices.reshape(8, 4, 2, 4)
    split = Mesh(devices, ("z", "x", "core", "head"))
    spec = P(("z", "x", "core"), "head")
    return jax.shard_map(
        on_device,
        mesh=split,
        in_specs=(spec, spec, spec, spec, P("head", None, None)),
        out_specs=(spec, spec, spec, spec),
        check_vma=False,
    )
```

```python
import functools
import math

import jax
import jax.numpy as jnp
from jax import lax
from jax.experimental import pallas as pl
from jax.experimental.pallas import tpu as pltpu
from jax.sharding import Mesh
from jax.sharding import PartitionSpec as P

HEAD_DIM = 128
GROUP = 4
TOPK = 8
NBLK = 32
HALF = 256
COLS = GROUP * HALF
SCALE = 1.0 / math.sqrt(HEAD_DIM)
SCALE2 = SCALE / math.log(2.0)
NEG = -1e30
MASKED = -3e38
BF = jnp.bfloat16
F32 = jnp.float32
SIZES = {"z": 8, "x": 4}
NT = (((1,), (1,)), ((), ()))
NN = (((1,), (0,)), ((), ()))
CORE_AT = 32
QUAD = 4
VMEM_LIMIT = 24 * 1024 * 1024
STAT = (2, 3, COLS)
ACC = (HEAD_DIM, COLS)
PAIR = (2, COLS, HEAD_DIM)
PIECE = (HALF, 2 * HEAD_DIM)


def dot(a, b, dims):
    return lax.dot_general(a, b, dims, preferred_element_type=F32)


def wide(a):
    return a.astype(F32)


def shift(a, axis, d):
    n = SIZES[axis]
    return lax.ppermute(a, (axis, "core"), [(2 * i + c, 2 * ((i + d * (1 - 2 * c)) % n) + c) for i in range(n) for c in range(2)])


def swap(a):
    return lax.ppermute(a, "core", [(0, 1), (1, 0)])


def keep_mask(off):
    i = lax.broadcasted_iota(jnp.int32, (HALF, HALF), 0)
    j = lax.broadcasted_iota(jnp.int32, (HALF, HALF), 1)
    return (i - j) <= off


def place_of(i, bases):
    base = bases[0]
    for a, b in enumerate(bases[1:], 1):
        base = jnp.where(i // QUAD == a, b, base)
    return base + i % QUAD


def fetch(i, kv_refs, kv_buf):
    for a, ref in enumerate(kv_refs):

        @pl.when(i // QUAD == a)
        def _():
            kv_buf[...] = ref[0]

    return kv_buf[...]


def query_refs(refs):
    return [ref.at[0] for ref in refs]


def grad_refs(refs):
    return [ref.at[1] for ref in refs]


def forward_kernel(bases, first, last, info, *refs):
    n = len(bases)
    kv_refs, refs = refs[:n], refs[n:]
    q_refs, g_refs, refs = query_refs(refs[:2]), grad_refs(refs[:2]), refs[2:]
    if not first:
        stat_in, acc_in, refs = refs[0], refs[1:3], refs[3:]
    stat_ref, acc_refs, (s_ref, p_ref, kv_buf) = refs[0], refs[1:3], refs[3:]
    i = pl.program_id(0)
    core = info[CORE_AT]

    @pl.when(i == 0)
    def _():
        if first:
            stat_ref[:, 0:1, :] = jnp.full((2, 1, COLS), NEG, F32)
            stat_ref[:, 1:3, :] = jnp.zeros((2, 2, COLS), F32)
            for half in range(2):
                acc_refs[half][...] = jnp.zeros(ACC, F32)
        else:
            stat_ref[...] = stat_in[...]
            for half in range(2):
                acc_refs[half][...] = acc_in[half][...]

    def step(masked):
        kv = fetch(i, kv_refs, kv_buf)
        k = kv[:, :HEAD_DIM]
        vt = jnp.transpose(kv[:, HEAD_DIM:])
        for half in range(2):
            s_ref[:, pl.ds(half * COLS, COLS)] = dot(k, q_refs[half][...], NT)
        for half in range(2):
            acc = acc_refs[half]
            if masked:
                keep = keep_mask(jnp.where(i == 0, half * HALF * (1 - 2 * core), HALF))
            for h in range(GROUP):
                cols = pl.ds(h * HALF, HALF)
                flat = pl.ds(half * COLS + h * HALF, HALF)
                s = s_ref[:, flat]
                if masked:
                    s = jnp.where(keep, s, MASKED)
                m_old = stat_ref[half, 0:1, cols]
                m_new = jnp.maximum(m_old, jnp.max(s, axis=0, keepdims=True) * SCALE2)
                alpha = jnp.exp2(m_old - m_new)
                p = jnp.exp2(s * SCALE2 - m_new)
                stat_ref[half, 0:1, cols] = m_new
                stat_ref[half, 1:2, cols] = stat_ref[half, 1:2, cols] * alpha + jnp.sum(p, axis=0, keepdims=True)
                acc[:, cols] = acc[:, cols] * alpha
                p_ref[:, flat] = p.astype(BF)
            acc[...] += dot(vt, p_ref[:, pl.ds(half * COLS, COLS)], NN)

    pl.when(info[place_of(i, bases)] > 0)(lambda: step(first))

    if last:

        @pl.when(i == QUAD * n - 1)
        def _():
            eye = (
                lax.broadcasted_iota(jnp.int32, (HEAD_DIM, HEAD_DIM), 0)
                == lax.broadcasted_iota(jnp.int32, (HEAD_DIM, HEAD_DIM), 1)
            ).astype(F32).astype(BF)
            for half in range(2):
                turned = dot(eye, g_refs[half][...], NT)
                stat_ref[half, 2:3, :] = jnp.sum(turned * acc_refs[half][...], axis=0, keepdims=True)


def combine(mine, other, half):
    m0 = mine[half, 0:1, :]
    m1 = other[1 - half, 0:1, :]
    m = jnp.maximum(m0, m1)
    e0 = jnp.exp2(m0 - m)
    e1 = jnp.exp2(m1 - m)
    total = mine[half, 1:2, :] * e0 + other[1 - half, 1:2, :] * e1
    return m + jnp.log2(total), e0 / total, e1 / total


def backward_kernel(bases, first, masks, info, *refs):
    n = len(bases)
    kv_refs, refs = refs[:n], refs[n:]
    q_refs, g_refs, refs = query_refs(refs[:2]), grad_refs(refs[:2]), refs[2:]
    mine, other, refs = refs[0], refs[1], refs[2:]
    if not first:
        dq_in, refs = refs[:2], refs[2:]
    dq_refs, out_refs, refs = refs[:2], refs[2 : 2 + n], refs[2 + n :]
    row_ref, s_ref, dp_ref, p_ref, ds_ref, kv_buf, out_buf = refs
    i = pl.program_id(0)
    core = info[CORE_AT]

    @pl.when(i == 0)
    def _():
        for half in range(2):
            lse, w0, w1 = combine(mine, other, half)
            row_ref[half, 0:1, :] = lse
            row_ref[half, 1:2, :] = mine[half, 2:3, :] * w0 + other[1 - half, 2:3, :] * w1
            dq_refs[half][...] = jnp.zeros(ACC, F32) if first else dq_in[half][...]

    def step(masked):
        kv = fetch(i, kv_refs, kv_buf)
        k = kv[:, :HEAD_DIM]
        v = kv[:, HEAD_DIM:]
        kt = jnp.transpose(k)
        for half in range(2):
            cols = pl.ds(half * COLS, COLS)
            s_ref[:, cols] = dot(k, q_refs[half][...], NT)
            dp_ref[:, cols] = dot(v, g_refs[half][...], NT)
        for half in range(2):
            if masked:
                keep = keep_mask(jnp.where(i == 0, half * HALF * (1 - 2 * core), HALF))
            for h in range(GROUP):
                cols = pl.ds(h * HALF, HALF)
                flat = pl.ds(half * COLS + h * HALF, HALF)
                p = jnp.exp2(s_ref[:, flat] * SCALE2 - row_ref[half, 0:1, cols])
                if masked:
                    p = jnp.where(keep, p, 0.0)
                p_ref[:, flat] = p.astype(BF)
                ds_ref[:, flat] = (p * (dp_ref[:, flat] - row_ref[half, 1:2, cols])).astype(BF)
            dq_refs[half][...] += dot(kt, ds_ref[:, pl.ds(half * COLS, COLS)], NN)
        dk = jnp.zeros((HALF, HEAD_DIM), F32)
        dv = jnp.zeros((HALF, HEAD_DIM), F32)
        for half in range(2):
            cols = pl.ds(half * COLS, COLS)
            dk = dk + dot(ds_ref[:, cols], q_refs[half][...], NN)
            dv = dv + dot(p_ref[:, cols], g_refs[half][...], NN)
        out_buf[:, :HEAD_DIM] = dk.astype(BF)
        out_buf[:, HEAD_DIM:] = dv.astype(BF)

    live = info[place_of(i, bases)] > 0
    pl.when(live)(lambda: step(masks))

    @pl.when(jnp.logical_not(live))
    def _():
        out_buf[...] = jnp.zeros(PIECE, BF)

    for a, ref in enumerate(out_refs):

        @pl.when(i // QUAD == a)
        def _():
            ref[0] = out_buf[...]


def finish_kernel(mine, other, acc_mine, acc_other, dq_mine, dq_other, att_ref, dq_ref):
    lse, w0, w1 = combine(mine, other, 0)
    for h in range(GROUP):
        cols = slice(h * HALF, (h + 1) * HALF)
        rows = slice(h * HEAD_DIM, (h + 1) * HEAD_DIM)
        out = acc_mine[:, cols] * w0[:, cols] + acc_other[:, cols] * w1[:, cols]
        att_ref[:, rows] = jnp.transpose(out).astype(BF)
        dq_ref[:, rows] = jnp.transpose((dq_mine[:, cols] + dq_other[:, cols]) * SCALE).astype(BF)


def whole(shape):
    return pl.BlockSpec(shape, lambda i, info: (0,) * len(shape))


def piece_specs(n):
    def spec(a):
        return pl.BlockSpec((1,) + PIECE, lambda i, info: (jnp.clip(i - QUAD * a, 0, QUAD - 1), 0, 0))

    return [spec(a) for a in range(n)]


def cost(flops):
    return pl.CostEstimate(flops=flops, bytes_accessed=1 << 16, transcendentals=0)


def forward(bases, info, kvs, qg, state, last):
    n = len(kvs)
    first = state is None
    ins = list(kvs) + list(qg) + ([] if first else list(state))
    specs = piece_specs(n) + [whole(PAIR)] * 2
    if not first:
        specs += [whole(STAT), whole(ACC), whole(ACC)]
    return pl.pallas_call(
        functools.partial(forward_kernel, bases, first, last),
        grid_spec=pltpu.PrefetchScalarGridSpec(
            num_scalar_prefetch=1,
            grid=(QUAD * n,),
            in_specs=specs,
            out_specs=[whole(STAT), whole(ACC), whole(ACC)],
            scratch_shapes=[
                pltpu.VMEM((HALF, 2 * COLS), F32),
                pltpu.VMEM((HALF, 2 * COLS), BF),
                pltpu.VMEM(PIECE, BF),
            ],
        ),
        out_shape=[jax.ShapeDtypeStruct(s, F32) for s in (STAT, ACC, ACC)],
        compiler_params=pltpu.CompilerParams(vmem_limit_bytes=VMEM_LIMIT),
        cost_estimate=cost(200_000_000),
        name="forward",
    )(info, *ins)


def backward(bases, info, kvs, qg, mine, other, dq):
    n = len(kvs)
    first = dq is None
    ins = list(kvs) + list(qg) + [mine, other] + ([] if first else list(dq))
    specs = piece_specs(n) + [whole(PAIR)] * 2 + [whole(STAT)] * 2
    if not first:
        specs += [whole(ACC), whole(ACC)]
    wide_shape = (HALF, 2 * COLS)
    res = pl.pallas_call(
        functools.partial(backward_kernel, bases, first, bases[0] == 0),
        grid_spec=pltpu.PrefetchScalarGridSpec(
            num_scalar_prefetch=1,
            grid=(QUAD * n,),
            in_specs=specs,
            out_specs=[whole(ACC), whole(ACC)] + piece_specs(n),
            scratch_shapes=[
                pltpu.VMEM((2, 2, COLS), F32),
                pltpu.VMEM(wide_shape, F32),
                pltpu.VMEM(wide_shape, F32),
                pltpu.VMEM(wide_shape, BF),
                pltpu.VMEM(wide_shape, BF),
                pltpu.VMEM(PIECE, BF),
                pltpu.VMEM(PIECE, BF),
            ],
        ),
        out_shape=[jax.ShapeDtypeStruct(ACC, F32)] * 2 + [jax.ShapeDtypeStruct(a.shape, BF) for a in kvs],
        compiler_params=pltpu.CompilerParams(vmem_limit_bytes=VMEM_LIMIT),
        cost_estimate=cost(200_000_000),
        name="backward",
    )(info, *ins)
    return res[:2], res[2:]


def finish(mine, other, acc_mine, acc_other, dq_mine, dq_other):
    shape = jax.ShapeDtypeStruct((HALF, GROUP * HEAD_DIM), BF)
    return pl.pallas_call(
        finish_kernel,
        in_specs=[VMEM] * 6,
        out_specs=[VMEM] * 2,
        out_shape=[shape, shape],
        compiler_params=SMALL,
        cost_estimate=pl.CostEstimate(flops=1 << 20, bytes_accessed=1 << 16, transcendentals=0),
        name="finish",
    )(mine, other, acc_mine, acc_other, dq_mine, dq_other)


VMEM = pl.BlockSpec(memory_space=pltpu.VMEM)
SMALL = pltpu.CompilerParams(vmem_limit_bytes=8 * 1024 * 1024)


def join_kernel(k_ref, v_ref, out_ref, sems):
    copies = [
        pltpu.make_async_copy(k_ref, out_ref.at[:, pl.ds(0, HEAD_DIM)], sems.at[0]),
        pltpu.make_async_copy(v_ref, out_ref.at[:, pl.ds(HEAD_DIM, HEAD_DIM)], sems.at[1]),
    ]
    for copy in copies:
        copy.start()
    for copy in copies:
        copy.wait()


def join(k, v):
    return pl.pallas_call(
        join_kernel,
        out_shape=jax.ShapeDtypeStruct(PIECE, BF),
        in_specs=[pl.BlockSpec(memory_space=pl.ANY)] * 2,
        out_specs=VMEM,
        scratch_shapes=[pltpu.SemaphoreType.DMA((2,))],
        name="join",
    )(k, v)


def prepare_kernel(query, grad_out, after, qg_ref):
    for h in range(GROUP):
        rows = slice(h * HALF, (h + 1) * HALF)
        cols = slice(h * HEAD_DIM, (h + 1) * HEAD_DIM)
        qg_ref[0, rows, :] = query[:, cols]
        qg_ref[1, rows, :] = grad_out[:, cols]


def prepare(query, grad_out, after):
    return pl.pallas_call(
        prepare_kernel,
        in_specs=[VMEM] * 2 + [pl.BlockSpec(memory_space=pl.ANY)],
        out_specs=VMEM,
        out_shape=jax.ShapeDtypeStruct(PAIR, BF),
        cost_estimate=cost(100_000_000),
        compiler_params=SMALL,
        name="prepare",
    )(query, grad_out, after)


def stack_kernel(*refs):
    for i in range(QUAD):
        refs[-1][i] = refs[i][...]


def stack(*pieces):
    return pl.pallas_call(stack_kernel, out_shape=jax.ShapeDtypeStruct((QUAD,) + PIECE, BF), in_specs=[VMEM] * QUAD, out_specs=VMEM, compiler_params=SMALL, name="stack")(*pieces)


def sum_high_kernel(own, one, three, keep, near_up, near_down, far):
    def total(i):
        return wide(own[i]) + wide(one[i]) + wide(three[i])

    keep[...] = total(0)
    near_down[...] = total(1).astype(BF)
    near_up[...] = total(2).astype(BF)
    far[...] = total(3).astype(BF)


def sum_high(own, one, three):
    shape = jax.ShapeDtypeStruct(PIECE, BF)
    return pl.pallas_call(
        sum_high_kernel,
        in_specs=[VMEM] * 3,
        out_specs=[VMEM] * 4,
        out_shape=[jax.ShapeDtypeStruct(PIECE, F32), shape, shape, shape],
        cost_estimate=cost(100_000_000),
        compiler_params=SMALL, name="sum_high",
    )(own, one, three)


def sum_low_kernel(own, one, three, own_out, near_down, near_up, keep):
    def total(i):
        return wide(own[i]) + wide(one[i]) + wide(three[i])

    own_out[...] = total(0)
    near_down[...] = total(1).astype(BF)
    near_up[...] = total(2).astype(BF)
    keep[...] = total(3)


def sum_low(own, one, three):
    kept = jax.ShapeDtypeStruct(PIECE, F32)
    shape = jax.ShapeDtypeStruct(PIECE, BF)
    return pl.pallas_call(
        sum_low_kernel,
        in_specs=[VMEM] * 3,
        out_specs=[VMEM] * 4,
        out_shape=[kept, shape, shape, kept],
        cost_estimate=cost(100_000_000),
        compiler_params=SMALL,
        name="sum_low",
    )(own, one, three)


def sum_two_kernel(high, low, down, far, up, two_down, two_up):
    two_down[...] = (low[...] + wide(down[...]) + wide(far[...])).astype(BF)
    two_up[...] = (high[...] + wide(up[...])).astype(BF)


def sum_two(high, low, down, far, up):
    shape = jax.ShapeDtypeStruct(PIECE, BF)
    return pl.pallas_call(
        sum_two_kernel,
        in_specs=[VMEM] * 5,
        out_specs=[VMEM] * 2,
        out_shape=[shape, shape],
        cost_estimate=cost(100_000_000),
        compiler_params=SMALL,
        name="sum_two",
    )(high, low, down, far, up)


def close_kernel(own, a, b, c, d, dk_ref, dv_ref):
    total = own[...] + wide(a[...]) + wide(b[...]) + wide(c[...]) + wide(d[...])
    dk_ref[...] = (total[:, :HEAD_DIM] * SCALE).astype(BF)
    dv_ref[...] = total[:, HEAD_DIM:].astype(BF)


def close(own, parts):
    shape = jax.ShapeDtypeStruct((HALF, HEAD_DIM), BF)
    return pl.pallas_call(
        close_kernel, out_shape=[shape, shape], in_specs=[VMEM] * 5, out_specs=[VMEM] * 2, compiler_params=SMALL, name="close"
    )(own, *parts)


def plan(gate):
    z = lax.axis_index("z")
    x = lax.axis_index("x")
    own = z * 4 + x
    totals = gate + lax.ppermute(gate, "head", [(0, 1), (1, 0), (2, 3), (3, 2)])
    totals = totals + lax.ppermute(totals, "head", [(0, 2), (2, 0), (1, 3), (3, 1)])
    row = lax.dynamic_slice_in_dim(totals, own, 1, 0)[0]
    columns = jnp.arange(NBLK, dtype=jnp.int32)
    ranked = jnp.where(columns < own, row * NBLK + columns, -1)
    rank = jnp.sum((ranked[None, :] > ranked[:, None]).astype(jnp.int32), axis=1)
    used = ((rank < TOPK) & (ranked >= 0)) | (columns == own)
    core = lax.axis_index("core")
    way = 1 - 2 * core
    dz = (way * (z - columns // 4)) % 8
    dx = (way * (x - columns % 4)) % 4
    pos = jnp.where(dz == 0, 0, jnp.where(dz <= 4, 2 * dz - 1, 2 * (8 - dz)))
    place = dx * 8 + pos
    live = jnp.sum((place[None, :] == columns[:, None]) & used[None, :], axis=1, dtype=jnp.int32)
    return jnp.concatenate([live, core[None]])


def on_device(query, key, value, grad_out, gate_score):
    piece = join(key, value)
    a1, b1 = shift(piece, "z", 1), shift(piece, "z", -1)
    a2, b2 = shift(piece, "z", 2), shift(piece, "z", -2)
    a3, b3, a4 = shift(a2, "z", 1), shift(b2, "z", -1), shift(a2, "z", 2)
    low0 = stack(piece, a1, b1, a2)
    high0 = stack(b2, a3, b3, a4)
    low1, high1 = shift(low0, "x", 1), shift(high0, "x", 1)
    low2, high2 = shift(low1, "x", 1), shift(high1, "x", 1)
    low3, high3 = shift(low0, "x", -1), shift(high0, "x", -1)

    qg = prepare(query, grad_out, a3)
    info = plan(gate_score[0])
    qg = (qg, swap(qg))

    state = forward((0, 4, 8, 12), info, [low0, high0, low1, high1], qg, None, False)
    state = forward((24, 16), info, [low3, low2], qg, state, False)
    mine, acc, acc_away = forward((28, 20), info, [high3, high2], qg, state, True)
    other = swap(mine)
    acc_other = swap(acc_away)

    dq, (high2,) = backward((20,), info, [high2], qg, mine, other, None)
    high2 = shift(high2, "x", -1)
    dq, (low2,) = backward((16,), info, [low2], qg, mine, other, dq)
    low2 = shift(low2, "x", -1)
    dq, (low3, high3) = backward((24, 28), info, [low3, high3], qg, mine, other, dq)
    high3, low3 = shift(high3, "x", 1), shift(low3, "x", 1)
    dq, (low1, high1) = backward((8, 12), info, [low1, high1], qg, mine, other, dq)
    high1 = shift((wide(high1) + wide(high2)).astype(BF), "x", -1)
    low1 = shift((wide(low1) + wide(low2)).astype(BF), "x", -1)
    dq, (low0, high0) = backward((0, 4), info, [low0, high0], qg, mine, other, dq)

    keep_high, up, down, far = sum_high(high0, high1, high3)
    down, far, up = shift(down, "z", -1), shift(far, "z", -2), shift(up, "z", 1)
    own, near_down, near_up, keep_low = sum_low(low0, low1, low3)
    two_down, two_up = sum_two(keep_high, keep_low, down, far, up)
    parts = [
        shift(near_down, "z", -1),
        shift(near_up, "z", 1),
        shift(two_up, "z", 2),
        shift(two_down, "z", -2),
    ]
    grad_key, grad_value = close(own, parts)
    attended, grad_query = finish(mine, other, acc, acc_other, dq[0], swap(dq[1]))
    return (attended, grad_query, grad_key, grad_value)


def solution(mesh):
    devices = mesh.devices.reshape(8, 4, 2, 4)
    split = Mesh(devices, ("z", "x", "core", "head"))
    spec = P(("z", "x", "core"), "head")
    return jax.shard_map(
        on_device,
        mesh=split,
        in_specs=(spec, spec, spec, spec, P("head", None, None)),
        out_specs=(spec, spec, spec, spec),
        check_vma=False,
    )
```

```python
import functools
import math

import jax
import jax.numpy as jnp
from jax import lax
from jax.experimental import pallas as pl
from jax.experimental.pallas import tpu as pltpu
from jax.sharding import Mesh
from jax.sharding import PartitionSpec as P

HEAD_DIM = 128
GROUP = 4
TOPK = 8
NBLK = 32
HALF = 256
COLS = GROUP * HALF
SCALE = 1.0 / math.sqrt(HEAD_DIM)
SCALE2 = SCALE / math.log(2.0)
NEG = -1e30
MASKED = -3e38
BF = jnp.bfloat16
F32 = jnp.float32
SIZES = {"z": 8, "x": 4}
NT = (((1,), (1,)), ((), ()))
NN = (((1,), (0,)), ((), ()))
CORE_AT = 32
QUAD = 4
VMEM_LIMIT = 24 * 1024 * 1024
STAT = (2, 3, COLS)
ACC = (HEAD_DIM, COLS)
PAIR = (2, COLS, HEAD_DIM)
PIECE = (HALF, 2 * HEAD_DIM)


def dot(a, b, dims):
    return lax.dot_general(a, b, dims, preferred_element_type=F32)


def wide(a):
    return a.astype(F32)


def shift(a, axis, d):
    n = SIZES[axis]
    return lax.ppermute(a, (axis, "core"), [(2 * i + c, 2 * ((i + d * (1 - 2 * c)) % n) + c) for i in range(n) for c in range(2)])


def swap(a):
    return lax.ppermute(a, "core", [(0, 1), (1, 0)])


def keep_mask(off):
    i = lax.broadcasted_iota(jnp.int32, (HALF, HALF), 0)
    j = lax.broadcasted_iota(jnp.int32, (HALF, HALF), 1)
    return (i - j) <= off


def place_of(i, bases):
    base = bases[0]
    for a, b in enumerate(bases[1:], 1):
        base = jnp.where(i // QUAD == a, b, base)
    return base + i % QUAD


def fetch(i, kv_refs, kv_buf):
    for a, ref in enumerate(kv_refs):

        @pl.when(i // QUAD == a)
        def _():
            kv_buf[...] = ref[0]

    return kv_buf[...]


def query_refs(refs):
    return [ref.at[0] for ref in refs]


def grad_refs(refs):
    return [ref.at[1] for ref in refs]


def forward_kernel(bases, first, last, info, *refs):
    n = len(bases)
    kv_refs, refs = refs[:n], refs[n:]
    q_refs, g_refs, refs = query_refs(refs[:2]), grad_refs(refs[:2]), refs[2:]
    if not first:
        stat_in, acc_in, refs = refs[0], refs[1:3], refs[3:]
    stat_ref, acc_refs, (s_ref, p_ref, kv_buf) = refs[0], refs[1:3], refs[3:]
    i = pl.program_id(0)
    core = info[CORE_AT]

    @pl.when(i == 0)
    def _():
        if first:
            stat_ref[:, 0:1, :] = jnp.full((2, 1, COLS), NEG, F32)
            stat_ref[:, 1:3, :] = jnp.zeros((2, 2, COLS), F32)
            for half in range(2):
                acc_refs[half][...] = jnp.zeros(ACC, F32)
        else:
            stat_ref[...] = stat_in[...]
            for half in range(2):
                acc_refs[half][...] = acc_in[half][...]

    def step(masked):
        kv = fetch(i, kv_refs, kv_buf)
        k = kv[:, :HEAD_DIM]
        vt = jnp.transpose(kv[:, HEAD_DIM:])
        for half in range(2):
            s_ref[:, pl.ds(half * COLS, COLS)] = dot(k, q_refs[half][...], NT)
        for half in range(2):
            acc = acc_refs[half]
            if masked:
                keep = keep_mask(jnp.where(i == 0, half * HALF * (1 - 2 * core), HALF))
            for h in range(GROUP):
                cols = pl.ds(h * HALF, HALF)
                flat = pl.ds(half * COLS + h * HALF, HALF)
                s = s_ref[:, flat]
                if masked:
                    s = jnp.where(keep, s, MASKED)
                m_old = stat_ref[half, 0:1, cols]
                m_new = jnp.maximum(m_old, jnp.max(s, axis=0, keepdims=True) * SCALE2)
                alpha = jnp.exp2(m_old - m_new)
                p = jnp.exp2(s * SCALE2 - m_new)
                stat_ref[half, 0:1, cols] = m_new
                stat_ref[half, 1:2, cols] = stat_ref[half, 1:2, cols] * alpha + jnp.sum(p, axis=0, keepdims=True)
                acc[:, cols] = acc[:, cols] * alpha
                p_ref[:, flat] = p.astype(BF)
            acc[...] += dot(vt, p_ref[:, pl.ds(half * COLS, COLS)], NN)

    pl.when(info[place_of(i, bases)] > 0)(lambda: step(first))

    if last:

        @pl.when(i == QUAD * n - 1)
        def _():
            eye = (
                lax.broadcasted_iota(jnp.int32, (HEAD_DIM, HEAD_DIM), 0)
                == lax.broadcasted_iota(jnp.int32, (HEAD_DIM, HEAD_DIM), 1)
            ).astype(F32).astype(BF)
            for half in range(2):
                turned = dot(eye, g_refs[half][...], NT)
                stat_ref[half, 2:3, :] = jnp.sum(turned * acc_refs[half][...], axis=0, keepdims=True)


def combine(mine, other, half):
    m0 = mine[half, 0:1, :]
    m1 = other[1 - half, 0:1, :]
    m = jnp.maximum(m0, m1)
    e0 = jnp.exp2(m0 - m)
    e1 = jnp.exp2(m1 - m)
    total = mine[half, 1:2, :] * e0 + other[1 - half, 1:2, :] * e1
    return m + jnp.log2(total), e0 / total, e1 / total


def backward_kernel(bases, first, masks, info, *refs):
    n = len(bases)
    kv_refs, refs = refs[:n], refs[n:]
    q_refs, g_refs, refs = query_refs(refs[:2]), grad_refs(refs[:2]), refs[2:]
    mine, other, refs = refs[0], refs[1], refs[2:]
    if not first:
        dq_in, refs = refs[:2], refs[2:]
    dq_refs, out_refs, refs = refs[:2], refs[2 : 2 + n], refs[2 + n :]
    row_ref, s_ref, dp_ref, p_ref, ds_ref, kv_buf, out_buf = refs
    i = pl.program_id(0)
    core = info[CORE_AT]

    @pl.when(i == 0)
    def _():
        for half in range(2):
            lse, w0, w1 = combine(mine, other, half)
            row_ref[half, 0:1, :] = lse
            row_ref[half, 1:2, :] = mine[half, 2:3, :] * w0 + other[1 - half, 2:3, :] * w1
            dq_refs[half][...] = jnp.zeros(ACC, F32) if first else dq_in[half][...]

    def step(masked):
        kv = fetch(i, kv_refs, kv_buf)
        k = kv[:, :HEAD_DIM]
        v = kv[:, HEAD_DIM:]
        kt = jnp.transpose(k)
        for half in range(2):
            cols = pl.ds(half * COLS, COLS)
            s_ref[:, cols] = dot(k, q_refs[half][...], NT)
            dp_ref[:, cols] = dot(v, g_refs[half][...], NT)
        for half in range(2):
            if masked:
                keep = keep_mask(jnp.where(i == 0, half * HALF * (1 - 2 * core), HALF))
            for h in range(GROUP):
                cols = pl.ds(h * HALF, HALF)
                flat = pl.ds(half * COLS + h * HALF, HALF)
                p = jnp.exp2(s_ref[:, flat] * SCALE2 - row_ref[half, 0:1, cols])
                if masked:
                    p = jnp.where(keep, p, 0.0)
                p_ref[:, flat] = p.astype(BF)
                ds_ref[:, flat] = (p * (dp_ref[:, flat] - row_ref[half, 1:2, cols])).astype(BF)
            dq_refs[half][...] += dot(kt, ds_ref[:, pl.ds(half * COLS, COLS)], NN)
        dk = jnp.zeros((HALF, HEAD_DIM), F32)
        dv = jnp.zeros((HALF, HEAD_DIM), F32)
        for half in range(2):
            cols = pl.ds(half * COLS, COLS)
            dk = dk + dot(ds_ref[:, cols], q_refs[half][...], NN)
            dv = dv + dot(p_ref[:, cols], g_refs[half][...], NN)
        out_buf[:, :HEAD_DIM] = dk.astype(BF)
        out_buf[:, HEAD_DIM:] = dv.astype(BF)

    live = info[place_of(i, bases)] > 0
    pl.when(live)(lambda: step(masks))

    @pl.when(jnp.logical_not(live))
    def _():
        out_buf[...] = jnp.zeros(PIECE, BF)

    for a, ref in enumerate(out_refs):

        @pl.when(i // QUAD == a)
        def _():
            ref[0] = out_buf[...]


def finish_kernel(mine, other, acc_mine, acc_other, dq_mine, dq_other, att_ref, dq_ref):
    lse, w0, w1 = combine(mine, other, 0)
    for h in range(GROUP):
        cols = slice(h * HALF, (h + 1) * HALF)
        rows = slice(h * HEAD_DIM, (h + 1) * HEAD_DIM)
        out = acc_mine[:, cols] * w0[:, cols] + acc_other[:, cols] * w1[:, cols]
        att_ref[:, rows] = jnp.transpose(out).astype(BF)
        dq_ref[:, rows] = jnp.transpose((dq_mine[:, cols] + dq_other[:, cols]) * SCALE).astype(BF)


def whole(shape):
    return pl.BlockSpec(shape, lambda i, info: (0,) * len(shape))


def piece_specs(n):
    def spec(a):
        return pl.BlockSpec((1,) + PIECE, lambda i, info: (jnp.clip(i - QUAD * a, 0, QUAD - 1), 0, 0))

    return [spec(a) for a in range(n)]


def cost(flops):
    return pl.CostEstimate(flops=flops, bytes_accessed=1 << 16, transcendentals=0)


def forward(bases, info, kvs, qg, state, last):
    n = len(kvs)
    first = state is None
    ins = list(kvs) + list(qg) + ([] if first else list(state))
    specs = piece_specs(n) + [whole(PAIR)] * 2
    if not first:
        specs += [whole(STAT), whole(ACC), whole(ACC)]
    return pl.pallas_call(
        functools.partial(forward_kernel, bases, first, last),
        grid_spec=pltpu.PrefetchScalarGridSpec(
            num_scalar_prefetch=1,
            grid=(QUAD * n,),
            in_specs=specs,
            out_specs=[whole(STAT), whole(ACC), whole(ACC)],
            scratch_shapes=[
                pltpu.VMEM((HALF, 2 * COLS), F32),
                pltpu.VMEM((HALF, 2 * COLS), BF),
                pltpu.VMEM(PIECE, BF),
            ],
        ),
        out_shape=[jax.ShapeDtypeStruct(s, F32) for s in (STAT, ACC, ACC)],
        compiler_params=pltpu.CompilerParams(vmem_limit_bytes=VMEM_LIMIT),
        cost_estimate=cost(200_000_000),
        name="forward",
    )(info, *ins)


def backward(bases, info, kvs, qg, mine, other, dq):
    n = len(kvs)
    first = dq is None
    ins = list(kvs) + list(qg) + [mine, other] + ([] if first else list(dq))
    specs = piece_specs(n) + [whole(PAIR)] * 2 + [whole(STAT)] * 2
    if not first:
        specs += [whole(ACC), whole(ACC)]
    wide_shape = (HALF, 2 * COLS)
    res = pl.pallas_call(
        functools.partial(backward_kernel, bases, first, bases[0] == 0),
        grid_spec=pltpu.PrefetchScalarGridSpec(
            num_scalar_prefetch=1,
            grid=(QUAD * n,),
            in_specs=specs,
            out_specs=[whole(ACC), whole(ACC)] + piece_specs(n),
            scratch_shapes=[
                pltpu.VMEM((2, 2, COLS), F32),
                pltpu.VMEM(wide_shape, F32),
                pltpu.VMEM(wide_shape, F32),
                pltpu.VMEM(wide_shape, BF),
                pltpu.VMEM(wide_shape, BF),
                pltpu.VMEM(PIECE, BF),
                pltpu.VMEM(PIECE, BF),
            ],
        ),
        out_shape=[jax.ShapeDtypeStruct(ACC, F32)] * 2 + [jax.ShapeDtypeStruct(a.shape, BF) for a in kvs],
        compiler_params=pltpu.CompilerParams(vmem_limit_bytes=VMEM_LIMIT),
        cost_estimate=cost(200_000_000),
        name="backward",
    )(info, *ins)
    return res[:2], res[2:]


def finish(mine, other, acc_mine, acc_other, dq_mine, dq_other):
    shape = jax.ShapeDtypeStruct((HALF, GROUP * HEAD_DIM), BF)
    return pl.pallas_call(
        finish_kernel,
        in_specs=[VMEM] * 6,
        out_specs=[VMEM] * 2,
        out_shape=[shape, shape],
        compiler_params=SMALL,
        cost_estimate=pl.CostEstimate(flops=1 << 20, bytes_accessed=1 << 16, transcendentals=0),
        name="finish",
    )(mine, other, acc_mine, acc_other, dq_mine, dq_other)


VMEM = pl.BlockSpec(memory_space=pltpu.VMEM)
SMALL = pltpu.CompilerParams(vmem_limit_bytes=8 * 1024 * 1024)


def join_kernel(k_ref, v_ref, out_ref, sems):
    copies = [
        pltpu.make_async_copy(k_ref, out_ref.at[:, pl.ds(0, HEAD_DIM)], sems.at[0]),
        pltpu.make_async_copy(v_ref, out_ref.at[:, pl.ds(HEAD_DIM, HEAD_DIM)], sems.at[1]),
    ]
    for copy in copies:
        copy.start()
    for copy in copies:
        copy.wait()


def join(k, v):
    return pl.pallas_call(
        join_kernel,
        out_shape=jax.ShapeDtypeStruct(PIECE, BF),
        in_specs=[pl.BlockSpec(memory_space=pl.ANY)] * 2,
        out_specs=VMEM,
        scratch_shapes=[pltpu.SemaphoreType.DMA((2,))],
        name="join",
    )(k, v)


def prepare_kernel(query, grad_out, after, qg_ref):
    for h in range(GROUP):
        rows = slice(h * HALF, (h + 1) * HALF)
        cols = slice(h * HEAD_DIM, (h + 1) * HEAD_DIM)
        qg_ref[0, rows, :] = query[:, cols]
        qg_ref[1, rows, :] = grad_out[:, cols]


def prepare(query, grad_out, after):
    return pl.pallas_call(
        prepare_kernel,
        in_specs=[VMEM] * 2 + [pl.BlockSpec(memory_space=pl.ANY)],
        out_specs=VMEM,
        out_shape=jax.ShapeDtypeStruct(PAIR, BF),
        cost_estimate=cost(100_000_000),
        compiler_params=SMALL,
        name="prepare",
    )(query, grad_out, after)


def stack_kernel(*refs):
    for i in range(QUAD):
        refs[-1][i] = refs[i][...]


def stack(*pieces):
    return pl.pallas_call(stack_kernel, out_shape=jax.ShapeDtypeStruct((QUAD,) + PIECE, BF), in_specs=[VMEM] * QUAD, out_specs=VMEM, compiler_params=SMALL, name="stack")(*pieces)


def sum_high_kernel(own, one, three, keep, near_up, near_down, far):
    def total(i):
        return wide(own[i]) + wide(one[i]) + wide(three[i])

    keep[...] = total(0)
    near_down[...] = total(1).astype(BF)
    near_up[...] = total(2).astype(BF)
    far[...] = total(3).astype(BF)


def sum_high(own, one, three):
    shape = jax.ShapeDtypeStruct(PIECE, BF)
    return pl.pallas_call(
        sum_high_kernel,
        in_specs=[VMEM] * 3,
        out_specs=[VMEM] * 4,
        out_shape=[jax.ShapeDtypeStruct(PIECE, F32), shape, shape, shape],
        cost_estimate=cost(100_000_000),
        compiler_params=SMALL, name="sum_high",
    )(own, one, three)


def sum_low_kernel(own, one, three, own_out, near_down, near_up, keep):
    def total(i):
        return wide(own[i]) + wide(one[i]) + wide(three[i])

    own_out[...] = total(0)
    near_down[...] = total(1).astype(BF)
    near_up[...] = total(2).astype(BF)
    keep[...] = total(3)


def sum_low(own, one, three):
    kept = jax.ShapeDtypeStruct(PIECE, F32)
    shape = jax.ShapeDtypeStruct(PIECE, BF)
    return pl.pallas_call(
        sum_low_kernel,
        in_specs=[VMEM] * 3,
        out_specs=[VMEM] * 4,
        out_shape=[kept, shape, shape, kept],
        cost_estimate=cost(100_000_000),
        compiler_params=SMALL,
        name="sum_low",
    )(own, one, three)


def sum_two_kernel(high, low, down, far, up, two_down, two_up):
    two_down[...] = (low[...] + wide(down[...]) + wide(far[...])).astype(BF)
    two_up[...] = (high[...] + wide(up[...])).astype(BF)


def sum_two(high, low, down, far, up):
    shape = jax.ShapeDtypeStruct(PIECE, BF)
    return pl.pallas_call(
        sum_two_kernel,
        in_specs=[VMEM] * 5,
        out_specs=[VMEM] * 2,
        out_shape=[shape, shape],
        cost_estimate=cost(100_000_000),
        compiler_params=SMALL,
        name="sum_two",
    )(high, low, down, far, up)


def close_kernel(own, a, b, c, d, dk_ref, dv_ref):
    total = own[...] + wide(a[...]) + wide(b[...]) + wide(c[...]) + wide(d[...])
    dk_ref[...] = (total[:, :HEAD_DIM] * SCALE).astype(BF)
    dv_ref[...] = total[:, HEAD_DIM:].astype(BF)


def close(own, parts):
    shape = jax.ShapeDtypeStruct((HALF, HEAD_DIM), BF)
    return pl.pallas_call(
        close_kernel, out_shape=[shape, shape], in_specs=[VMEM] * 5, out_specs=[VMEM] * 2, compiler_params=SMALL, name="close"
    )(own, *parts)


def plan(gate):
    z = lax.axis_index("z")
    x = lax.axis_index("x")
    own = z * 4 + x
    totals = gate + lax.ppermute(gate, "head", [(0, 1), (1, 0), (2, 3), (3, 2)])
    totals = totals + lax.ppermute(totals, "head", [(0, 2), (2, 0), (1, 3), (3, 1)])
    row = lax.dynamic_slice_in_dim(totals, own, 1, 0)[0]
    columns = jnp.arange(NBLK, dtype=jnp.int32)
    ranked = jnp.where(columns < own, row * NBLK + columns, -1)
    rank = jnp.sum((ranked[None, :] > ranked[:, None]).astype(jnp.int32), axis=1)
    used = ((rank < TOPK) & (ranked >= 0)) | (columns == own)
    core = lax.axis_index("core")
    way = 1 - 2 * core
    dz = (way * (z - columns // 4)) % 8
    dx = (way * (x - columns % 4)) % 4
    pos = jnp.where(dz == 0, 0, jnp.where(dz <= 4, 2 * dz - 1, 2 * (8 - dz)))
    place = dx * 8 + pos
    live = jnp.sum((place[None, :] == columns[:, None]) & used[None, :], axis=1, dtype=jnp.int32)
    return jnp.concatenate([live, core[None]])


def on_device(query, key, value, grad_out, gate_score):
    piece = join(key, value)
    a1, b1 = shift(piece, "z", 1), shift(piece, "z", -1)
    a2, b2 = shift(piece, "z", 2), shift(piece, "z", -2)
    a3, b3, a4 = shift(a2, "z", 1), shift(b2, "z", -1), shift(a2, "z", 2)
    low0 = stack(piece, a1, b1, a2)
    high0 = stack(b2, a3, b3, a4)
    low1, high1 = shift(low0, "x", 1), shift(high0, "x", 1)
    low2, high2 = shift(low1, "x", 1), shift(high1, "x", 1)
    low3, high3 = shift(low0, "x", -1), shift(high0, "x", -1)

    qg = prepare(query, grad_out, a3)
    info = plan(gate_score[0])
    qg = (qg, swap(qg))

    state = forward((0, 4, 8, 12), info, [low0, high0, low1, high1], qg, None, False)
    state = forward((24, 16, 28), info, [low3, low2, high3], qg, state, False)
    mine, acc, acc_away = forward((20,), info, [high2], qg, state, True)
    other = swap(mine)
    acc_other = swap(acc_away)

    dq, (high2,) = backward((20,), info, [high2], qg, mine, other, None)
    high2 = shift(high2, "x", -1)
    dq, (low2,) = backward((16,), info, [low2], qg, mine, other, dq)
    low2 = shift(low2, "x", -1)
    dq, (low3, high3) = backward((24, 28), info, [low3, high3], qg, mine, other, dq)
    high3, low3 = shift(high3, "x", 1), shift(low3, "x", 1)
    dq, (low1, high1) = backward((8, 12), info, [low1, high1], qg, mine, other, dq)
    high1 = shift((wide(high1) + wide(high2)).astype(BF), "x", -1)
    low1 = shift((wide(low1) + wide(low2)).astype(BF), "x", -1)
    dq, (low0, high0) = backward((0, 4), info, [low0, high0], qg, mine, other, dq)

    keep_high, up, down, far = sum_high(high0, high1, high3)
    down, far, up = shift(down, "z", -1), shift(far, "z", -2), shift(up, "z", 1)
    own, near_down, near_up, keep_low = sum_low(low0, low1, low3)
    two_down, two_up = sum_two(keep_high, keep_low, down, far, up)
    parts = [
        shift(near_down, "z", -1),
        shift(near_up, "z", 1),
        shift(two_up, "z", 2),
        shift(two_down, "z", -2),
    ]
    grad_key, grad_value = close(own, parts)
    attended, grad_query = finish(mine, other, acc, acc_other, dq[0], swap(dq[1]))
    return (attended, grad_query, grad_key, grad_value)


def solution(mesh):
    devices = mesh.devices.reshape(8, 4, 2, 4)
    split = Mesh(devices, ("z", "x", "core", "head"))
    spec = P(("z", "x", "core"), "head")
    return jax.shard_map(
        on_device,
        mesh=split,
        in_specs=(spec, spec, spec, spec, P("head", None, None)),
        out_specs=(spec, spec, spec, spec),
        check_vma=False,
    )
```

```python
import functools
import math

import jax
import jax.numpy as jnp
from jax import lax
from jax.experimental import pallas as pl
from jax.experimental.pallas import tpu as pltpu
from jax.sharding import Mesh
from jax.sharding import PartitionSpec as P

HEAD_DIM = 128
GROUP = 4
TOPK = 8
NBLK = 32
HALF = 256
COLS = GROUP * HALF
SCALE = 1.0 / math.sqrt(HEAD_DIM)
SCALE2 = SCALE / math.log(2.0)
NEG = -1e30
MASKED = -3e38
BF = jnp.bfloat16
F32 = jnp.float32
SIZES = {"z": 8, "x": 4}
NT = (((1,), (1,)), ((), ()))
NN = (((1,), (0,)), ((), ()))
CORE_AT = 32
QUAD = 4
VMEM_LIMIT = 24 * 1024 * 1024
STAT = (2, 3, COLS)
ACC = (HEAD_DIM, COLS)
PAIR = (2, COLS, HEAD_DIM)
PIECE = (HALF, 2 * HEAD_DIM)


def dot(a, b, dims):
    return lax.dot_general(a, b, dims, preferred_element_type=F32)


def wide(a):
    return a.astype(F32)


def shift(a, axis, d):
    n = SIZES[axis]
    return lax.ppermute(a, (axis, "core"), [(2 * i + c, 2 * ((i + d * (1 - 2 * c)) % n) + c) for i in range(n) for c in range(2)])


def swap(a):
    return lax.ppermute(a, "core", [(0, 1), (1, 0)])


def keep_mask(off):
    i = lax.broadcasted_iota(jnp.int32, (HALF, HALF), 0)
    j = lax.broadcasted_iota(jnp.int32, (HALF, HALF), 1)
    return (i - j) <= off


def place_of(i, bases):
    base = bases[0]
    for a, b in enumerate(bases[1:], 1):
        base = jnp.where(i // QUAD == a, b, base)
    return base + i % QUAD


def fetch(i, kv_refs, kv_buf):
    for a, ref in enumerate(kv_refs):

        @pl.when(i // QUAD == a)
        def _():
            kv_buf[...] = ref[0]

    return kv_buf[...]


def query_refs(refs):
    return [ref.at[0] for ref in refs]


def grad_refs(refs):
    return [ref.at[1] for ref in refs]


def forward_kernel(bases, first, last, info, *refs):
    n = len(bases)
    kv_refs, refs = refs[:n], refs[n:]
    q_refs, g_refs, refs = query_refs(refs[:2]), grad_refs(refs[:2]), refs[2:]
    if not first:
        stat_in, acc_in, refs = refs[0], refs[1:3], refs[3:]
    stat_ref, acc_refs, (s_ref, p_ref, kv_buf) = refs[0], refs[1:3], refs[3:]
    i = pl.program_id(0)
    core = info[CORE_AT]

    @pl.when(i == 0)
    def _():
        if first:
            stat_ref[:, 0:1, :] = jnp.full((2, 1, COLS), NEG, F32)
            stat_ref[:, 1:3, :] = jnp.zeros((2, 2, COLS), F32)
            for half in range(2):
                acc_refs[half][...] = jnp.zeros(ACC, F32)
        else:
            stat_ref[...] = stat_in[...]
            for half in range(2):
                acc_refs[half][...] = acc_in[half][...]

    def step(masked):
        kv = fetch(i, kv_refs, kv_buf)
        k = kv[:, :HEAD_DIM]
        vt = jnp.transpose(kv[:, HEAD_DIM:])
        for half in range(2):
            s_ref[:, pl.ds(half * COLS, COLS)] = dot(k, q_refs[half][...], NT)
        for half in range(2):
            acc = acc_refs[half]
            if masked:
                keep = keep_mask(jnp.where(i == 0, half * HALF * (1 - 2 * core), HALF))
            for h in range(GROUP):
                cols = pl.ds(h * HALF, HALF)
                flat = pl.ds(half * COLS + h * HALF, HALF)
                s = s_ref[:, flat]
                if masked:
                    s = jnp.where(keep, s, MASKED)
                m_old = stat_ref[half, 0:1, cols]
                m_new = jnp.maximum(m_old, jnp.max(s, axis=0, keepdims=True) * SCALE2)
                alpha = jnp.exp2(m_old - m_new)
                p = jnp.exp2(s * SCALE2 - m_new)
                stat_ref[half, 0:1, cols] = m_new
                stat_ref[half, 1:2, cols] = stat_ref[half, 1:2, cols] * alpha + jnp.sum(p, axis=0, keepdims=True)
                acc[:, cols] = acc[:, cols] * alpha
                p_ref[:, flat] = p.astype(BF)
            acc[...] += dot(vt, p_ref[:, pl.ds(half * COLS, COLS)], NN)

    pl.when(info[place_of(i, bases)] > 0)(lambda: step(first))

    if last:

        @pl.when(i == QUAD * n - 1)
        def _():
            eye = (
                lax.broadcasted_iota(jnp.int32, (HEAD_DIM, HEAD_DIM), 0)
                == lax.broadcasted_iota(jnp.int32, (HEAD_DIM, HEAD_DIM), 1)
            ).astype(F32).astype(BF)
            for half in range(2):
                turned = dot(eye, g_refs[half][...], NT)
                stat_ref[half, 2:3, :] = jnp.sum(turned * acc_refs[half][...], axis=0, keepdims=True)


def combine(mine, other, half):
    m0 = mine[half, 0:1, :]
    m1 = other[1 - half, 0:1, :]
    m = jnp.maximum(m0, m1)
    e0 = jnp.exp2(m0 - m)
    e1 = jnp.exp2(m1 - m)
    total = mine[half, 1:2, :] * e0 + other[1 - half, 1:2, :] * e1
    return m + jnp.log2(total), e0 / total, e1 / total


def backward_kernel(bases, first, masks, info, *refs):
    n = len(bases)
    kv_refs, refs = refs[:n], refs[n:]
    q_refs, g_refs, refs = query_refs(refs[:2]), grad_refs(refs[:2]), refs[2:]
    mine, other, refs = refs[0], refs[1], refs[2:]
    if not first:
        dq_in, refs = refs[:2], refs[2:]
    dq_refs, out_refs, refs = refs[:2], refs[2 : 2 + n], refs[2 + n :]
    row_ref, s_ref, dp_ref, p_ref, ds_ref, kv_buf, out_buf = refs
    i = pl.program_id(0)
    core = info[CORE_AT]

    @pl.when(i == 0)
    def _():
        for half in range(2):
            lse, w0, w1 = combine(mine, other, half)
            row_ref[half, 0:1, :] = lse
            row_ref[half, 1:2, :] = mine[half, 2:3, :] * w0 + other[1 - half, 2:3, :] * w1
            dq_refs[half][...] = jnp.zeros(ACC, F32) if first else dq_in[half][...]

    def step(masked):
        kv = fetch(i, kv_refs, kv_buf)
        k = kv[:, :HEAD_DIM]
        v = kv[:, HEAD_DIM:]
        kt = jnp.transpose(k)
        for half in range(2):
            cols = pl.ds(half * COLS, COLS)
            s_ref[:, cols] = dot(k, q_refs[half][...], NT)
            dp_ref[:, cols] = dot(v, g_refs[half][...], NT)
        for half in range(2):
            if masked:
                keep = keep_mask(jnp.where(i == 0, half * HALF * (1 - 2 * core), HALF))
            for h in range(GROUP):
                cols = pl.ds(h * HALF, HALF)
                flat = pl.ds(half * COLS + h * HALF, HALF)
                p = jnp.exp2(s_ref[:, flat] * SCALE2 - row_ref[half, 0:1, cols])
                if masked:
                    p = jnp.where(keep, p, 0.0)
                p_ref[:, flat] = p.astype(BF)
                ds_ref[:, flat] = (p * (dp_ref[:, flat] - row_ref[half, 1:2, cols])).astype(BF)
            dq_refs[half][...] += dot(kt, ds_ref[:, pl.ds(half * COLS, COLS)], NN)
        dk = jnp.zeros((HALF, HEAD_DIM), F32)
        dv = jnp.zeros((HALF, HEAD_DIM), F32)
        for half in range(2):
            cols = pl.ds(half * COLS, COLS)
            dk = dk + dot(ds_ref[:, cols], q_refs[half][...], NN)
            dv = dv + dot(p_ref[:, cols], g_refs[half][...], NN)
        out_buf[:, :HEAD_DIM] = dk.astype(BF)
        out_buf[:, HEAD_DIM:] = dv.astype(BF)

    live = info[place_of(i, bases)] > 0
    pl.when(live)(lambda: step(masks))

    @pl.when(jnp.logical_not(live))
    def _():
        out_buf[...] = jnp.zeros(PIECE, BF)

    for a, ref in enumerate(out_refs):

        @pl.when(i // QUAD == a)
        def _():
            ref[0] = out_buf[...]


def finish_kernel(mine, other, acc_mine, acc_other, dq_mine, dq_other, att_ref, dq_ref):
    lse, w0, w1 = combine(mine, other, 0)
    for h in range(GROUP):
        cols = slice(h * HALF, (h + 1) * HALF)
        rows = slice(h * HEAD_DIM, (h + 1) * HEAD_DIM)
        out = acc_mine[:, cols] * w0[:, cols] + acc_other[:, cols] * w1[:, cols]
        att_ref[:, rows] = jnp.transpose(out).astype(BF)
        dq_ref[:, rows] = jnp.transpose((dq_mine[:, cols] + dq_other[:, cols]) * SCALE).astype(BF)


def whole(shape):
    return pl.BlockSpec(shape, lambda i, info: (0,) * len(shape))


def piece_specs(n):
    def spec(a):
        return pl.BlockSpec((1,) + PIECE, lambda i, info: (jnp.clip(i - QUAD * a, 0, QUAD - 1), 0, 0))

    return [spec(a) for a in range(n)]


def cost(flops):
    return pl.CostEstimate(flops=flops, bytes_accessed=1 << 16, transcendentals=0)


def forward(bases, info, kvs, qg, state, last):
    n = len(kvs)
    first = state is None
    ins = list(kvs) + list(qg) + ([] if first else list(state))
    specs = piece_specs(n) + [whole(PAIR)] * 2
    if not first:
        specs += [whole(STAT), whole(ACC), whole(ACC)]
    return pl.pallas_call(
        functools.partial(forward_kernel, bases, first, last),
        grid_spec=pltpu.PrefetchScalarGridSpec(
            num_scalar_prefetch=1,
            grid=(QUAD * n,),
            in_specs=specs,
            out_specs=[whole(STAT), whole(ACC), whole(ACC)],
            scratch_shapes=[
                pltpu.VMEM((HALF, 2 * COLS), F32),
                pltpu.VMEM((HALF, 2 * COLS), BF),
                pltpu.VMEM(PIECE, BF),
            ],
        ),
        out_shape=[jax.ShapeDtypeStruct(s, F32) for s in (STAT, ACC, ACC)],
        compiler_params=pltpu.CompilerParams(vmem_limit_bytes=VMEM_LIMIT),
        cost_estimate=cost(200_000_000),
        name="forward",
    )(info, *ins)


def backward(bases, info, kvs, qg, mine, other, dq):
    n = len(kvs)
    first = dq is None
    ins = list(kvs) + list(qg) + [mine, other] + ([] if first else list(dq))
    specs = piece_specs(n) + [whole(PAIR)] * 2 + [whole(STAT)] * 2
    if not first:
        specs += [whole(ACC), whole(ACC)]
    wide_shape = (HALF, 2 * COLS)
    res = pl.pallas_call(
        functools.partial(backward_kernel, bases, first, bases[0] == 0),
        grid_spec=pltpu.PrefetchScalarGridSpec(
            num_scalar_prefetch=1,
            grid=(QUAD * n,),
            in_specs=specs,
            out_specs=[whole(ACC), whole(ACC)] + piece_specs(n),
            scratch_shapes=[
                pltpu.VMEM((2, 2, COLS), F32),
                pltpu.VMEM(wide_shape, F32),
                pltpu.VMEM(wide_shape, F32),
                pltpu.VMEM(wide_shape, BF),
                pltpu.VMEM(wide_shape, BF),
                pltpu.VMEM(PIECE, BF),
                pltpu.VMEM(PIECE, BF),
            ],
        ),
        out_shape=[jax.ShapeDtypeStruct(ACC, F32)] * 2 + [jax.ShapeDtypeStruct(a.shape, BF) for a in kvs],
        compiler_params=pltpu.CompilerParams(vmem_limit_bytes=VMEM_LIMIT),
        cost_estimate=cost(200_000_000),
        name="backward",
    )(info, *ins)
    return res[:2], res[2:]


def finish(mine, other, acc_mine, acc_other, dq_mine, dq_other):
    shape = jax.ShapeDtypeStruct((HALF, GROUP * HEAD_DIM), BF)
    return pl.pallas_call(
        finish_kernel,
        in_specs=[VMEM] * 6,
        out_specs=[VMEM] * 2,
        out_shape=[shape, shape],
        compiler_params=SMALL,
        cost_estimate=pl.CostEstimate(flops=1 << 20, bytes_accessed=1 << 16, transcendentals=0),
        name="finish",
    )(mine, other, acc_mine, acc_other, dq_mine, dq_other)


VMEM = pl.BlockSpec(memory_space=pltpu.VMEM)
SMALL = pltpu.CompilerParams(vmem_limit_bytes=8 * 1024 * 1024)


def join_kernel(k_ref, v_ref, out_ref, sems):
    copies = [
        pltpu.make_async_copy(k_ref, out_ref.at[:, pl.ds(0, HEAD_DIM)], sems.at[0]),
        pltpu.make_async_copy(v_ref, out_ref.at[:, pl.ds(HEAD_DIM, HEAD_DIM)], sems.at[1]),
    ]
    for copy in copies:
        copy.start()
    for copy in copies:
        copy.wait()


def join(k, v):
    return pl.pallas_call(
        join_kernel,
        out_shape=jax.ShapeDtypeStruct(PIECE, BF),
        in_specs=[pl.BlockSpec(memory_space=pl.ANY)] * 2,
        out_specs=VMEM,
        scratch_shapes=[pltpu.SemaphoreType.DMA((2,))],
        name="join",
    )(k, v)


def prepare_kernel(query, grad_out, after, qg_ref):
    for h in range(GROUP):
        rows = slice(h * HALF, (h + 1) * HALF)
        cols = slice(h * HEAD_DIM, (h + 1) * HEAD_DIM)
        qg_ref[0, rows, :] = query[:, cols]
        qg_ref[1, rows, :] = grad_out[:, cols]


def prepare(query, grad_out, after):
    return pl.pallas_call(
        prepare_kernel,
        in_specs=[VMEM] * 2 + [pl.BlockSpec(memory_space=pl.ANY)],
        out_specs=VMEM,
        out_shape=jax.ShapeDtypeStruct(PAIR, BF),
        cost_estimate=cost(100_000_000),
        compiler_params=SMALL,
        name="prepare",
    )(query, grad_out, after)


def stack_kernel(*refs):
    for i in range(QUAD):
        refs[-1][i] = refs[i][...]


def stack(*pieces):
    return pl.pallas_call(stack_kernel, out_shape=jax.ShapeDtypeStruct((QUAD,) + PIECE, BF), in_specs=[VMEM] * QUAD, out_specs=VMEM, compiler_params=SMALL, name="stack")(*pieces)


def sum_high_kernel(own, one, three, keep, near_up, near_down, far):
    def total(i):
        return wide(own[i]) + wide(one[i]) + wide(three[i])

    keep[...] = total(0)
    near_down[...] = total(1).astype(BF)
    near_up[...] = total(2).astype(BF)
    far[...] = total(3).astype(BF)


def sum_high(own, one, three):
    shape = jax.ShapeDtypeStruct(PIECE, BF)
    return pl.pallas_call(
        sum_high_kernel,
        in_specs=[VMEM] * 3,
        out_specs=[VMEM] * 4,
        out_shape=[jax.ShapeDtypeStruct(PIECE, F32), shape, shape, shape],
        cost_estimate=cost(100_000_000),
        compiler_params=SMALL, name="sum_high",
    )(own, one, three)


def sum_low_kernel(own, one, three, own_out, near_down, near_up, keep):
    def total(i):
        return wide(own[i]) + wide(one[i]) + wide(three[i])

    own_out[...] = total(0)
    near_down[...] = total(1).astype(BF)
    near_up[...] = total(2).astype(BF)
    keep[...] = total(3)


def sum_low(own, one, three):
    kept = jax.ShapeDtypeStruct(PIECE, F32)
    shape = jax.ShapeDtypeStruct(PIECE, BF)
    return pl.pallas_call(
        sum_low_kernel,
        in_specs=[VMEM] * 3,
        out_specs=[VMEM] * 4,
        out_shape=[kept, shape, shape, kept],
        cost_estimate=cost(100_000_000),
        compiler_params=SMALL,
        name="sum_low",
    )(own, one, three)


def sum_two_kernel(high, low, down, far, up, two_down, two_up):
    two_down[...] = (low[...] + wide(down[...]) + wide(far[...])).astype(BF)
    two_up[...] = (high[...] + wide(up[...])).astype(BF)


def sum_two(high, low, down, far, up):
    shape = jax.ShapeDtypeStruct(PIECE, BF)
    return pl.pallas_call(
        sum_two_kernel,
        in_specs=[VMEM] * 5,
        out_specs=[VMEM] * 2,
        out_shape=[shape, shape],
        cost_estimate=cost(100_000_000),
        compiler_params=SMALL,
        name="sum_two",
    )(high, low, down, far, up)


def close_kernel(own, a, b, c, d, dk_ref, dv_ref):
    total = own[...] + wide(a[...]) + wide(b[...]) + wide(c[...]) + wide(d[...])
    dk_ref[...] = (total[:, :HEAD_DIM] * SCALE).astype(BF)
    dv_ref[...] = total[:, HEAD_DIM:].astype(BF)


def close(own, parts):
    shape = jax.ShapeDtypeStruct((HALF, HEAD_DIM), BF)
    return pl.pallas_call(
        close_kernel, out_shape=[shape, shape], in_specs=[VMEM] * 5, out_specs=[VMEM] * 2, compiler_params=SMALL, name="close"
    )(own, *parts)


def plan(gate):
    z = lax.axis_index("z")
    x = lax.axis_index("x")
    own = z * 4 + x
    totals = gate + lax.ppermute(gate, "head", [(0, 1), (1, 0), (2, 3), (3, 2)])
    totals = totals + lax.ppermute(totals, "head", [(0, 2), (2, 0), (1, 3), (3, 1)])
    row = lax.dynamic_slice_in_dim(totals, own, 1, 0)[0]
    columns = jnp.arange(NBLK, dtype=jnp.int32)
    ranked = jnp.where(columns < own, row * NBLK + columns, -1)
    rank = jnp.sum((ranked[None, :] > ranked[:, None]).astype(jnp.int32), axis=1)
    used = ((rank < TOPK) & (ranked >= 0)) | (columns == own)
    core = lax.axis_index("core")
    way = 1 - 2 * core
    dz = (way * (z - columns // 4)) % 8
    dx = (way * (x - columns % 4)) % 4
    pos = jnp.where(dz == 0, 0, jnp.where(dz <= 4, 2 * dz - 1, 2 * (8 - dz)))
    place = dx * 8 + pos
    live = jnp.sum((place[None, :] == columns[:, None]) & used[None, :], axis=1, dtype=jnp.int32)
    return jnp.concatenate([live, core[None]])


def on_device(query, key, value, grad_out, gate_score):
    piece = join(key, value)
    a1, b1 = shift(piece, "z", 1), shift(piece, "z", -1)
    a2, b2 = shift(piece, "z", 2), shift(piece, "z", -2)
    a3, b3, a4 = shift(a2, "z", 1), shift(b2, "z", -1), shift(a2, "z", 2)
    low0 = stack(piece, a1, b1, a2)
    high0 = stack(b2, a3, b3, a4)
    low1, high1 = shift(low0, "x", 1), shift(high0, "x", 1)
    low2, high2 = shift(low1, "x", 1), shift(high1, "x", 1)
    low3, high3 = shift(low0, "x", -1), shift(high0, "x", -1)

    qg = prepare(query, grad_out, a3)
    info = plan(gate_score[0])
    qg = (qg, swap(qg))

    state = forward((0, 4, 8, 12), info, [low0, high0, low1, high1], qg, None, False)
    state = forward((24, 16), info, [low3, low2], qg, state, False)
    mine, acc, acc_away = forward((28, 20), info, [high3, high2], qg, state, True)
    other = swap(mine)
    acc_other = swap(acc_away)

    dq, (high2,) = backward((20,), info, [high2], qg, mine, other, None)
    high2 = shift(high2, "x", -1)
    dq, (low2,) = backward((16,), info, [low2], qg, mine, other, dq)
    low2 = shift(low2, "x", -1)
    dq, (low1, high1) = backward((8, 12), info, [low1, high1], qg, mine, other, dq)
    dq, (low3, high3) = backward((24, 28), info, [low3, high3], qg, mine, other, dq)
    high3, low3 = shift(high3, "x", 1), shift(low3, "x", 1)
    high1 = shift((wide(high1) + wide(high2)).astype(BF), "x", -1)
    low1 = shift((wide(low1) + wide(low2)).astype(BF), "x", -1)
    dq, (low0, high0) = backward((0, 4), info, [low0, high0], qg, mine, other, dq)

    keep_high, up, down, far = sum_high(high0, high1, high3)
    down, far, up = shift(down, "z", -1), shift(far, "z", -2), shift(up, "z", 1)
    own, near_down, near_up, keep_low = sum_low(low0, low1, low3)
    two_down, two_up = sum_two(keep_high, keep_low, down, far, up)
    parts = [
        shift(near_down, "z", -1),
        shift(near_up, "z", 1),
        shift(two_up, "z", 2),
        shift(two_down, "z", -2),
    ]
    grad_key, grad_value = close(own, parts)
    attended, grad_query = finish(mine, other, acc, acc_other, dq[0], swap(dq[1]))
    return (attended, grad_query, grad_key, grad_value)


def solution(mesh):
    devices = mesh.devices.reshape(8, 4, 2, 4)
    split = Mesh(devices, ("z", "x", "core", "head"))
    spec = P(("z", "x", "core"), "head")
    return jax.shard_map(
        on_device,
        mesh=split,
        in_specs=(spec, spec, spec, spec, P("head", None, None)),
        out_specs=(spec, spec, spec, spec),
        check_vma=False,
    )
```
